128 devices in a mesh: gx: 4 (over z_lo, core), gy: 4 (over y), gz: 8 (over z_hi, x).
Axes of the slice: x: 4, y: 4, z: 4 (z_hi: 2, z_lo: 2; z = z_hi * 2 + z_lo), core: 2. Of those that a mesh axis runs over, the one named last changes fastest.
Arguments:
- displacement: float32 [3, 98304], P(None, ('gx', 'gy', 'gz')), may hold values from -2.5 to 2.5
- neighbour_mask: int32 [98304], P(('gx', 'gy', 'gz')), may hold values from 0 to 1, as said below
- reverse_slot: int32 [98304], P(('gx', 'gy', 'gz')), may hold values from 0 to 1199, as said below
- send_edges: int32 [53248], P(('gx', 'gy', 'gz')), may hold values from 0 to 767
- species: int32 [4096], P(('gx', 'gy', 'gz')), may hold values from 0 to 84
- prev_tokens: bfloat16 [98304, 256], P(('gx', 'gy', 'gz')), may hold values from -6 to 6
- atom_state: bfloat16 [4096, 256], P(('gx', 'gy', 'gz')), may hold values from -6 to 6
- species_table: bfloat16 [85, 256], replicated, may hold values from -6 to 6
- w_neigh: bfloat16 [256, 256], replicated, may hold values from -0.375 to 0.375
- w_vec: float32 [3, 256], replicated, may hold values from -3.5 to 3.5
- w_rbf: float32 [64, 256], replicated, may hold values from -3 to 3
- gains: float32 [5, 256], replicated, may hold values from 0.25 to 1.75
- w_qkv: bfloat16 [2, 256, 768], replicated, may hold values from -0.375 to 0.375
- w_out: bfloat16 [2, 256, 256], replicated, may hold values from -0.375 to 0.375
- w_up: bfloat16 [2, 256, 512], replicated, may hold values from -0.375 to 0.375
- w_down: bfloat16 [2, 512, 256], replicated, may hold values from -0.25 to 0.25
- w_energy: float32 [256], replicated, may hold values from -0.375 to 0.375
Outputs:
- edge_tokens: bfloat16 [98304, 256], P(('gx', 'gy', 'gz'))
- atom_energy: float32 [4096], P(('gx', 'gy', 'gz'))
- forces: float32 [3, 4096], P(None, ('gx', 'gy', 'gz'))
The draws below stay inside these ranges and needn't reach their ends.
Inputs may be any that keep to these rules, and one draw needn't show every extreme that they name: `neighbour_mask`: on each atom the first n of its 24 slots are 1 and the rest 0, with 20 <= n <= 24. `reverse_slot`: on each device, every value v >= 768 with (v - 768) // 16 != 13 is taken by exactly one edge whose neighbour_mask is 1, and no value has (v - 768) // 16 == 13; every edge of a device's first 4 atoms has a value below 768. `send_edges`: local edge numbers of the sending device.
All inputs are finite; a program needn't handle non-finite values.
Results may differ from the reference program's by a relative error of at most 0.014.
Values may be sent and summed in bfloat16 or wider, within the bound.
No kernel may reach another device: no remote copies, remote signals or barrier semaphores. Data moves between devices by JAX's collectives and lax.ppermute only.
A program may use at most 128 MiB of HBM per device.

```python
import math
import jax
import jax.numpy as jnp
from jax import lax

D = 256
HEADS = 8
FF = 512
NB = 64
NSPEC = 85
NBR = 24
ATOM_DEV = 32
INNER_DEV = 4
SLOTS = 16
EDGE_DEV = 768
ATOMS = 4096
EDGES = 98304
SEND_ALL = 53248
N_GX = 4
N_GY = 4
N_GZ = 8


def shared_layout(key):
    devices_all = EDGES // EDGE_DEV
    count_key = jax.random.fold_in(key, 11)
    order_key = jax.random.fold_in(key, 12)
    local_key = jax.random.fold_in(key, 13)
    counts = jax.random.randint(count_key, (devices_all, ATOM_DEV, 1), 20, NBR + 1)
    position = jnp.arange(NBR, dtype=jnp.int32)[None, None, :]
    live_slots = (position < counts).astype(jnp.int32).reshape(devices_all, EDGE_DEV)
    atom_index = jnp.arange(EDGE_DEV, dtype=jnp.int32) // NBR
    eligible = (live_slots > 0) & (atom_index[None, :] >= INNER_DEV)
    offset_big = 16384 * EDGE_DEV
    scores = jax.random.randint(order_key, (devices_all, EDGE_DEV), 0, 16384) * EDGE_DEV + jnp.arange(EDGE_DEV, dtype=jnp.int32)[None, :]
    scores = jnp.where(eligible, scores, scores + offset_big)
    sorted_edges = jnp.argsort(scores, axis=1, stable=True)
    edge_rank = jnp.argsort(sorted_edges, axis=1, stable=True).astype(jnp.int32)
    sent_total = 26 * SLOTS
    bucket_index = edge_rank // SLOTS
    bucket_index = bucket_index + (bucket_index >= 13).astype(jnp.int32)
    remote_value = EDGE_DEV + bucket_index * SLOTS + edge_rank % SLOTS
    local_value = jax.random.randint(local_key, (devices_all, EDGE_DEV), 0, EDGE_DEV)
    reverse = jnp.where(edge_rank < sent_total, remote_value, local_value)
    return (live_slots.reshape(-1).astype(jnp.int32), reverse.reshape(-1).astype(jnp.int32))


def draw_neighbour_mask(key, part):
    live_slots, reverse = shared_layout(key)
    return live_slots


def draw_reverse_slot(key, part):
    live_slots, reverse = shared_layout(key)
    return reverse


def plant(result, own_key, smallest, top_value):
    dims = result.shape
    index_at = [jax.random.randint(jax.random.fold_in(own_key, axis), (), 0, dims[axis]) for axis in range(len(dims))]
    result = result.at[tuple(index_at)].set(smallest)
    longest = dims.index(max(dims))
    index_at[longest] = (index_at[longest] + 1) % dims[longest]
    return result.at[tuple(index_at)].set(top_value)


def block_scale(stream_key, extent, pieces, least, largest):
    level, own = 1.0, jax.random.fold_in(stream_key, 6)
    for axis_at, parts in pieces:
        heights = jnp.exp(jax.random.uniform(jax.random.fold_in(own, axis_at), (parts,), jnp.float32, least / len(pieces), largest / len(pieces)))
        level = level * jnp.repeat(heights, extent[axis_at] // parts).reshape([-1 if axis == axis_at else 1 for axis in range(len(extent))])
    return level


def scatter_about(own_key, extent, deviation, limit, split=(), held_as=jnp.bfloat16):
    entries = deviation * jax.random.normal(own_key, extent, jnp.float32)
    if split:
        entries = entries * block_scale(own_key, extent, split, -0.22, 0.18)
    return jnp.clip(entries, -limit, limit).astype(held_as)


def setup_inputs(seed: int = 0) -> dict:
    key_list = jax.random.split(jax.random.key(seed), 18)
    return {
        "displacement": jnp.clip(jax.random.uniform(key_list[0], (3, EDGES), jnp.float32, -2.5, 2.5) * block_scale(key_list[0], (3, EDGES), ((1, 128),), -0.4, 0.0), -2.5, 2.5),
        "neighbour_mask": draw_neighbour_mask(jax.random.fold_in(key_list[17], 71), 0),
        "reverse_slot": draw_reverse_slot(jax.random.fold_in(key_list[17], 71), 0),
        "send_edges": plant(jax.random.randint(key_list[3], (SEND_ALL,), 0, EDGE_DEV), jax.random.fold_in(key_list[3], 1), 0, EDGE_DEV - 1).astype(jnp.int32),
        "species": plant(jax.random.randint(key_list[4], (ATOMS,), 0, NSPEC), jax.random.fold_in(key_list[4], 1), 0, NSPEC - 1).astype(jnp.int32),
        "prev_tokens": scatter_about(key_list[5], (EDGES, D), 1.0, 6.0, ((0, 128),)),
        "atom_state": scatter_about(key_list[6], (ATOMS, D), 1.0, 6.0, ((0, 128),)),
        "species_table": scatter_about(key_list[7], (NSPEC, D), 1.0, 6.0),
        "w_neigh": scatter_about(key_list[8], (D, D), D ** -0.5, 0.375),
        "w_vec": scatter_about(key_list[9], (3, D), 3 ** -0.5, 3.5, (), jnp.float32),
        "w_rbf": scatter_about(key_list[10], (NB, D), 4 ** -0.5, 3.0, (), jnp.float32),
        "gains": jnp.clip(1.0 + 0.15 * jax.random.normal(key_list[11], (5, D), jnp.float32), 0.25, 1.75),
        "w_qkv": scatter_about(key_list[12], (2, D, 3 * D), D ** -0.5, 0.375),
        "w_out": scatter_about(key_list[13], (2, D, D), D ** -0.5, 0.375),
        "w_up": scatter_about(key_list[14], (2, D, FF), D ** -0.5, 0.375),
        "w_down": scatter_about(key_list[15], (2, FF, D), FF ** -0.5, 0.25),
        "w_energy": scatter_about(key_list[16], (D,), D ** -0.5, 0.375, (), jnp.float32),
    }


score_cap = 8.0
cutoff_radius = 5.0
norm_eps = 1e-06

def rms_scaled(stream, gain):
    return stream * lax.rsqrt(lax.optimization_barrier(jnp.mean(stream * stream, axis=-1, keepdims=True)) + norm_eps) * gain

def atom_block(displace, incoming, live_slots, centre_embed, gains, w_vec, w_rbf, w_qkv, w_out, w_up, w_down, w_energy):
    edge_count = incoming.shape[0]
    feature_width = incoming.shape[1]
    atom_count = centre_embed.shape[0]
    per_atom = edge_count // atom_count
    basis_count = w_rbf.shape[0]
    head_count = HEADS
    head_size = feature_width // head_count
    distance = jnp.sqrt(lax.optimization_barrier(jnp.sum(displace * displace, axis=0)) + 0.5)
    cutoff = 0.5 * (jnp.cos(jnp.pi * distance / cutoff_radius) + 1.0)
    centres = 0.5 + 4.0 * jnp.arange(basis_count, dtype=jnp.float32) / (basis_count - 1)
    spacing = 8.0 / basis_count
    radial = jnp.exp(-jnp.square((distance[None, :] - centres[:, None]) / spacing))
    contract_dims = (((0,), (0,)), ((), ()))
    geometry = lax.dot_general(displace, w_vec, contract_dims, precision=lax.Precision.HIGHEST, preferred_element_type=jnp.float32)
    geometry = geometry + lax.dot_general(radial, w_rbf, contract_dims, precision=lax.Precision.HIGHEST, preferred_element_type=jnp.float32)
    stream = cutoff[:, None] * geometry + incoming.astype(jnp.float32) + jnp.repeat(centre_embed, per_atom, axis=0)
    key_weight = (live_slots * cutoff).reshape(atom_count, 1, 1, per_atom)
    for layer_index in range(2):
        normed = rms_scaled(stream, gains[2 * layer_index]).astype(jnp.bfloat16)
        projected = jnp.dot(normed, w_qkv[layer_index], preferred_element_type=jnp.float32).astype(jnp.bfloat16)
        triple = projected.reshape(atom_count, per_atom, 3, head_count, head_size).astype(jnp.float32)
        scores = jnp.einsum('aqhd,akhd->ahqk', triple[:, :, 0], triple[:, :, 1]) / math.sqrt(head_size)
        weights = key_weight * jnp.exp(score_cap * jnp.tanh(scores / score_cap))
        weights = (weights / lax.optimization_barrier(jnp.sum(weights, axis=-1, keepdims=True))).astype(jnp.bfloat16)
        attended = jnp.einsum('ahqk,akhd->aqhd', weights.astype(jnp.float32), triple[:, :, 2])
        attended = attended.astype(jnp.bfloat16).reshape(edge_count, feature_width)
        stream = stream + jnp.dot(attended, w_out[layer_index], preferred_element_type=jnp.float32)
        normed = rms_scaled(stream, gains[2 * layer_index + 1]).astype(jnp.bfloat16)
        hidden = jax.nn.silu(jnp.dot(normed, w_up[layer_index], preferred_element_type=jnp.float32)).astype(jnp.bfloat16)
        stream = stream + jnp.dot(hidden, w_down[layer_index], preferred_element_type=jnp.float32)
    tokens = stream.astype(jnp.bfloat16)
    readout = jnp.dot(rms_scaled(stream, gains[4]), w_energy, precision=lax.Precision.HIGHEST)
    energy = lax.optimization_barrier(jnp.sum((live_slots * cutoff * readout).reshape(atom_count, per_atom), axis=1))
    return (energy, tokens)

def energy_and_force_terms(displace, incoming, live_slots, centre_embed, gains, w_vec, w_rbf, w_qkv, w_out, w_up, w_down, w_energy):

    def energy_of(moved_edges):
        return atom_block(moved_edges, incoming, live_slots, centre_embed, gains, w_vec, w_rbf, w_qkv, w_out, w_up, w_down, w_energy)
    energy, pull_back, tokens = jax.vjp(energy_of, displace, has_aux=True)
    edge_grad = pull_back(jnp.ones_like(energy))[0]
    return (energy, tokens, edge_grad)

def partner_index(reverse_slot, send_edges):
    edge_ids = jnp.arange(EDGES, dtype=jnp.int32)
    device = edge_ids // EDGE_DEV
    grid_first = device // (N_GY * N_GZ)
    grid_second = device // N_GZ % N_GY
    grid_third = device % N_GZ
    slot_offset = jnp.maximum(reverse_slot - EDGE_DEV, 0)
    bucket_index = slot_offset // SLOTS
    slot_index = slot_offset % SLOTS
    shift_first = bucket_index // 9 - 1
    shift_second = bucket_index // 3 % 3 - 1
    shift_third = bucket_index % 3 - 1
    source = ((grid_first + shift_first) % N_GX * N_GY + (grid_second + shift_second) % N_GY) * N_GZ + (grid_third + shift_third) % N_GZ
    mirror = 26 - bucket_index
    mirror_packed = mirror - (mirror > 13).astype(jnp.int32)
    sent_edge = send_edges[(source * 26 * SLOTS + mirror_packed * SLOTS + slot_index).astype(jnp.int32)]
    remote_value = source * EDGE_DEV + sent_edge
    local_value = device * EDGE_DEV + reverse_slot
    return jnp.where(reverse_slot >= EDGE_DEV, remote_value, local_value).astype(jnp.int32)

def reference(displacement, neighbour_mask, reverse_slot, send_edges, species, prev_tokens, atom_state, species_table, w_neigh, w_vec, w_rbf, gains, w_qkv, w_out, w_up, w_down, w_energy):
    device_count = N_GX * N_GY * N_GZ
    projected = jnp.dot(atom_state, w_neigh, preferred_element_type=jnp.float32)
    message = (prev_tokens.reshape(ATOMS, NBR, D) + projected[:, None, :]).astype(jnp.bfloat16).reshape(EDGES, D)
    partner = partner_index(reverse_slot, send_edges)
    incoming = message[partner]
    live_slots = neighbour_mask.astype(jnp.float32)
    one_hot = (species[:, None] == jnp.arange(NSPEC, dtype=jnp.int32)[None, :]).astype(jnp.bfloat16)
    centre_embed = jnp.dot(one_hot, species_table, preferred_element_type=jnp.float32)

    def per_device(device):
        edge_start = (device * EDGE_DEV).astype(jnp.int32)
        atom_start = (device * ATOM_DEV).astype(jnp.int32)
        return energy_and_force_terms(lax.dynamic_slice_in_dim(displacement, edge_start, EDGE_DEV, 1), lax.dynamic_slice_in_dim(incoming, edge_start, EDGE_DEV, 0), lax.dynamic_slice_in_dim(live_slots, edge_start, EDGE_DEV, 0), lax.dynamic_slice_in_dim(centre_embed, atom_start, ATOM_DEV, 0), gains, w_vec, w_rbf, w_qkv, w_out, w_up, w_down, w_energy)
    energy, tokens, edge_grad = lax.map(per_device, jnp.arange(device_count, dtype=jnp.int32))
    edge_grad = jnp.transpose(edge_grad, (1, 0, 2)).reshape(3, EDGES)
    partner_grad = edge_grad[:, partner]
    forces = lax.optimization_barrier(jnp.sum((live_slots * (edge_grad - partner_grad)).reshape(3, ATOMS, NBR), axis=2))
    return (tokens.reshape(EDGES, D), energy.reshape(ATOMS), forces)
```

```python
import math

import jax
import jax.numpy as jnp
from jax import lax
from jax.experimental import pallas as pl
from jax.experimental.pallas import tpu as pltpu
from jax.sharding import PartitionSpec as P

HEADS = 8
NBR = 24
ATOMS_DEV = 32
EDGE_DEV = 768
D = 256
FF = 512
NB = 64
NSPEC = 85
SLOTS = 16
SIDE = 9 * SLOTS
NFEAT = 72
score_cap = 8.0
cutoff_radius = 5.0
norm_eps = 1e-06

BF = jnp.bfloat16
F32 = jnp.float32
VMEM = pltpu.VMEM


def dot_nn(a, b):
    return lax.dot_general(a, b, (((1,), (0,)), ((), ())), preferred_element_type=F32)


def dot_nt(a, b):
    return lax.dot_general(a, b, (((1,), (1,)), ((), ())), preferred_element_type=F32)


def dot_tn(a, b):
    return lax.dot_general(a, b, (((0,), (0,)), ((), ())), preferred_element_type=F32)


def iota(shape, axis):
    return lax.broadcasted_iota(jnp.int32, shape, axis)


def split2(x):
    hi = x.astype(BF)
    lo = (x - hi.astype(F32)).astype(BF)
    return hi, lo


def as_column(row):
    return jnp.broadcast_to(row, (8, row.shape[1])).T[:, 0:1]


def atom_rows(count, dtype=BF):
    edge = iota((count * NBR, count), 0)
    first = iota((count * NBR, count), 1) * NBR
    return jnp.where((edge >= first) & (edge < first + NBR), 1.0, 0.0).astype(dtype)


def one_hot_lanes(column, width):
    lanes = iota((column.shape[0], width), 1).astype(F32)
    return jnp.where(lanes == column, 1.0, 0.0).astype(BF)


def message_kernel(state, w_neigh, prev, send, message, low, mid, high):
    projected = dot_nn(state[...], w_neigh[...])
    expand = atom_rows(ATOMS_DEV)
    hi, lo = split2(projected)
    rest = (projected - hi.astype(F32) - lo.astype(F32)).astype(BF)
    wide = dot_nn(expand, hi) + dot_nn(expand, lo) + dot_nn(expand, rest)
    out = (prev[...].astype(F32) + wide).astype(BF)
    message[...] = out
    pick = one_hot_lanes(as_column(send[...].astype(F32)), EDGE_DEV)
    payload = dot_nn(pick, out).astype(BF)
    low[...] = payload[0:SIDE]
    mid[...] = payload[SIDE : 2 * SIDE]
    high[...] = payload[2 * SIDE : 3 * SIDE]


def remote_index(slot):
    far = slot - EDGE_DEV
    bucket = far >> 4
    pair = (bucket * 11) >> 5
    third = bucket - 3 * pair
    return jnp.where(far >= 0, third * SIDE + pair * SLOTS + (far & 15), -1).astype(F32)


def geometry_kernel(
    disp, mask, slot, species, message, table, w_vec, w_rbf, base, kwb, feat, rows, mt, wfeat
):
    d = disp[...]
    dist = jnp.sqrt(jnp.sum(d * d, axis=0, keepdims=True) + 0.5)
    angle = (math.pi / cutoff_radius) * dist
    cut = 0.5 * (jnp.cos(angle) + 1.0)
    live = mask[...].astype(F32)
    kw = live * cut
    centres = 0.5 + 4.0 * iota((NB, 1), 0).astype(F32) / (NB - 1)
    offset = dist - centres
    radial = jnp.exp(-jnp.square(offset * (NB / 8.0)))
    feat[0:NB, :] = radial
    feat[NB:NFEAT, :] = jnp.zeros((NFEAT - NB, EDGE_DEV), F32)
    feat[NB : NB + 3, :] = d
    wfeat[0:NB, :] = w_rbf[...]
    wfeat[NB:NFEAT, :] = jnp.zeros((NFEAT - NB, D), F32)
    wfeat[NB : NB + 3, :] = w_vec[...]
    rows[0:1, :] = dist
    rows[1:2, :] = cut
    rows[2:3, :] = live
    rows[3:4, :] = kw
    rows[4:5, :] = (-0.5 * math.pi / cutoff_radius) * jnp.sin(angle)
    rows[5:8, :] = jnp.zeros((3, EDGE_DEV), F32)
    scaled = feat[...] * cut
    hi = scaled.astype(BF).astype(F32)
    left = jnp.concatenate([hi, scaled - hi, hi], axis=0).T.astype(BF)
    w = wfeat[...]
    whi = w.astype(BF).astype(F32)
    right = jnp.concatenate([whi, whi, w - whi], axis=0).astype(BF)
    kind = jnp.where(iota((NSPEC, ATOMS_DEV), 0) == species[...], 1.0, 0.0).astype(BF)
    centre = dot_tn(kind, table[...]).astype(BF)
    expand = atom_rows(ATOMS_DEV)
    slot_row = slot[...]
    local = one_hot_lanes(as_column(slot_row.astype(F32)), EDGE_DEV)
    base[...] = dot_nn(left, right) + dot_nn(expand, centre) + dot_nn(local, message[...])
    kwb[...] = jnp.broadcast_to(as_column(kw), (EDGE_DEV, 128))
    far = one_hot_lanes(as_column(remote_index(slot_row)), 3 * SIDE)
    live_rows = expand.astype(F32) * as_column(live)
    mt[...] = dot_tn(live_rows.astype(BF), far)


def rms_factor(x):
    return lax.rsqrt(jnp.mean(x * x, axis=-1, keepdims=True) + norm_eps)


def rms_back(x, r, z):
    inner = jnp.mean(x * z, axis=-1, keepdims=True)
    return r * z - x * (r * r * r * inner)


ROWS = 192
GROUP = 4


def layer_kernel(
    base,
    arr_r,
    arr_m,
    arr_l,
    slot,
    kwb,
    feat,
    rows,
    wfeat,
    gains,
    w_qkv,
    w_out,
    w_up,
    w_down,
    w_energy,
    send,
    tokens,
    energy,
    grad,
    low,
    mid,
    high,
    xs,
    qkv,
    ups,
    probs,
    slope,
    att,
    dqkv,
    acc,
):
    edges = base.shape[0]
    atoms = edges // NBR
    blocks = [slice(i, i + ROWS) for i in range(0, edges, ROWS)]
    lane_head = iota((1, 128), 1) >> 5
    head_lanes = [lane_head == h for h in range(4)]
    row_head = iota((128, 128), 0)
    mask_low = (iota((128, 128), 1) >> 5) * NBR
    block_mask = jnp.where(
        (row_head >= mask_low) & (row_head < mask_low + NBR), 1.0, 0.0
    ).astype(BF)
    score_scale = 1.0 / (math.sqrt(D // HEADS) * score_cap)
    slope_scale = 1.0 / math.sqrt(D // HEADS)

    def spread(x):
        two = jnp.concatenate([x, x], axis=0).astype(BF)
        return jnp.concatenate([two, two, jnp.zeros((32, 128), BF)], axis=0) * block_mask

    def gather_heads(wide):
        out = jnp.where(head_lanes[0], wide[0:NBR], 0.0)
        for h in range(1, 4):
            out = jnp.where(head_lanes[h], wide[h * NBR : (h + 1) * NBR], out)
        return out

    far = one_hot_lanes(as_column(remote_index(slot[...])), 3 * SIDE)
    arrived = jnp.concatenate([arr_r[...], arr_m[...], arr_l[...]], axis=0)
    x = [base[b, :] + dot_nn(far[b], arrived) for b in blocks]

    for layer in range(2):
        for b, v in zip(blocks, x):
            xs[2 * layer, b, :] = v
        gain = gains[2 * layer : 2 * layer + 1, :]
        normed = [(v * rms_factor(v) * gain).astype(BF) for v in x]
        for b, v in zip(blocks, normed):
            qkv[layer, b, :] = dot_nn(v, w_qkv[layer])

        @pl.loop(0, atoms // GROUP)
        def _(step):
            for u in range(GROUP):
                span = pl.ds(pl.multiple_of(step * (GROUP * NBR) + u * NBR, 8), NBR)
                weight = kwb[span, :]
                for g in range(2):
                    c = 128 * g
                    q = spread(qkv[layer, span, c : c + 128])
                    k = qkv[layer, span, D + c : D + c + 128].astype(BF)
                    v = qkv[layer, span, 2 * D + c : 2 * D + c + 128].astype(BF)
                    t = jnp.tanh(dot_nt(k, q) * score_scale)
                    e = weight * jnp.exp(score_cap * t)
                    p = e * (1.0 / jnp.sum(e, axis=0, keepdims=True))
                    probs[layer, span, c : c + 128] = p
                    slope[layer, span, c : c + 128] = (1.0 - t * t) * slope_scale
                    att[span, c : c + 128] = gather_heads(dot_tn(p.astype(BF), v))

        x = [xs[2 * layer, b, :] + dot_nn(att[b, :].astype(BF), w_out[layer]) for b in blocks]
        for b, v in zip(blocks, x):
            xs[2 * layer + 1, b, :] = v
        gain = gains[2 * layer + 1 : 2 * layer + 2, :]
        normed = [(v * rms_factor(v) * gain).astype(BF) for v in x]
        up = [dot_nn(v, w_up[layer]) for v in normed]
        for b, v in zip(blocks, up):
            ups[layer, b, :] = v
        hidden = [(u / (1.0 + jnp.exp(-u))).astype(BF) for u in up]
        x = [v + dot_nn(h, w_down[layer]) for v, h in zip(x, hidden)]

    read = gains[4:5, :] * w_energy[...]
    ones8 = jnp.ones((8, 128), BF)
    readout = []
    dx = []
    for b, v in zip(blocks, x):
        tokens[b, :] = v.astype(BF)
        r = rms_factor(v)
        scaled = v * r
        terms = scaled * read
        part_hi, part_lo = split2(terms[:, 0:128] + terms[:, 128:256])
        readout.append(dot_nt(ones8, part_hi) + dot_nt(ones8, part_lo))
        total = jnp.sum(terms, axis=-1, keepdims=True) * (1.0 / D)
        kw_col = kwb[b, 0:1]
        dx.append((kw_col * r) * (read - scaled * total))
    readout = jnp.concatenate(readout, axis=1)[0:1]
    live = rows[2:3, :]
    kw = rows[3:4, :]
    parts = kw * readout
    part_hi = parts.astype(BF).astype(F32)
    stacked = jnp.concatenate(
        [jnp.broadcast_to(part_hi, (8, edges)), jnp.broadcast_to(parts - part_hi, (8, edges))], axis=0
    ).astype(BF)
    summed = dot_nn(stacked, atom_rows(atoms))
    energy[...] = summed[0:1] + summed[8:9]

    for layer in (1, 0):
        dhid = [dot_nt(v.astype(BF), w_down[layer]) for v in dx]
        dup = []
        for b, dh in zip(blocks, dhid):
            u = ups[layer, b, :]
            sig = 1.0 / (1.0 + jnp.exp(-u))
            dup.append((dh * (sig * (1.0 + u * (1.0 - sig)))).astype(BF))
        gain = gains[2 * layer + 1 : 2 * layer + 2, :]
        dnorm = [dot_nt(v, w_up[layer]) * gain for v in dup]
        new = []
        for b, v, dn in zip(blocks, dx, dnorm):
            xv = xs[2 * layer + 1, b, :]
            new.append(v + rms_back(xv, rms_factor(xv), dn))
        dx = new
        for b, v in zip(blocks, dx):
            att[b, :] = dot_nt(v.astype(BF), w_out[layer])

        @pl.loop(0, atoms // GROUP)
        def _(step):
            for u in range(GROUP):
                span = pl.ds(pl.multiple_of(step * (GROUP * NBR) + u * NBR, 8), NBR)
                total = None
                for g in range(2):
                    c = 128 * g
                    q = spread(qkv[layer, span, c : c + 128])
                    k = qkv[layer, span, D + c : D + c + 128].astype(BF)
                    v = qkv[layer, span, 2 * D + c : 2 * D + c + 128].astype(BF)
                    do = spread(att[span, c : c + 128])
                    p = probs[layer, span, c : c + 128]
                    dp = dot_nt(v, do)
                    inner = jnp.sum(p * dp, axis=0, keepdims=True)
                    dl = p * (dp - inner)
                    total = dl if total is None else total + dl
                    ds = (dl * slope[layer, span, c : c + 128]).astype(BF)
                    dqkv[span, c : c + 128] = gather_heads(dot_tn(ds, k))
                    dqkv[span, D + c : D + c + 128] = dot_nn(ds, q)
                    dqkv[span, 2 * D + c : 2 * D + c + 128] = dot_nn(p.astype(BF), do)
                if layer == 1:
                    acc[span, :] = total
                else:
                    acc[span, :] = acc[span, :] + total

        gain = gains[2 * layer : 2 * layer + 1, :]
        dnorm = [dot_nt(dqkv[b, :].astype(BF), w_qkv[layer]) * gain for b in blocks]
        new = []
        for b, v, dn in zip(blocks, dx, dnorm):
            xv = xs[2 * layer, b, :]
            new.append(v + rms_back(xv, rms_factor(xv), dn))
        dx = new

    w = wfeat[...]
    whi = w.astype(BF)
    wlo = (w - whi.astype(F32)).astype(BF)
    back = []
    acc_row = []
    for b, v in zip(blocks, dx):
        hi, lo = split2(v)
        back.append(dot_nt(whi, hi) + dot_nt(whi, lo) + dot_nt(wlo, hi))
        part_hi, part_lo = split2(acc[b, :])
        acc_row.append(dot_nt(ones8, part_hi) + dot_nt(ones8, part_lo))
    back = jnp.concatenate(back, axis=1)
    acc_row = jnp.concatenate(acc_row, axis=1)[0:1]
    dist = rows[0:1, :]
    cut = rows[1:2, :]
    f = feat[...]
    dcut = jnp.sum(f * back, axis=0, keepdims=True) + live * (readout + acc_row / cut)
    centres = 0.5 + 4.0 * iota((NB, 1), 0).astype(F32) / (NB - 1)
    dradial = back[0:NB] * f[0:NB] * (dist - centres)
    ddist = dcut * rows[4:5, :] - (2.0 * (NB / 8.0) ** 2) * cut * jnp.sum(
        dradial, axis=0, keepdims=True
    )
    g = cut * back[NB:NFEAT] + f[NB:NFEAT] * (ddist / dist)
    grad[...] = g
    ghi = g.astype(BF).astype(F32)
    both = jnp.concatenate([ghi, g - ghi], axis=0).astype(BF)
    pick = jnp.where(iota((edges, 3 * SIDE), 0) == send[...], 1.0, 0.0).astype(BF)
    out = dot_nn(both, pick)
    out = out[0:8] + out[8:16]
    low[...] = out[:, 0:SIDE]
    mid[...] = out[:, SIDE : 2 * SIDE]
    high[...] = out[:, 2 * SIDE : 3 * SIDE]


def local_force_kernel(grad, slot, rows, out):
    g = grad[...]
    ghi = g.astype(BF).astype(F32)
    both = jnp.concatenate([ghi, g - ghi], axis=0).astype(BF)
    local = one_hot_lanes(as_column(slot[...].astype(F32)), EDGE_DEV)
    partner = dot_nt(both, local)
    diff = (g - partner[0:8] - partner[8:16]) * rows[2:3, :]
    hi = diff.astype(BF).astype(F32)
    both = jnp.concatenate([hi, diff - hi], axis=0).astype(BF)
    summed = dot_nn(both, atom_rows(ATOMS_DEV))
    out[...] = summed[0:8] + summed[8:16]


def force_kernel(partial, mt, r, m, l, forces):
    pieces = []
    for part in (r, m, l):
        for a in range(3):
            for b in range(3):
                pieces.append(part[b, a])
    table = jnp.concatenate(pieces, axis=1)
    hi = table.astype(BF).astype(F32)
    both = jnp.concatenate([hi, table - hi], axis=0).astype(BF)
    far = dot_nt(both, mt[...].astype(BF))
    forces[...] = (partial[...] - far[0:8] - far[8:16])[0:3]


def vmem_call(kernel, outs, *args, scratch=(), limit=60 * 2**20):
    spec = pl.BlockSpec(memory_space=VMEM)
    return pl.pallas_call(
        kernel,
        out_shape=outs,
        in_specs=[spec] * len(args),
        out_specs=jax.tree.map(lambda _: spec, outs),
        scratch_shapes=list(scratch),
        compiler_params=pltpu.CompilerParams(vmem_limit_bytes=limit),
    )(*args)


def shape(dims, dtype=F32):
    return jax.ShapeDtypeStruct(dims, dtype)


def messages(atom_state, w_neigh, prev_tokens, send):
    side = shape((SIDE, D), BF)
    return vmem_call(
        message_kernel,
        [shape((EDGE_DEV, D), BF), side, side, side],
        atom_state,
        w_neigh,
        prev_tokens,
        send,
    )


def geometry(disp, mask, slot, species, message, table, w_vec, w_rbf):
    return vmem_call(
        geometry_kernel,
        [
            shape((EDGE_DEV, D)),
            shape((EDGE_DEV, 128)),
            shape((NFEAT, EDGE_DEV)),
            shape((8, EDGE_DEV)),
            shape((ATOMS_DEV, 3 * SIDE)),
            shape((NFEAT, D)),
        ],
        disp,
        mask,
        slot,
        species,
        message,
        table,
        w_vec,
        w_rbf,
    )


def layers(base, arr, slot, kwb, feat, rows, wfeat, gains, w_qkv, w_out, w_up, w_down, w_energy, send):
    side = shape((8, SIDE))
    n = EDGE_DEV
    return vmem_call(
        layer_kernel,
        [shape((n, D), BF), shape((1, ATOMS_DEV)), shape((8, n)), side, side, side],
        base,
        *arr,
        slot,
        kwb,
        feat,
        rows,
        wfeat,
        gains,
        w_qkv,
        w_out,
        w_up,
        w_down,
        w_energy,
        send,
        scratch=[
            VMEM((4, n, D), F32),
            VMEM((2, n, 3 * D), F32),
            VMEM((2, n, FF), F32),
            VMEM((2, n, D), F32),
            VMEM((2, n, D), F32),
            VMEM((n, D), F32),
            VMEM((n, 3 * D), F32),
            VMEM((n, 128), F32),
        ],
    )


def to_right(x, axis):
    count = lax.axis_size(axis)
    return lax.ppermute(x, axis, [(i, (i + 1) % count) for i in range(count)])


def to_left(x, axis):
    count = lax.axis_size(axis)
    return lax.ppermute(x, axis, [((i + 1) % count, i) for i in range(count)])


def on_device(
    displacement,
    neighbour_mask,
    reverse_slot,
    send_edges,
    species,
    prev_tokens,
    atom_state,
    species_table,
    w_neigh,
    w_vec,
    w_rbf,
    gains,
    w_qkv,
    w_out,
    w_up,
    w_down,
    w_energy,
):
    centre = jnp.full((SLOTS,), -1, jnp.int32)
    send = jnp.concatenate([send_edges[: 13 * SLOTS], centre, send_edges[13 * SLOTS :]])
    send = send.reshape(1, 3 * SIDE)
    slot = reverse_slot.reshape(1, EDGE_DEV)
    message, low, mid, high = messages(atom_state, w_neigh, prev_tokens, send)
    right, left = to_right(high, "gx"), to_left(low, "gx")
    base, kwb, feat, rows, mt, wfeat = geometry(
        displacement,
        neighbour_mask.reshape(1, EDGE_DEV),
        slot,
        species.reshape(1, ATOMS_DEV),
        message,
        species_table,
        w_vec,
        w_rbf,
    )
    cells = [v.reshape(3, 3, SLOTS, D) for v in (right, mid, left)]
    high, mid, low = (jnp.stack([v[i] for v in cells]) for i in (2, 1, 0))
    right, left = to_right(high, "gy"), to_left(low, "gy")
    cells = (right, mid, left)
    high, mid, low = (jnp.stack([v[:, i] for v in cells], axis=1) for i in (2, 1, 0))
    right, left = to_right(high, "gz"), to_left(low, "gz")
    arr = [v.reshape(SIDE, D) for v in (right, mid, left)]
    tokens, energy, grad, low, mid, high = layers(
        base,
        arr,
        slot,
        kwb,
        feat,
        rows,
        wfeat,
        gains,
        w_qkv,
        w_out,
        w_up,
        w_down,
        w_energy.reshape(1, D),
        send,
    )
    right, left = to_right(high, "gx"), to_left(low, "gx")
    partial = vmem_call(local_force_kernel, shape((8, ATOMS_DEV)), grad, slot, rows)
    cells = jnp.stack([right, mid, left])
    cut = 3 * SLOTS
    right, left = to_right(cells[:, :, 2 * cut :], "gy"), to_left(cells[:, :, :cut], "gy")
    cells = jnp.stack([right, cells[:, :, cut : 2 * cut], left])
    cut = SLOTS
    right, left = to_right(cells[..., 2 * cut :], "gz"), to_left(cells[..., :cut], "gz")
    mid = cells[..., cut : 2 * cut]
    forces = vmem_call(force_kernel, shape((3, ATOMS_DEV)), partial, mt, right, mid, left)
    return (tokens, energy.reshape(ATOMS_DEV), forces)


def solution(mesh):
    return jax.shard_map(
        on_device,
        mesh=mesh,
        in_specs=(
            P(None, ("gx", "gy", "gz")),
            P(("gx", "gy", "gz")),
            P(("gx", "gy", "gz")),
            P(("gx", "gy", "gz")),
            P(("gx", "gy", "gz")),
            P(("gx", "gy", "gz"), None),
            P(("gx", "gy", "gz"), None),
            P(),
            P(),
            P(),
            P(),
            P(),
            P(),
            P(),
            P(),
            P(),
            P(),
        ),
        out_specs=(P(("gx", "gy", "gz"), None), P(("gx", "gy", "gz")), P(None, ("gx", "gy", "gz"))),
        check_vma=False,
    )
```

```python
import math

import jax
import jax.numpy as jnp
from jax import lax
from jax.experimental import pallas as pl
from jax.experimental.pallas import tpu as pltpu
from jax.sharding import PartitionSpec as P

HEADS = 8
NBR = 24
ATOMS_DEV = 32
EDGE_DEV = 768
D = 256
FF = 512
NB = 64
NSPEC = 85
SLOTS = 16
SIDE = 9 * SLOTS
NFEAT = 72
score_cap = 8.0
cutoff_radius = 5.0
norm_eps = 1e-06

BF = jnp.bfloat16
F32 = jnp.float32
VMEM = pltpu.VMEM


def dot_nn(a, b):
    return lax.dot_general(a, b, (((1,), (0,)), ((), ())), preferred_element_type=F32)


def dot_nt(a, b):
    return lax.dot_general(a, b, (((1,), (1,)), ((), ())), preferred_element_type=F32)


def dot_tn(a, b):
    return lax.dot_general(a, b, (((0,), (0,)), ((), ())), preferred_element_type=F32)


def iota(shape, axis):
    return lax.broadcasted_iota(jnp.int32, shape, axis)


def split2(x):
    hi = x.astype(BF)
    lo = (x - hi.astype(F32)).astype(BF)
    return hi, lo


def as_column(row):
    return jnp.broadcast_to(row, (8, row.shape[1])).T[:, 0:1]


def atom_rows(count, dtype=BF):
    edge = iota((count * NBR, count), 0)
    first = iota((count * NBR, count), 1) * NBR
    return jnp.where((edge >= first) & (edge < first + NBR), 1.0, 0.0).astype(dtype)


def one_hot_lanes(column, width):
    lanes = iota((column.shape[0], width), 1).astype(F32)
    return jnp.where(lanes == column, 1.0, 0.0).astype(BF)


def message_kernel(state, w_neigh, prev, send, message, low, mid, high):
    projected = dot_nn(state[...], w_neigh[...])
    expand = atom_rows(ATOMS_DEV)
    hi, lo = split2(projected)
    rest = (projected - hi.astype(F32) - lo.astype(F32)).astype(BF)
    wide = dot_nn(expand, hi) + dot_nn(expand, lo) + dot_nn(expand, rest)
    out = (prev[...].astype(F32) + wide).astype(BF)
    message[...] = out
    pick = one_hot_lanes(as_column(send[...].astype(F32)), EDGE_DEV)
    payload = dot_nn(pick, out).astype(BF)
    low[...] = payload[0:SIDE]
    mid[...] = payload[SIDE : 2 * SIDE]
    high[...] = payload[2 * SIDE : 3 * SIDE]


def remote_index(slot):
    far = slot - EDGE_DEV
    bucket = far >> 4
    pair = (bucket * 11) >> 5
    third = bucket - 3 * pair
    return jnp.where(far >= 0, third * SIDE + pair * SLOTS + (far & 15), -1).astype(F32)


def geometry_kernel(
    disp, mask, slot, species, message, table, w_vec, w_rbf, base, kwb, feat, rows, mt, wfeat
):
    d = disp[...]
    dist = jnp.sqrt(jnp.sum(d * d, axis=0, keepdims=True) + 0.5)
    angle = (math.pi / cutoff_radius) * dist
    cut = 0.5 * (jnp.cos(angle) + 1.0)
    live = mask[...].astype(F32)
    kw = live * cut
    centres = 0.5 + 4.0 * iota((NB, 1), 0).astype(F32) / (NB - 1)
    offset = dist - centres
    radial = jnp.exp(-jnp.square(offset * (NB / 8.0)))
    feat[0:NB, :] = radial
    feat[NB:NFEAT, :] = jnp.zeros((NFEAT - NB, EDGE_DEV), F32)
    feat[NB : NB + 3, :] = d
    wfeat[0:NB, :] = w_rbf[...]
    wfeat[NB:NFEAT, :] = jnp.zeros((NFEAT - NB, D), F32)
    wfeat[NB : NB + 3, :] = w_vec[...]
    rows[0:1, :] = dist
    rows[1:2, :] = cut
    rows[2:3, :] = live
    rows[3:4, :] = kw
    rows[4:5, :] = (-0.5 * math.pi / cutoff_radius) * jnp.sin(angle)
    rows[5:8, :] = jnp.zeros((3, EDGE_DEV), F32)
    scaled = feat[...] * cut
    hi = scaled.astype(BF).astype(F32)
    left = jnp.concatenate([hi, scaled - hi, hi], axis=0).T.astype(BF)
    w = wfeat[...]
    whi = w.astype(BF).astype(F32)
    right = jnp.concatenate([whi, whi, w - whi], axis=0).astype(BF)
    kind = jnp.where(iota((NSPEC, ATOMS_DEV), 0) == species[...], 1.0, 0.0).astype(BF)
    centre = dot_tn(kind, table[...]).astype(BF)
    expand = atom_rows(ATOMS_DEV)
    slot_row = slot[...]
    local = one_hot_lanes(as_column(slot_row.astype(F32)), EDGE_DEV)
    base[...] = dot_nn(left, right) + dot_nn(expand, centre) + dot_nn(local, message[...])
    kwb[...] = jnp.broadcast_to(as_column(kw), (EDGE_DEV, 128))
    far = one_hot_lanes(as_column(remote_index(slot_row)), 3 * SIDE)
    live_rows = expand.astype(F32) * as_column(live)
    mt[...] = dot_tn(live_rows.astype(BF), far)


def rms_factor(x):
    return lax.rsqrt(jnp.mean(x * x, axis=-1, keepdims=True) + norm_eps)


def rms_back(x, r, z):
    inner = jnp.mean(x * z, axis=-1, keepdims=True)
    return r * z - x * (r * r * r * inner)


ROWS = 384
GROUP = 16


def layer_kernel(
    base,
    arr_r,
    arr_m,
    arr_l,
    slot,
    kwb,
    feat,
    rows,
    wfeat,
    gains,
    w_qkv,
    w_out,
    w_up,
    w_down,
    w_energy,
    send,
    tokens,
    energy,
    grad,
    low,
    mid,
    high,
    xs,
    qkv,
    ups,
    probs,
    slope,
    att,
    dqkv,
    acc,
):
    edges = base.shape[0]
    atoms = edges // NBR
    blocks = [slice(i, i + ROWS) for i in range(0, edges, ROWS)]
    lane_head = iota((1, 128), 1) >> 5
    head_lanes = [lane_head == h for h in range(4)]
    row_head = iota((128, 128), 0)
    mask_low = (iota((128, 128), 1) >> 5) * NBR
    block_mask = jnp.where(
        (row_head >= mask_low) & (row_head < mask_low + NBR), 1.0, 0.0
    ).astype(BF)
    score_scale = 1.0 / (math.sqrt(D // HEADS) * score_cap)
    slope_scale = 1.0 / math.sqrt(D // HEADS)

    def spread(x):
        two = jnp.concatenate([x, x], axis=0).astype(BF)
        return jnp.concatenate([two, two, jnp.zeros((32, 128), BF)], axis=0) * block_mask

    def gather_heads(wide):
        out = jnp.where(head_lanes[0], wide[0:NBR], 0.0)
        for h in range(1, 4):
            out = jnp.where(head_lanes[h], wide[h * NBR : (h + 1) * NBR], out)
        return out

    far = one_hot_lanes(as_column(remote_index(slot[...])), 3 * SIDE)
    arrived = jnp.concatenate([arr_r[...], arr_m[...], arr_l[...]], axis=0)
    x = [base[b, :] + dot_nn(far[b], arrived) for b in blocks]

    for layer in range(2):
        for b, v in zip(blocks, x):
            xs[2 * layer, b, :] = v
        gain = gains[2 * layer : 2 * layer + 1, :]
        normed = [(v * rms_factor(v) * gain).astype(BF) for v in x]
        for b, v in zip(blocks, normed):
            qkv[layer, b, :] = dot_nn(v, w_qkv[layer])

        @pl.loop(0, atoms // GROUP)
        def _(step):
            spans = [
                pl.ds(pl.multiple_of(step * (GROUP * NBR) + u * NBR, 8), NBR) for u in range(GROUP)
            ]
            at = [(s, 128 * g) for s in spans for g in range(2)]
            q = [spread(qkv[layer, s, c : c + 128]) for s, c in at]
            k = [qkv[layer, s, D + c : D + c + 128].astype(BF) for s, c in at]
            v = [qkv[layer, s, 2 * D + c : 2 * D + c + 128].astype(BF) for s, c in at]
            t = [dot_nt(kk, qq) for kk, qq in zip(k, q)]
            t = [jnp.tanh(tt * score_scale) for tt in t]
            e = [kwb[s, :] * jnp.exp(score_cap * tt) for (s, c), tt in zip(at, t)]
            p = [ee * (1.0 / jnp.sum(ee, axis=0, keepdims=True)) for ee in e]
            o = [dot_tn(pp.astype(BF), vv) for pp, vv in zip(p, v)]
            o = [gather_heads(oo) for oo in o]
            for i, (s, c) in enumerate(at):
                probs[layer, s, c : c + 128] = p[i]
                slope[layer, s, c : c + 128] = (1.0 - t[i] * t[i]) * slope_scale
                att[s, c : c + 128] = o[i]

        x = [xs[2 * layer, b, :] + dot_nn(att[b, :].astype(BF), w_out[layer]) for b in blocks]
        for b, v in zip(blocks, x):
            xs[2 * layer + 1, b, :] = v
        gain = gains[2 * layer + 1 : 2 * layer + 2, :]
        normed = [(v * rms_factor(v) * gain).astype(BF) for v in x]
        up = [dot_nn(v, w_up[layer]) for v in normed]
        for b, v in zip(blocks, up):
            ups[layer, b, :] = v
        hidden = [(u / (1.0 + jnp.exp(-u))).astype(BF) for u in up]
        x = [v + dot_nn(h, w_down[layer]) for v, h in zip(x, hidden)]

    read = gains[4:5, :] * w_energy[...]
    ones8 = jnp.ones((8, 128), BF)
    readout = []
    dx = []
    for b, v in zip(blocks, x):
        tokens[b, :] = v.astype(BF)
        r = rms_factor(v)
        scaled = v * r
        terms = scaled * read
        part_hi, part_lo = split2(terms[:, 0:128] + terms[:, 128:256])
        readout.append(dot_nt(ones8, part_hi) + dot_nt(ones8, part_lo))
        total = jnp.sum(terms, axis=-1, keepdims=True) * (1.0 / D)
        kw_col = kwb[b, 0:1]
        dx.append((kw_col * r) * (read - scaled * total))
    readout = jnp.concatenate(readout, axis=1)[0:1]
    live = rows[2:3, :]
    kw = rows[3:4, :]
    parts = kw * readout
    part_hi = parts.astype(BF).astype(F32)
    stacked = jnp.concatenate(
        [jnp.broadcast_to(part_hi, (8, edges)), jnp.broadcast_to(parts - part_hi, (8, edges))], axis=0
    ).astype(BF)
    summed = dot_nn(stacked, atom_rows(atoms))
    energy[...] = summed[0:1] + summed[8:9]

    for layer in (1, 0):
        dhid = [dot_nt(v.astype(BF), w_down[layer]) for v in dx]
        dup = []
        for b, dh in zip(blocks, dhid):
            u = ups[layer, b, :]
            sig = 1.0 / (1.0 + jnp.exp(-u))
            dup.append((dh * (sig * (1.0 + u * (1.0 - sig)))).astype(BF))
        gain = gains[2 * layer + 1 : 2 * layer + 2, :]
        dnorm = [dot_nt(v, w_up[layer]) * gain for v in dup]
        new = []
        for b, v, dn in zip(blocks, dx, dnorm):
            xv = xs[2 * layer + 1, b, :]
            new.append(v + rms_back(xv, rms_factor(xv), dn))
        dx = new
        for b, v in zip(blocks, dx):
            att[b, :] = dot_nt(v.astype(BF), w_out[layer])

        @pl.loop(0, atoms // GROUP)
        def _(step):
            spans = [
                pl.ds(pl.multiple_of(step * (GROUP * NBR) + u * NBR, 8), NBR) for u in range(GROUP)
            ]
            at = [(s, 128 * g) for s in spans for g in range(2)]
            do = [spread(att[s, c : c + 128]) for s, c in at]
            v = [qkv[layer, s, 2 * D + c : 2 * D + c + 128].astype(BF) for s, c in at]
            p = [probs[layer, s, c : c + 128] for s, c in at]
            dp = [dot_nt(vv, dd) for vv, dd in zip(v, do)]
            dv = [dot_nn(pp.astype(BF), dd) for pp, dd in zip(p, do)]
            q = [spread(qkv[layer, s, c : c + 128]) for s, c in at]
            k = [qkv[layer, s, D + c : D + c + 128].astype(BF) for s, c in at]
            dl = [pp * (dd - jnp.sum(pp * dd, axis=0, keepdims=True)) for pp, dd in zip(p, dp)]
            ds = [(dd * slope[layer, s, c : c + 128]).astype(BF) for (s, c), dd in zip(at, dl)]
            dk = [dot_nn(dd, qq) for dd, qq in zip(ds, q)]
            dq = [gather_heads(dot_tn(dd, kk)) for dd, kk in zip(ds, k)]
            old = [acc[s, :] for s in spans] if layer == 0 else None
            for i, (s, c) in enumerate(at):
                dqkv[s, c : c + 128] = dq[i]
                dqkv[s, D + c : D + c + 128] = dk[i]
                dqkv[s, 2 * D + c : 2 * D + c + 128] = dv[i]
            for u, s in enumerate(spans):
                total = dl[2 * u] + dl[2 * u + 1]
                acc[s, :] = total if layer == 1 else old[u] + total

        gain = gains[2 * layer : 2 * layer + 1, :]
        dnorm = [dot_nt(dqkv[b, :].astype(BF), w_qkv[layer]) * gain for b in blocks]
        new = []
        for b, v, dn in zip(blocks, dx, dnorm):
            xv = xs[2 * layer, b, :]
            new.append(v + rms_back(xv, rms_factor(xv), dn))
        dx = new

    w = wfeat[...]
    whi = w.astype(BF)
    wlo = (w - whi.astype(F32)).astype(BF)
    back = []
    acc_row = []
    for b, v in zip(blocks, dx):
        hi, lo = split2(v)
        back.append(dot_nt(whi, hi) + dot_nt(whi, lo) + dot_nt(wlo, hi))
        part_hi, part_lo = split2(acc[b, :])
        acc_row.append(dot_nt(ones8, part_hi) + dot_nt(ones8, part_lo))
    back = jnp.concatenate(back, axis=1)
    acc_row = jnp.concatenate(acc_row, axis=1)[0:1]
    dist = rows[0:1, :]
    cut = rows[1:2, :]
    f = feat[...]
    dcut = jnp.sum(f * back, axis=0, keepdims=True) + live * (readout + acc_row / cut)
    centres = 0.5 + 4.0 * iota((NB, 1), 0).astype(F32) / (NB - 1)
    dradial = back[0:NB] * f[0:NB] * (dist - centres)
    ddist = dcut * rows[4:5, :] - (2.0 * (NB / 8.0) ** 2) * cut * jnp.sum(
        dradial, axis=0, keepdims=True
    )
    g = cut * back[NB:NFEAT] + f[NB:NFEAT] * (ddist / dist)
    grad[...] = g
    ghi = g.astype(BF).astype(F32)
    both = jnp.concatenate([ghi, g - ghi], axis=0).astype(BF)
    pick = jnp.where(iota((edges, 3 * SIDE), 0) == send[...], 1.0, 0.0).astype(BF)
    out = dot_nn(both, pick)
    out = out[0:8] + out[8:16]
    low[...] = out[:, 0:SIDE]
    mid[...] = out[:, SIDE : 2 * SIDE]
    high[...] = out[:, 2 * SIDE : 3 * SIDE]


def local_force_kernel(grad, slot, rows, out):
    g = grad[...]
    ghi = g.astype(BF).astype(F32)
    both = jnp.concatenate([ghi, g - ghi], axis=0).astype(BF)
    local = one_hot_lanes(as_column(slot[...].astype(F32)), EDGE_DEV)
    partner = dot_nt(both, local)
    diff = (g - partner[0:8] - partner[8:16]) * rows[2:3, :]
    hi = diff.astype(BF).astype(F32)
    both = jnp.concatenate([hi, diff - hi], axis=0).astype(BF)
    summed = dot_nn(both, atom_rows(ATOMS_DEV))
    out[...] = summed[0:8] + summed[8:16]


def force_kernel(partial, mt, r, m, l, forces):
    pieces = []
    for part in (r, m, l):
        for a in range(3):
            for b in range(3):
                pieces.append(part[b, a])
    table = jnp.concatenate(pieces, axis=1)
    hi = table.astype(BF).astype(F32)
    both = jnp.concatenate([hi, table - hi], axis=0).astype(BF)
    far = dot_nt(both, mt[...].astype(BF))
    forces[...] = (partial[...] - far[0:8] - far[8:16])[0:3]


def vmem_call(kernel, outs, *args, scratch=(), limit=60 * 2**20):
    spec = pl.BlockSpec(memory_space=VMEM)
    return pl.pallas_call(
        kernel,
        out_shape=outs,
        in_specs=[spec] * len(args),
        out_specs=jax.tree.map(lambda _: spec, outs),
        scratch_shapes=list(scratch),
        compiler_params=pltpu.CompilerParams(vmem_limit_bytes=limit),
    )(*args)


def shape(dims, dtype=F32):
    return jax.ShapeDtypeStruct(dims, dtype)


def messages(atom_state, w_neigh, prev_tokens, send):
    side = shape((SIDE, D), BF)
    return vmem_call(
        message_kernel,
        [shape((EDGE_DEV, D), BF), side, side, side],
        atom_state,
        w_neigh,
        prev_tokens,
        send,
    )


def geometry(disp, mask, slot, species, message, table, w_vec, w_rbf):
    return vmem_call(
        geometry_kernel,
        [
            shape((EDGE_DEV, D)),
            shape((EDGE_DEV, 128)),
            shape((NFEAT, EDGE_DEV)),
            shape((8, EDGE_DEV)),
            shape((ATOMS_DEV, 3 * SIDE)),
            shape((NFEAT, D)),
        ],
        disp,
        mask,
        slot,
        species,
        message,
        table,
        w_vec,
        w_rbf,
    )


def layers(base, arr, slot, kwb, feat, rows, wfeat, gains, w_qkv, w_out, w_up, w_down, w_energy, send):
    side = shape((8, SIDE))
    n = EDGE_DEV
    return vmem_call(
        layer_kernel,
        [shape((n, D), BF), shape((1, ATOMS_DEV)), shape((8, n)), side, side, side],
        base,
        *arr,
        slot,
        kwb,
        feat,
        rows,
        wfeat,
        gains,
        w_qkv,
        w_out,
        w_up,
        w_down,
        w_energy,
        send,
        scratch=[
            VMEM((4, n, D), F32),
            VMEM((2, n, 3 * D), F32),
            VMEM((2, n, FF), F32),
            VMEM((2, n, D), F32),
            VMEM((2, n, D), F32),
            VMEM((n, D), F32),
            VMEM((n, 3 * D), F32),
            VMEM((n, 128), F32),
        ],
    )


def to_right(x, axis):
    count = lax.axis_size(axis)
    return lax.ppermute(x, axis, [(i, (i + 1) % count) for i in range(count)])


def to_left(x, axis):
    count = lax.axis_size(axis)
    return lax.ppermute(x, axis, [((i + 1) % count, i) for i in range(count)])


def on_device(
    displacement,
    neighbour_mask,
    reverse_slot,
    send_edges,
    species,
    prev_tokens,
    atom_state,
    species_table,
    w_neigh,
    w_vec,
    w_rbf,
    gains,
    w_qkv,
    w_out,
    w_up,
    w_down,
    w_energy,
):
    centre = jnp.full((SLOTS,), -1, jnp.int32)
    send = jnp.concatenate([send_edges[: 13 * SLOTS], centre, send_edges[13 * SLOTS :]])
    send = send.reshape(1, 3 * SIDE)
    slot = reverse_slot.reshape(1, EDGE_DEV)
    message, low, mid, high = messages(atom_state, w_neigh, prev_tokens, send)
    right, left = to_right(high, "gx"), to_left(low, "gx")
    base, kwb, feat, rows, mt, wfeat = geometry(
        displacement,
        neighbour_mask.reshape(1, EDGE_DEV),
        slot,
        species.reshape(1, ATOMS_DEV),
        message,
        species_table,
        w_vec,
        w_rbf,
    )
    cells = [v.reshape(3, 3, SLOTS, D) for v in (right, mid, left)]
    high, mid, low = (jnp.stack([v[i] for v in cells]) for i in (2, 1, 0))
    right, left = to_right(high, "gy"), to_left(low, "gy")
    cells = (right, mid, left)
    high, mid, low = (jnp.stack([v[:, i] for v in cells], axis=1) for i in (2, 1, 0))
    right, left = to_right(high, "gz"), to_left(low, "gz")
    arr = [v.reshape(SIDE, D) for v in (right, mid, left)]
    tokens, energy, grad, low, mid, high = layers(
        base,
        arr,
        slot,
        kwb,
        feat,
        rows,
        wfeat,
        gains,
        w_qkv,
        w_out,
        w_up,
        w_down,
        w_energy.reshape(1, D),
        send,
    )
    right, left = to_right(high, "gx"), to_left(low, "gx")
    partial = vmem_call(local_force_kernel, shape((8, ATOMS_DEV)), grad, slot, rows)
    cells = jnp.stack([right, mid, left])
    cut = 3 * SLOTS
    right, left = to_right(cells[:, :, 2 * cut :], "gy"), to_left(cells[:, :, :cut], "gy")
    cells = jnp.stack([right, cells[:, :, cut : 2 * cut], left])
    cut = SLOTS
    right, left = to_right(cells[..., 2 * cut :], "gz"), to_left(cells[..., :cut], "gz")
    mid = cells[..., cut : 2 * cut]
    forces = vmem_call(force_kernel, shape((3, ATOMS_DEV)), partial, mt, right, mid, left)
    return (tokens, energy.reshape(ATOMS_DEV), forces)


def solution(mesh):
    return jax.shard_map(
        on_device,
        mesh=mesh,
        in_specs=(
            P(None, ("gx", "gy", "gz")),
            P(("gx", "gy", "gz")),
            P(("gx", "gy", "gz")),
            P(("gx", "gy", "gz")),
            P(("gx", "gy", "gz")),
            P(("gx", "gy", "gz"), None),
            P(("gx", "gy", "gz"), None),
            P(),
            P(),
            P(),
            P(),
            P(),
            P(),
            P(),
            P(),
            P(),
            P(),
        ),
        out_specs=(P(("gx", "gy", "gz"), None), P(("gx", "gy", "gz")), P(None, ("gx", "gy", "gz"))),
        check_vma=False,
    )
```

```python
import math

import jax
import jax.numpy as jnp
from jax import lax
from jax.experimental import pallas as pl
from jax.experimental.pallas import tpu as pltpu
from jax.sharding import PartitionSpec as P

HEADS = 8
NBR = 24
ATOMS_DEV = 32
EDGE_DEV = 768
D = 256
FF = 512
NB = 64
NSPEC = 85
SLOTS = 16
SIDE = 9 * SLOTS
NFEAT = 72
score_cap = 8.0
cutoff_radius = 5.0
norm_eps = 1e-06
AXES = ("gx", "gy", "gz")

BF = jnp.bfloat16
F32 = jnp.float32
VMEM = pltpu.VMEM


def dot_nn(a, b):
    return lax.dot_general(a, b, (((1,), (0,)), ((), ())), preferred_element_type=F32)


def dot_nt(a, b):
    return lax.dot_general(a, b, (((1,), (1,)), ((), ())), preferred_element_type=F32)


def dot_tn(a, b):
    return lax.dot_general(a, b, (((0,), (0,)), ((), ())), preferred_element_type=F32)


def iota(shape, axis):
    return lax.broadcasted_iota(jnp.int32, shape, axis)


def split2(x):
    hi = x.astype(BF)
    lo = (x - hi.astype(F32)).astype(BF)
    return hi, lo


def as_column(row):
    return jnp.broadcast_to(row, (8, row.shape[1])).T[:, 0:1]


def atom_rows(count, dtype=BF):
    edge = iota((count * NBR, count), 0)
    first = iota((count * NBR, count), 1) * NBR
    return jnp.where((edge >= first) & (edge < first + NBR), 1.0, 0.0).astype(dtype)


def one_hot_lanes(column, width):
    lanes = iota((column.shape[0], width), 1).astype(F32)
    return jnp.where(lanes == column, 1.0, 0.0).astype(BF)


def message_kernel(state, w_neigh, prev, send, message, low, mid, high, where, order):
    projected = dot_nn(state[...], w_neigh[...])
    expand = atom_rows(ATOMS_DEV)
    hi, lo = split2(projected)
    rest = (projected - hi.astype(F32) - lo.astype(F32)).astype(BF)
    wide = dot_nn(expand, hi) + dot_nn(expand, lo) + dot_nn(expand, rest)
    out = (prev[...].astype(F32) + wide).astype(BF)
    message[...] = out
    count = 26 * SLOTS
    sent = jnp.broadcast_to(send[...].reshape(1, count).astype(F32), (8, count)).T
    flips = [lax.axis_index(axis) & 1 for axis in AXES]
    for bucket in range(27):
        place = 0
        for axis, digit in enumerate((bucket // 9, bucket // 3 % 3, bucket % 3)):
            place = place * 3 + digit + flips[axis] * (2 - 2 * digit)
        rows = pl.ds(pl.multiple_of(place * SLOTS, SLOTS), SLOTS)
        if bucket == 13:
            order[rows, :] = jnp.full((SLOTS, 8), -1.0, F32)
        else:
            start = (bucket - (bucket > 13)) * SLOTS
            order[rows, :] = sent[start : start + SLOTS]
    column = order[...]
    where[...] = column
    payload = dot_nn(one_hot_lanes(column[:, 0:1], EDGE_DEV), out).astype(BF)
    low[...] = payload[0:SIDE]
    mid[...] = payload[SIDE : 2 * SIDE]
    high[...] = payload[2 * SIDE : 3 * SIDE]


def remote_index(slot):
    far = slot - EDGE_DEV
    bucket = far >> 4
    pair = (bucket * 11) >> 5
    first = (pair * 11) >> 5
    digits = [first, pair - 3 * first, bucket - 3 * pair]
    for i, axis in enumerate(AXES):
        flip = lax.axis_index(axis) & 1
        digits[i] = digits[i] + flip * (2 - 2 * digits[i])
    place = digits[2] * SIDE + (digits[0] * 3 + digits[1]) * SLOTS + (far & 15)
    return jnp.where(far >= 0, place, -1).astype(F32)


def geometry_kernel(
    disp, mask, slot, species, message, table, w_vec, w_rbf, base, kwb, feat, rows, mt, wfeat
):
    d = disp[...]
    dist = jnp.sqrt(jnp.sum(d * d, axis=0, keepdims=True) + 0.5)
    angle = (math.pi / cutoff_radius) * dist
    cut = 0.5 * (jnp.cos(angle) + 1.0)
    live = mask[...].reshape(1, EDGE_DEV).astype(F32)
    kw = live * cut
    centres = 0.5 + 4.0 * iota((NB, 1), 0).astype(F32) / (NB - 1)
    offset = dist - centres
    radial = jnp.exp(-jnp.square(offset * (NB / 8.0)))
    feat[0:NB, :] = radial
    feat[NB:NFEAT, :] = jnp.zeros((NFEAT - NB, EDGE_DEV), F32)
    feat[NB : NB + 3, :] = d
    wfeat[0:NB, :] = w_rbf[...]
    wfeat[NB:NFEAT, :] = jnp.zeros((NFEAT - NB, D), F32)
    wfeat[NB : NB + 3, :] = w_vec[...]
    rows[0:1, :] = dist
    rows[1:2, :] = cut
    rows[2:3, :] = live
    rows[3:4, :] = kw
    rows[4:5, :] = (-0.5 * math.pi / cutoff_radius) * jnp.sin(angle)
    rows[5:8, :] = jnp.zeros((3, EDGE_DEV), F32)
    scaled = feat[...] * cut
    hi = scaled.astype(BF).astype(F32)
    left = jnp.concatenate([hi, scaled - hi, hi], axis=0).T.astype(BF)
    w = wfeat[...]
    whi = w.astype(BF).astype(F32)
    right = jnp.concatenate([whi, whi, w - whi], axis=0).astype(BF)
    kind = jnp.where(iota((NSPEC, ATOMS_DEV), 0) == species[...].reshape(1, ATOMS_DEV), 1.0, 0.0).astype(BF)
    centre = dot_tn(kind, table[...]).astype(BF)
    expand = atom_rows(ATOMS_DEV)
    slot_row = slot[...].reshape(1, EDGE_DEV)
    local = one_hot_lanes(as_column(slot_row.astype(F32)), EDGE_DEV)
    base[...] = dot_nn(left, right) + dot_nn(expand, centre) + dot_nn(local, message[...])
    kwb[...] = jnp.broadcast_to(as_column(kw), (EDGE_DEV, 128))
    far = one_hot_lanes(as_column(remote_index(slot_row)), 3 * SIDE)
    live_rows = expand.astype(F32) * as_column(live)
    mt[...] = dot_tn(live_rows.astype(BF), far)


def rms_factor(x):
    return lax.rsqrt(jnp.mean(x * x, axis=-1, keepdims=True) + norm_eps)


def rms_back(x, r, z):
    inner = jnp.mean(x * z, axis=-1, keepdims=True)
    return r * z - x * (r * r * r * inner)


ROWS = 384
GROUP = 16


def layer_kernel(
    base,
    arr_r,
    arr_m,
    arr_l,
    slot,
    kwb,
    feat,
    rows,
    wfeat,
    gains,
    w_qkv,
    w_out,
    w_up,
    w_down,
    w_energy,
    send,
    tokens,
    energy,
    grad,
    low,
    mid,
    high,
    xs,
    qkv,
    ups,
    probs,
    slope,
    att,
    dqkv,
    acc,
):
    edges = base.shape[0]
    atoms = edges // NBR
    blocks = [slice(i, i + ROWS) for i in range(0, edges, ROWS)]
    lane_head = iota((1, 128), 1) >> 5
    head_lanes = [lane_head == h for h in range(4)]
    row_head = iota((128, 128), 0)
    mask_low = (iota((128, 128), 1) >> 5) * NBR
    block_mask = jnp.where(
        (row_head >= mask_low) & (row_head < mask_low + NBR), 1.0, 0.0
    ).astype(BF)
    score_scale = 1.0 / (math.sqrt(D // HEADS) * score_cap)
    slope_scale = 1.0 / math.sqrt(D // HEADS)

    def spread(x):
        two = jnp.concatenate([x, x], axis=0).astype(BF)
        return jnp.concatenate([two, two, jnp.zeros((32, 128), BF)], axis=0) * block_mask

    def gather_heads(wide):
        out = jnp.where(head_lanes[0], wide[0:NBR], 0.0)
        for h in range(1, 4):
            out = jnp.where(head_lanes[h], wide[h * NBR : (h + 1) * NBR], out)
        return out

    far = one_hot_lanes(as_column(remote_index(slot[...].reshape(1, EDGE_DEV))), 3 * SIDE)
    arrived = jnp.concatenate([arr_r[...], arr_m[...], arr_l[...]], axis=0)
    x = [base[b, :] + dot_nn(far[b], arrived) for b in blocks]

    for layer in range(2):
        for b, v in zip(blocks, x):
            xs[2 * layer, b, :] = v
        gain = gains[2 * layer : 2 * layer + 1, :]
        normed = [(v * rms_factor(v) * gain).astype(BF) for v in x]
        for b, v in zip(blocks, normed):
            qkv[layer, b, :] = dot_nn(v, w_qkv[layer])

        @pl.loop(0, atoms // GROUP)
        def _(step):
            spans = [
                pl.ds(pl.multiple_of(step * (GROUP * NBR) + u * NBR, 8), NBR) for u in range(GROUP)
            ]
            at = [(s, 128 * g) for s in spans for g in range(2)]
            q = [spread(qkv[layer, s, c : c + 128]) for s, c in at]
            k = [qkv[layer, s, D + c : D + c + 128].astype(BF) for s, c in at]
            v = [qkv[layer, s, 2 * D + c : 2 * D + c + 128].astype(BF) for s, c in at]
            t = [dot_nt(kk, qq) for kk, qq in zip(k, q)]
            t = [jnp.tanh(tt * score_scale) for tt in t]
            e = [kwb[s, :] * jnp.exp(score_cap * tt) for (s, c), tt in zip(at, t)]
            p = [ee * (1.0 / jnp.sum(ee, axis=0, keepdims=True)) for ee in e]
            o = [dot_tn(pp.astype(BF), vv) for pp, vv in zip(p, v)]
            o = [gather_heads(oo) for oo in o]
            for i, (s, c) in enumerate(at):
                probs[layer, s, c : c + 128] = p[i]
                slope[layer, s, c : c + 128] = (1.0 - t[i] * t[i]) * slope_scale
                att[s, c : c + 128] = o[i]

        x = [xs[2 * layer, b, :] + dot_nn(att[b, :].astype(BF), w_out[layer]) for b in blocks]
        for b, v in zip(blocks, x):
            xs[2 * layer + 1, b, :] = v
        gain = gains[2 * layer + 1 : 2 * layer + 2, :]
        normed = [(v * rms_factor(v) * gain).astype(BF) for v in x]
        up = [dot_nn(v, w_up[layer]) for v in normed]
        for b, v in zip(blocks, up):
            ups[layer, b, :] = v
        hidden = [(u / (1.0 + jnp.exp(-u))).astype(BF) for u in up]
        x = [v + dot_nn(h, w_down[layer]) for v, h in zip(x, hidden)]

    read = gains[4:5, :] * w_energy[...]
    ones8 = jnp.ones((8, 128), BF)
    readout = []
    dx = []
    for b, v in zip(blocks, x):
        tokens[b, :] = v.astype(BF)
        r = rms_factor(v)
        scaled = v * r
        terms = scaled * read
        part_hi, part_lo = split2(terms[:, 0:128] + terms[:, 128:256])
        readout.append(dot_nt(ones8, part_hi) + dot_nt(ones8, part_lo))
        total = jnp.sum(terms, axis=-1, keepdims=True) * (1.0 / D)
        kw_col = kwb[b, 0:1]
        dx.append((kw_col * r) * (read - scaled * total))
    readout = jnp.concatenate(readout, axis=1)[0:1]
    live = rows[2:3, :]
    kw = rows[3:4, :]
    parts = kw * readout
    part_hi = parts.astype(BF).astype(F32)
    stacked = jnp.concatenate(
        [jnp.broadcast_to(part_hi, (8, edges)), jnp.broadcast_to(parts - part_hi, (8, edges))], axis=0
    ).astype(BF)
    summed = dot_nn(stacked, atom_rows(atoms))
    energy[...] = summed[0:1] + summed[8:9]

    for layer in (1, 0):
        dhid = [dot_nt(v.astype(BF), w_down[layer]) for v in dx]
        dup = []
        for b, dh in zip(blocks, dhid):
            u = ups[layer, b, :]
            sig = 1.0 / (1.0 + jnp.exp(-u))
            dup.append((dh * (sig * (1.0 + u * (1.0 - sig)))).astype(BF))
        gain = gains[2 * layer + 1 : 2 * layer + 2, :]
        dnorm = [dot_nt(v, w_up[layer]) * gain for v in dup]
        new = []
        for b, v, dn in zip(blocks, dx, dnorm):
            xv = xs[2 * layer + 1, b, :]
            new.append(v + rms_back(xv, rms_factor(xv), dn))
        dx = new
        for b, v in zip(blocks, dx):
            att[b, :] = dot_nt(v.astype(BF), w_out[layer])

        @pl.loop(0, atoms // GROUP)
        def _(step):
            spans = [
                pl.ds(pl.multiple_of(step * (GROUP * NBR) + u * NBR, 8), NBR) for u in range(GROUP)
            ]
            at = [(s, 128 * g) for s in spans for g in range(2)]
            do = [spread(att[s, c : c + 128]) for s, c in at]
            v = [qkv[layer, s, 2 * D + c : 2 * D + c + 128].astype(BF) for s, c in at]
            p = [probs[layer, s, c : c + 128] for s, c in at]
            dp = [dot_nt(vv, dd) for vv, dd in zip(v, do)]
            dv = [dot_nn(pp.astype(BF), dd) for pp, dd in zip(p, do)]
            q = [spread(qkv[layer, s, c : c + 128]) for s, c in at]
            k = [qkv[layer, s, D + c : D + c + 128].astype(BF) for s, c in at]
            dl = [pp * (dd - jnp.sum(pp * dd, axis=0, keepdims=True)) for pp, dd in zip(p, dp)]
            ds = [(dd * slope[layer, s, c : c + 128]).astype(BF) for (s, c), dd in zip(at, dl)]
            dk = [dot_nn(dd, qq) for dd, qq in zip(ds, q)]
            dq = [gather_heads(dot_tn(dd, kk)) for dd, kk in zip(ds, k)]
            old = [acc[s, :] for s in spans] if layer == 0 else None
            for i, (s, c) in enumerate(at):
                dqkv[s, c : c + 128] = dq[i]
                dqkv[s, D + c : D + c + 128] = dk[i]
                dqkv[s, 2 * D + c : 2 * D + c + 128] = dv[i]
            for u, s in enumerate(spans):
                total = dl[2 * u] + dl[2 * u + 1]
                acc[s, :] = total if layer == 1 else old[u] + total

        gain = gains[2 * layer : 2 * layer + 1, :]
        dnorm = [dot_nt(dqkv[b, :].astype(BF), w_qkv[layer]) * gain for b in blocks]
        new = []
        for b, v, dn in zip(blocks, dx, dnorm):
            xv = xs[2 * layer, b, :]
            new.append(v + rms_back(xv, rms_factor(xv), dn))
        dx = new

    w = wfeat[...]
    whi = w.astype(BF)
    wlo = (w - whi.astype(F32)).astype(BF)
    back = []
    acc_row = []
    for b, v in zip(blocks, dx):
        hi, lo = split2(v)
        back.append(dot_nt(whi, hi) + dot_nt(whi, lo) + dot_nt(wlo, hi))
        part_hi, part_lo = split2(acc[b, :])
        acc_row.append(dot_nt(ones8, part_hi) + dot_nt(ones8, part_lo))
    back = jnp.concatenate(back, axis=1)
    acc_row = jnp.concatenate(acc_row, axis=1)[0:1]
    dist = rows[0:1, :]
    cut = rows[1:2, :]
    f = feat[...]
    dcut = jnp.sum(f * back, axis=0, keepdims=True) + live * (readout + acc_row / cut)
    centres = 0.5 + 4.0 * iota((NB, 1), 0).astype(F32) / (NB - 1)
    dradial = back[0:NB] * f[0:NB] * (dist - centres)
    ddist = dcut * rows[4:5, :] - (2.0 * (NB / 8.0) ** 2) * cut * jnp.sum(
        dradial, axis=0, keepdims=True
    )
    g = cut * back[NB:NFEAT] + f[NB:NFEAT] * (ddist / dist)
    grad[...] = g
    ghi = g.astype(BF).astype(F32)
    both = jnp.concatenate([ghi, g - ghi], axis=0).astype(BF)
    out = dot_nt(both, one_hot_lanes(send[:, 0:1], edges))
    out = out[0:8] + out[8:16]
    low[...] = out[:, 0:SIDE]
    mid[...] = out[:, SIDE : 2 * SIDE]
    high[...] = out[:, 2 * SIDE : 3 * SIDE]


def local_force_kernel(grad, slot, rows, out):
    g = grad[...]
    ghi = g.astype(BF).astype(F32)
    both = jnp.concatenate([ghi, g - ghi], axis=0).astype(BF)
    local = one_hot_lanes(as_column(slot[...].reshape(1, EDGE_DEV).astype(F32)), EDGE_DEV)
    partner = dot_nt(both, local)
    diff = (g - partner[0:8] - partner[8:16]) * rows[2:3, :]
    hi = diff.astype(BF).astype(F32)
    both = jnp.concatenate([hi, diff - hi], axis=0).astype(BF)
    summed = dot_nn(both, atom_rows(ATOMS_DEV))
    out[...] = summed[0:8] + summed[8:16]


def force_kernel(partial, mt, r, m, l, forces):
    pieces = []
    for part in (r, m, l):
        for a in range(3):
            for b in range(3):
                pieces.append(part[b, a])
    table = jnp.concatenate(pieces, axis=1)
    hi = table.astype(BF).astype(F32)
    both = jnp.concatenate([hi, table - hi], axis=0).astype(BF)
    far = dot_nt(both, mt[...].astype(BF))
    forces[...] = (partial[...] - far[0:8] - far[8:16])[0:3]


def vmem_call(kernel, outs, *args, scratch=(), limit=60 * 2**20):
    spec = pl.BlockSpec(memory_space=VMEM)
    return pl.pallas_call(
        kernel,
        out_shape=outs,
        in_specs=[spec] * len(args),
        out_specs=jax.tree.map(lambda _: spec, outs),
        scratch_shapes=list(scratch),
        compiler_params=pltpu.CompilerParams(vmem_limit_bytes=limit),
    )(*args)


def shape(dims, dtype=F32):
    return jax.ShapeDtypeStruct(dims, dtype)


def messages(atom_state, w_neigh, prev_tokens, send):
    side = shape((SIDE, D), BF)
    return vmem_call(
        message_kernel,
        [shape((EDGE_DEV, D), BF), side, side, side, shape((3 * SIDE, 8))],
        atom_state,
        w_neigh,
        prev_tokens,
        send,
        scratch=[VMEM((3 * SIDE, 8), F32)],
    )


def geometry(disp, mask, slot, species, message, table, w_vec, w_rbf):
    return vmem_call(
        geometry_kernel,
        [
            shape((EDGE_DEV, D)),
            shape((EDGE_DEV, 128)),
            shape((NFEAT, EDGE_DEV)),
            shape((8, EDGE_DEV)),
            shape((ATOMS_DEV, 3 * SIDE)),
            shape((NFEAT, D)),
        ],
        disp,
        mask,
        slot,
        species,
        message,
        table,
        w_vec,
        w_rbf,
    )


def layers(base, arr, slot, kwb, feat, rows, wfeat, gains, w_qkv, w_out, w_up, w_down, w_energy, send):
    side = shape((8, SIDE))
    n = EDGE_DEV
    return vmem_call(
        layer_kernel,
        [shape((n, D), BF), shape((1, ATOMS_DEV)), shape((8, n)), side, side, side],
        base,
        *arr,
        slot,
        kwb,
        feat,
        rows,
        wfeat,
        gains,
        w_qkv,
        w_out,
        w_up,
        w_down,
        w_energy,
        send,
        scratch=[
            VMEM((4, n, D), F32),
            VMEM((2, n, 3 * D), F32),
            VMEM((2, n, FF), F32),
            VMEM((2, n, D), F32),
            VMEM((2, n, D), F32),
            VMEM((n, D), F32),
            VMEM((n, 3 * D), F32),
            VMEM((n, 128), F32),
        ],
    )


def exchange(low, high, axis):
    count = lax.axis_size(axis)
    outer = [(i, (i + 1 if i % 2 else i - 1) % count) for i in range(count)]
    inner = [(i, i + 1 if i % 2 == 0 else i - 1) for i in range(count)]
    return lax.ppermute(low, axis, outer), lax.ppermute(high, axis, inner)


def on_device(
    displacement,
    neighbour_mask,
    reverse_slot,
    send_edges,
    species,
    prev_tokens,
    atom_state,
    species_table,
    w_neigh,
    w_vec,
    w_rbf,
    gains,
    w_qkv,
    w_out,
    w_up,
    w_down,
    w_energy,
):
    message, low, mid, high, where = messages(atom_state, w_neigh, prev_tokens, send_edges)
    low, high = exchange(low, high, "gx")
    cells = [v.reshape(3, 3, SLOTS, D) for v in (low, mid, high)]
    low, mid, high = (jnp.stack([v[i] for v in cells]) for i in range(3))
    low, mid, high = lax.optimization_barrier((low, mid, high))
    low, high = exchange(low, high, "gy")
    cells = (low, mid, high)
    low, mid, high = (jnp.stack([v[:, i] for v in cells], axis=1) for i in range(3))
    low, mid, high, late = lax.optimization_barrier((low, mid, high, displacement))
    low, high = exchange(low, high, "gz")
    base, kwb, feat, rows, mt, wfeat = geometry(
        late, neighbour_mask, reverse_slot, species, message, species_table, w_vec, w_rbf
    )
    arr = [v.reshape(SIDE, D) for v in (low, mid, high)]
    tokens, energy, grad, low, mid, high = layers(
        base,
        arr,
        reverse_slot,
        kwb,
        feat,
        rows,
        wfeat,
        gains,
        w_qkv,
        w_out,
        w_up,
        w_down,
        w_energy.reshape(1, D),
        where,
    )
    low, high = exchange(low, high, "gx")
    cells = jnp.stack([low, mid, high])
    cut = 3 * SLOTS
    low, mid, high = (cells[:, :, i * cut : (i + 1) * cut] for i in range(3))
    low, high = exchange(low, high, "gy")
    cells = jnp.stack([low, mid, high])
    cut = SLOTS
    low, mid, high = (cells[..., i * cut : (i + 1) * cut] for i in range(3))
    low, mid, high, late = lax.optimization_barrier((low, mid, high, grad))
    low, high = exchange(low, high, "gz")
    partial = vmem_call(
        local_force_kernel, shape((8, ATOMS_DEV)), late, reverse_slot, rows
    )
    forces = vmem_call(force_kernel, shape((3, ATOMS_DEV)), partial, mt, low, mid, high)
    return (tokens, energy.reshape(ATOMS_DEV), forces)


def solution(mesh):
    return jax.shard_map(
        on_device,
        mesh=mesh,
        in_specs=(
            P(None, ("gx", "gy", "gz")),
            P(("gx", "gy", "gz")),
            P(("gx", "gy", "gz")),
            P(("gx", "gy", "gz")),
            P(("gx", "gy", "gz")),
            P(("gx", "gy", "gz"), None),
            P(("gx", "gy", "gz"), None),
            P(),
            P(),
            P(),
            P(),
            P(),
            P(),
            P(),
            P(),
            P(),
            P(),
        ),
        out_specs=(P(("gx", "gy", "gz"), None), P(("gx", "gy", "gz")), P(None, ("gx", "gy", "gz"))),
        check_vma=False,
    )
```

```python
import math

import jax
import jax.numpy as jnp
from jax import lax
from jax.experimental import pallas as pl
from jax.experimental.pallas import tpu as pltpu
from jax.sharding import PartitionSpec as P

HEADS = 8
NBR = 24
ATOMS_DEV = 32
EDGE_DEV = 768
D = 256
FF = 512
NB = 64
NSPEC = 85
SLOTS = 16
SIDE = 9 * SLOTS
NFEAT = 72
score_cap = 8.0
cutoff_radius = 5.0
norm_eps = 1e-06
AXES = ("gx", "gy", "gz")

BF = jnp.bfloat16
F32 = jnp.float32
VMEM = pltpu.VMEM


def dot_nn(a, b):
    return lax.dot_general(a, b, (((1,), (0,)), ((), ())), preferred_element_type=F32)


def dot_nt(a, b):
    return lax.dot_general(a, b, (((1,), (1,)), ((), ())), preferred_element_type=F32)


def dot_tn(a, b):
    return lax.dot_general(a, b, (((0,), (0,)), ((), ())), preferred_element_type=F32)


def iota(shape, axis):
    return lax.broadcasted_iota(jnp.int32, shape, axis)


def split2(x):
    hi = x.astype(BF)
    lo = (x - hi.astype(F32)).astype(BF)
    return hi, lo


def as_column(row):
    return jnp.broadcast_to(row, (8, row.shape[1])).T[:, 0:1]


def atom_rows(count, dtype=BF):
    edge = iota((count * NBR, count), 0)
    first = iota((count * NBR, count), 1) * NBR
    return jnp.where((edge >= first) & (edge < first + NBR), 1.0, 0.0).astype(dtype)


def one_hot_lanes(column, width):
    lanes = iota((column.shape[0], width), 1).astype(F32)
    return jnp.where(lanes == column, 1.0, 0.0).astype(BF)


def message_kernel(state, w_neigh, prev, send, message, low, mid, high, where, order):
    projected = dot_nn(state[...], w_neigh[...])
    expand = atom_rows(ATOMS_DEV)
    hi, lo = split2(projected)
    rest = (projected - hi.astype(F32) - lo.astype(F32)).astype(BF)
    wide = dot_nn(expand, hi) + dot_nn(expand, lo) + dot_nn(expand, rest)
    out = (prev[...].astype(F32) + wide).astype(BF)
    message[...] = out
    count = 26 * SLOTS
    sent = jnp.broadcast_to(send[...].reshape(1, count).astype(F32), (8, count)).T
    flips = [lax.axis_index(axis) & 1 for axis in AXES]
    for bucket in range(27):
        place = 0
        for axis, digit in enumerate((bucket // 9, bucket // 3 % 3, bucket % 3)):
            place = place * 3 + digit + flips[axis] * (2 - 2 * digit)
        rows = pl.ds(pl.multiple_of(place * SLOTS, SLOTS), SLOTS)
        if bucket == 13:
            order[rows, :] = jnp.full((SLOTS, 8), -1.0, F32)
        else:
            start = (bucket - (bucket > 13)) * SLOTS
            order[rows, :] = sent[start : start + SLOTS]
    column = order[...]
    where[...] = column
    payload = dot_nn(one_hot_lanes(column[:, 0:1], EDGE_DEV), out).astype(BF)
    low[...] = payload[0:SIDE]
    mid[...] = payload[SIDE : 2 * SIDE]
    high[...] = payload[2 * SIDE : 3 * SIDE]


def remote_index(slot):
    far = slot - EDGE_DEV
    bucket = far >> 4
    pair = (bucket * 11) >> 5
    first = (pair * 11) >> 5
    digits = [first, pair - 3 * first, bucket - 3 * pair]
    for i, axis in enumerate(AXES):
        flip = lax.axis_index(axis) & 1
        digits[i] = digits[i] + flip * (2 - 2 * digits[i])
    place = digits[2] * SIDE + (digits[0] * 3 + digits[1]) * SLOTS + (far & 15)
    return jnp.where(far >= 0, place, -1).astype(F32)


def lookup_kernel(slot, mask, where, far, pick, mt):
    slot_row = slot[...].reshape(1, EDGE_DEV)
    live = mask[...].reshape(1, EDGE_DEV).astype(F32)
    hot = one_hot_lanes(as_column(remote_index(slot_row)), 3 * SIDE)
    far[...] = hot
    pick[...] = one_hot_lanes(where[:, 0:1], EDGE_DEV)
    live_rows = atom_rows(ATOMS_DEV, F32) * as_column(live)
    mt[...] = dot_tn(live_rows.astype(BF), hot)


def geometry_kernel(
    disp, mask, slot, species, message, table, w_vec, w_rbf, base, kwb, feat, rows, wfeat
):
    d = disp[...]
    dist = jnp.sqrt(jnp.sum(d * d, axis=0, keepdims=True) + 0.5)
    angle = (math.pi / cutoff_radius) * dist
    cut = 0.5 * (jnp.cos(angle) + 1.0)
    live = mask[...].reshape(1, EDGE_DEV).astype(F32)
    kw = live * cut
    centres = 0.5 + 4.0 * iota((NB, 1), 0).astype(F32) / (NB - 1)
    offset = dist - centres
    radial = jnp.exp(-jnp.square(offset * (NB / 8.0)))
    feat[0:NB, :] = radial
    feat[NB:NFEAT, :] = jnp.zeros((NFEAT - NB, EDGE_DEV), F32)
    feat[NB : NB + 3, :] = d
    wfeat[0:NB, :] = w_rbf[...]
    wfeat[NB:NFEAT, :] = jnp.zeros((NFEAT - NB, D), F32)
    wfeat[NB : NB + 3, :] = w_vec[...]
    rows[0:1, :] = dist
    rows[1:2, :] = cut
    rows[2:3, :] = live
    rows[3:4, :] = kw
    rows[4:5, :] = (-0.5 * math.pi / cutoff_radius) * jnp.sin(angle)
    rows[5:8, :] = jnp.zeros((3, EDGE_DEV), F32)
    scaled = feat[...] * cut
    hi = scaled.astype(BF).astype(F32)
    left = jnp.concatenate([hi, scaled - hi, hi], axis=0).T.astype(BF)
    w = wfeat[...]
    whi = w.astype(BF).astype(F32)
    right = jnp.concatenate([whi, whi, w - whi], axis=0).astype(BF)
    kind = jnp.where(iota((NSPEC, ATOMS_DEV), 0) == species[...].reshape(1, ATOMS_DEV), 1.0, 0.0).astype(BF)
    centre = dot_tn(kind, table[...]).astype(BF)
    expand = atom_rows(ATOMS_DEV)
    slot_row = slot[...].reshape(1, EDGE_DEV)
    local = one_hot_lanes(as_column(slot_row.astype(F32)), EDGE_DEV)
    base[...] = dot_nn(left, right) + dot_nn(expand, centre) + dot_nn(local, message[...])
    kwb[...] = jnp.broadcast_to(as_column(kw), (EDGE_DEV, 128))


def sigmoid(u):
    return 0.5 * jnp.tanh(0.5 * u) + 0.5


def rms_factor(x):
    return lax.rsqrt(jnp.mean(x * x, axis=-1, keepdims=True) + norm_eps)


def rms_back(x, r, z):
    inner = jnp.mean(x * z, axis=-1, keepdims=True)
    return r * z - x * (r * r * r * inner)


LIMIT = 40 * 2**20
ROWS = 384
GROUP = 16


def layer_kernel(
    base,
    arr_r,
    arr_m,
    arr_l,
    far,
    kwb,
    feat,
    rows,
    wfeat,
    gains,
    w_qkv,
    w_out,
    w_up,
    w_down,
    w_energy,
    pick,
    tokens,
    reads,
    grad,
    low,
    mid,
    high,
    xs,
    qkv,
    ups,
    probs,
    slope,
    att,
    dqkv,
    acc,
):
    edges = base.shape[0]
    atoms = edges // NBR
    blocks = [slice(i, i + ROWS) for i in range(0, edges, ROWS)]
    lane_head = iota((1, 128), 1) >> 5
    head_lanes = [lane_head == h for h in range(4)]
    row_head = iota((128, 128), 0)
    mask_low = (iota((128, 128), 1) >> 5) * NBR
    block_mask = jnp.where(
        (row_head >= mask_low) & (row_head < mask_low + NBR), 1.0, 0.0
    ).astype(BF)
    score_scale = 1.0 / (math.sqrt(D // HEADS) * score_cap)
    slope_scale = 1.0 / math.sqrt(D // HEADS)

    def spread(x):
        two = jnp.concatenate([x, x], axis=0).astype(BF)
        return jnp.concatenate([two, two, jnp.zeros((32, 128), BF)], axis=0) * block_mask

    def gather_heads(wide):
        out = jnp.where(head_lanes[0], wide[0:NBR], 0.0)
        for h in range(1, 4):
            out = jnp.where(head_lanes[h], wide[h * NBR : (h + 1) * NBR], out)
        return out

    arrived = jnp.concatenate([arr_r[...], arr_m[...], arr_l[...]], axis=0)
    x = [base[b, :] + dot_nn(far[b, :], arrived) for b in blocks]

    for layer in range(2):
        for b, v in zip(blocks, x):
            xs[2 * layer, b, :] = v
        gain = gains[2 * layer : 2 * layer + 1, :]
        normed = [(v * rms_factor(v) * gain).astype(BF) for v in x]
        for b, v in zip(blocks, normed):
            qkv[layer, b, :] = dot_nn(v, w_qkv[layer])

        @pl.loop(0, atoms // GROUP)
        def _(step):
            spans = [
                pl.ds(pl.multiple_of(step * (GROUP * NBR) + u * NBR, 8), NBR) for u in range(GROUP)
            ]
            at = [(s, 128 * g) for s in spans for g in range(2)]
            q = [spread(qkv[layer, s, c : c + 128]) for s, c in at]
            k = [qkv[layer, s, D + c : D + c + 128].astype(BF) for s, c in at]
            v = [qkv[layer, s, 2 * D + c : 2 * D + c + 128].astype(BF) for s, c in at]
            t = [dot_nt(kk, qq) for kk, qq in zip(k, q)]
            t = [jnp.tanh(tt * score_scale) for tt in t]
            e = [kwb[s, :] * jnp.exp(score_cap * tt) for (s, c), tt in zip(at, t)]
            p = [ee * (1.0 / jnp.sum(ee, axis=0, keepdims=True)) for ee in e]
            o = [dot_tn(pp.astype(BF), vv) for pp, vv in zip(p, v)]
            o = [gather_heads(oo) for oo in o]
            for i, (s, c) in enumerate(at):
                probs[layer, s, c : c + 128] = p[i]
                slope[layer, s, c : c + 128] = (1.0 - t[i] * t[i]) * slope_scale
                att[s, c : c + 128] = o[i]

        x = [xs[2 * layer, b, :] + dot_nn(att[b, :].astype(BF), w_out[layer]) for b in blocks]
        for b, v in zip(blocks, x):
            xs[2 * layer + 1, b, :] = v
        gain = gains[2 * layer + 1 : 2 * layer + 2, :]
        normed = [(v * rms_factor(v) * gain).astype(BF) for v in x]
        up = [dot_nn(v, w_up[layer]) for v in normed]
        for b, v in zip(blocks, up):
            ups[layer, b, :] = v
        hidden = [(u * sigmoid(u)).astype(BF) for u in up]
        x = [v + dot_nn(h, w_down[layer]) for v, h in zip(x, hidden)]

    read = gains[4:5, :] * w_energy[...]
    ones8 = jnp.ones((8, 128), BF)
    readout = []
    dx = []
    for b, v in zip(blocks, x):
        tokens[b, :] = v.astype(BF)
        r = rms_factor(v)
        scaled = v * r
        terms = scaled * read
        part_hi, part_lo = split2(terms[:, 0:128] + terms[:, 128:256])
        readout.append(dot_nt(ones8, part_hi) + dot_nt(ones8, part_lo))
        total = jnp.sum(terms, axis=-1, keepdims=True) * (1.0 / D)
        kw_col = kwb[b, 0:1]
        dx.append((kw_col * r) * (read - scaled * total))
    readout = jnp.concatenate(readout, axis=1)[0:1]
    live = rows[2:3, :]
    reads[...] = readout

    for layer in (1, 0):
        dhid = [dot_nt(v.astype(BF), w_down[layer]) for v in dx]
        dup = []
        for b, dh in zip(blocks, dhid):
            u = ups[layer, b, :]
            sig = sigmoid(u)
            dup.append((dh * (sig * (1.0 + u * (1.0 - sig)))).astype(BF))
        gain = gains[2 * layer + 1 : 2 * layer + 2, :]
        dnorm = [dot_nt(v, w_up[layer]) * gain for v in dup]
        new = []
        for b, v, dn in zip(blocks, dx, dnorm):
            xv = xs[2 * layer + 1, b, :]
            new.append(v + rms_back(xv, rms_factor(xv), dn))
        dx = new
        for b, v in zip(blocks, dx):
            att[b, :] = dot_nt(v.astype(BF), w_out[layer])

        @pl.loop(0, atoms // GROUP)
        def _(step):
            spans = [
                pl.ds(pl.multiple_of(step * (GROUP * NBR) + u * NBR, 8), NBR) for u in range(GROUP)
            ]
            at = [(s, 128 * g) for s in spans for g in range(2)]
            do = [spread(att[s, c : c + 128]) for s, c in at]
            v = [qkv[layer, s, 2 * D + c : 2 * D + c + 128].astype(BF) for s, c in at]
            p = [probs[layer, s, c : c + 128] for s, c in at]
            dp = [dot_nt(vv, dd) for vv, dd in zip(v, do)]
            dv = [dot_nn(pp.astype(BF), dd) for pp, dd in zip(p, do)]
            q = [spread(qkv[layer, s, c : c + 128]) for s, c in at]
            k = [qkv[layer, s, D + c : D + c + 128].astype(BF) for s, c in at]
            dl = [pp * (dd - jnp.sum(pp * dd, axis=0, keepdims=True)) for pp, dd in zip(p, dp)]
            ds = [(dd * slope[layer, s, c : c + 128]).astype(BF) for (s, c), dd in zip(at, dl)]
            dk = [dot_nn(dd, qq) for dd, qq in zip(ds, q)]
            dq = [gather_heads(dot_tn(dd, kk)) for dd, kk in zip(ds, k)]
            old = [acc[s, :] for s in spans] if layer == 0 else None
            for i, (s, c) in enumerate(at):
                dqkv[s, c : c + 128] = dq[i]
                dqkv[s, D + c : D + c + 128] = dk[i]
                dqkv[s, 2 * D + c : 2 * D + c + 128] = dv[i]
            for u, s in enumerate(spans):
                total = dl[2 * u] + dl[2 * u + 1]
                acc[s, :] = total if layer == 1 else old[u] + total

        gain = gains[2 * layer : 2 * layer + 1, :]
        dnorm = [dot_nt(dqkv[b, :].astype(BF), w_qkv[layer]) * gain for b in blocks]
        new = []
        for b, v, dn in zip(blocks, dx, dnorm):
            xv = xs[2 * layer, b, :]
            new.append(v + rms_back(xv, rms_factor(xv), dn))
        dx = new

    w = wfeat[...]
    whi = w.astype(BF)
    wlo = (w - whi.astype(F32)).astype(BF)
    back = []
    acc_row = []
    for b, v in zip(blocks, dx):
        hi, lo = split2(v)
        back.append(dot_nt(whi, hi) + dot_nt(whi, lo) + dot_nt(wlo, hi))
        part_hi, part_lo = split2(acc[b, :])
        acc_row.append(dot_nt(ones8, part_hi) + dot_nt(ones8, part_lo))
    back = jnp.concatenate(back, axis=1)
    acc_row = jnp.concatenate(acc_row, axis=1)[0:1]
    dist = rows[0:1, :]
    cut = rows[1:2, :]
    f = feat[...]
    dcut = jnp.sum(f * back, axis=0, keepdims=True) + live * (readout + acc_row / cut)
    centres = 0.5 + 4.0 * iota((NB, 1), 0).astype(F32) / (NB - 1)
    dradial = back[0:NB] * f[0:NB] * (dist - centres)
    ddist = dcut * rows[4:5, :] - (2.0 * (NB / 8.0) ** 2) * cut * jnp.sum(
        dradial, axis=0, keepdims=True
    )
    g = cut * back[NB:NFEAT] + f[NB:NFEAT] * (ddist / dist)
    grad[...] = g
    ghi = g.astype(BF).astype(F32)
    both = jnp.concatenate([ghi, g - ghi], axis=0).astype(BF)
    out = dot_nt(both, pick[...])
    out = out[0:8] + out[8:16]
    low[...] = out[:, 0:SIDE]
    mid[...] = out[:, SIDE : 2 * SIDE]
    high[...] = out[:, 2 * SIDE : 3 * SIDE]


def local_force_kernel(grad, slot, rows, reads, out, energy):
    parts = rows[3:4, :] * reads[...]
    hi = parts.astype(BF).astype(F32)
    wide = jnp.broadcast_to(hi, (8, EDGE_DEV))
    rest = jnp.broadcast_to(parts - hi, (8, EDGE_DEV))
    summed = dot_nn(jnp.concatenate([wide, rest], axis=0).astype(BF), atom_rows(ATOMS_DEV))
    energy[...] = summed[0:1] + summed[8:9]
    g = grad[...]
    ghi = g.astype(BF).astype(F32)
    both = jnp.concatenate([ghi, g - ghi], axis=0).astype(BF)
    local = one_hot_lanes(as_column(slot[...].reshape(1, EDGE_DEV).astype(F32)), EDGE_DEV)
    partner = dot_nt(both, local)
    diff = (g - partner[0:8] - partner[8:16]) * rows[2:3, :]
    hi = diff.astype(BF).astype(F32)
    both = jnp.concatenate([hi, diff - hi], axis=0).astype(BF)
    summed = dot_nn(both, atom_rows(ATOMS_DEV))
    out[...] = summed[0:8] + summed[8:16]


def force_kernel(partial, mt, r, m, l, forces):
    pieces = []
    for part in (r, m, l):
        for a in range(3):
            for b in range(3):
                pieces.append(part[b, a])
    table = jnp.concatenate(pieces, axis=1)
    hi = table.astype(BF).astype(F32)
    both = jnp.concatenate([hi, table - hi], axis=0).astype(BF)
    far = dot_nt(both, mt[...].astype(BF))
    forces[...] = (partial[...] - far[0:8] - far[8:16])[0:3]


def vmem_call(kernel, outs, *args, scratch=(), limit=12 * 2**20):
    spec = pl.BlockSpec(memory_space=VMEM)
    return pl.pallas_call(
        kernel,
        out_shape=outs,
        in_specs=[spec] * len(args),
        out_specs=jax.tree.map(lambda _: spec, outs),
        scratch_shapes=list(scratch),
        compiler_params=pltpu.CompilerParams(vmem_limit_bytes=limit),
    )(*args)


def shape(dims, dtype=F32):
    return jax.ShapeDtypeStruct(dims, dtype)


def messages(atom_state, w_neigh, prev_tokens, send):
    side = shape((SIDE, D), BF)
    return vmem_call(
        message_kernel,
        [shape((EDGE_DEV, D), BF), side, side, side, shape((3 * SIDE, 8))],
        atom_state,
        w_neigh,
        prev_tokens,
        send,
        scratch=[VMEM((3 * SIDE, 8), F32)],
    )


def geometry(disp, mask, slot, species, message, table, w_vec, w_rbf):
    return vmem_call(
        geometry_kernel,
        [
            shape((EDGE_DEV, D)),
            shape((EDGE_DEV, 128)),
            shape((NFEAT, EDGE_DEV)),
            shape((8, EDGE_DEV)),
            shape((NFEAT, D)),
        ],
        disp,
        mask,
        slot,
        species,
        message,
        table,
        w_vec,
        w_rbf,
    )


def lookups(slot, mask, where):
    outs = [shape((EDGE_DEV, 3 * SIDE), BF), shape((3 * SIDE, EDGE_DEV), BF), shape((ATOMS_DEV, 3 * SIDE))]
    return vmem_call(lookup_kernel, outs, slot, mask, where)


def layers(base, arr, far, kwb, feat, rows, wfeat, gains, w_qkv, w_out, w_up, w_down, w_energy, pick):
    side = shape((8, SIDE))
    n = EDGE_DEV
    return vmem_call(
        layer_kernel,
        [shape((n, D), BF), shape((1, n)), shape((8, n)), side, side, side],
        base,
        *arr,
        far,
        kwb,
        feat,
        rows,
        wfeat,
        gains,
        w_qkv,
        w_out,
        w_up,
        w_down,
        w_energy,
        pick,
        limit=LIMIT,
        scratch=[
            VMEM((4, n, D), F32),
            VMEM((2, n, 3 * D), F32),
            VMEM((2, n, FF), F32),
            VMEM((2, n, D), F32),
            VMEM((2, n, D), F32),
            VMEM((n, D), F32),
            VMEM((n, 3 * D), F32),
            VMEM((n, 128), F32),
        ],
    )


def exchange(low, high, axis):
    count = lax.axis_size(axis)
    outer = [(i, (i + 1 if i % 2 else i - 1) % count) for i in range(count)]
    inner = [(i, i + 1 if i % 2 == 0 else i - 1) for i in range(count)]
    return lax.ppermute(low, axis, outer), lax.ppermute(high, axis, inner)


def on_device(
    displacement,
    neighbour_mask,
    reverse_slot,
    send_edges,
    species,
    prev_tokens,
    atom_state,
    species_table,
    w_neigh,
    w_vec,
    w_rbf,
    gains,
    w_qkv,
    w_out,
    w_up,
    w_down,
    w_energy,
):
    message, low, mid, high, where = messages(atom_state, w_neigh, prev_tokens, send_edges)
    low, high = exchange(low, high, "gx")
    cells = [v.reshape(3, 3, SLOTS, D) for v in (low, mid, high)]
    low, mid, high = (jnp.stack([v[i] for v in cells]) for i in range(3))
    low, high, where = lax.optimization_barrier((low, high, where))
    low, high = exchange(low, high, "gy")
    far, pick, mt = lookups(reverse_slot, neighbour_mask, where)
    cells = (low, mid, high)
    low, mid, high = (jnp.stack([v[:, i] for v in cells], axis=1) for i in range(3))
    low, high, late = lax.optimization_barrier((low, high, displacement))
    low, high = exchange(low, high, "gz")
    base, kwb, feat, rows, wfeat = geometry(
        late, neighbour_mask, reverse_slot, species, message, species_table, w_vec, w_rbf
    )
    arr = [v.reshape(SIDE, D) for v in (low, mid, high)]
    tokens, reads, grad, low, mid, high = layers(
        base,
        arr,
        far,
        kwb,
        feat,
        rows,
        wfeat,
        gains,
        w_qkv,
        w_out,
        w_up,
        w_down,
        w_energy.reshape(1, D),
        pick,
    )
    low, high = exchange(low, high, "gx")
    cells = jnp.stack([low, mid, high])
    cut = 3 * SLOTS
    low, mid, high = (cells[:, :, i * cut : (i + 1) * cut] for i in range(3))
    low, high = exchange(low, high, "gy")
    cells = jnp.stack([low, mid, high])
    cut = SLOTS
    low, mid, high = (cells[..., i * cut : (i + 1) * cut] for i in range(3))
    low, high, late = lax.optimization_barrier((low, high, grad))
    low, high = exchange(low, high, "gz")
    partial, energy = vmem_call(
        local_force_kernel,
        [shape((8, ATOMS_DEV)), shape((1, ATOMS_DEV))],
        late,
        reverse_slot,
        rows,
        reads,
    )
    forces = vmem_call(force_kernel, shape((3, ATOMS_DEV)), partial, mt, low, mid, high)
    return (tokens, energy.reshape(ATOMS_DEV), forces)


def solution(mesh):
    return jax.shard_map(
        on_device,
        mesh=mesh,
        in_specs=(
            P(None, ("gx", "gy", "gz")),
            P(("gx", "gy", "gz")),
            P(("gx", "gy", "gz")),
            P(("gx", "gy", "gz")),
            P(("gx", "gy", "gz")),
            P(("gx", "gy", "gz"), None),
            P(("gx", "gy", "gz"), None),
            P(),
            P(),
            P(),
            P(),
            P(),
            P(),
            P(),
            P(),
            P(),
            P(),
        ),
        out_specs=(P(("gx", "gy", "gz"), None), P(("gx", "gy", "gz")), P(None, ("gx", "gy", "gz"))),
        check_vma=False,
    )
```

```python
import math

import jax
import jax.numpy as jnp
from jax import lax
from jax.experimental import pallas as pl
from jax.experimental.pallas import tpu as pltpu
from jax.sharding import PartitionSpec as P

HEADS = 8
NBR = 24
ATOMS_DEV = 32
EDGE_DEV = 768
D = 256
FF = 512
NB = 64
NSPEC = 85
SLOTS = 16
SIDE = 9 * SLOTS
NFEAT = 72
score_cap = 8.0
cutoff_radius = 5.0
norm_eps = 1e-06
AXES = ("gx", "gy", "gz")

BF = jnp.bfloat16
F32 = jnp.float32
VMEM = pltpu.VMEM


def dot_nn(a, b):
    return lax.dot_general(a, b, (((1,), (0,)), ((), ())), preferred_element_type=F32)


def dot_nt(a, b):
    return lax.dot_general(a, b, (((1,), (1,)), ((), ())), preferred_element_type=F32)


def dot_tn(a, b):
    return lax.dot_general(a, b, (((0,), (0,)), ((), ())), preferred_element_type=F32)


def iota(shape, axis):
    return lax.broadcasted_iota(jnp.int32, shape, axis)


def split2(x):
    hi = x.astype(BF)
    lo = (x - hi.astype(F32)).astype(BF)
    return hi, lo


def as_column(row):
    return jnp.broadcast_to(row, (8, row.shape[1])).T[:, 0:1]


def atom_rows(count, dtype=BF):
    edge = iota((count * NBR, count), 0)
    first = iota((count * NBR, count), 1) * NBR
    return jnp.where((edge >= first) & (edge < first + NBR), 1.0, 0.0).astype(dtype)


def one_hot_lanes(column, width):
    lanes = iota((column.shape[0], width), 1).astype(F32)
    return jnp.where(lanes == column, 1.0, 0.0).astype(BF)


def message_kernel(
    state_far,
    w_far,
    prev_far,
    send_far,
    message,
    low,
    mid,
    high,
    where,
    order,
    send,
    state,
    w_neigh,
    prev,
    sems,
):
    moves = [
        pltpu.make_async_copy(src, dst, sems.at[i])
        for i, (src, dst) in enumerate(
            ((send_far, send), (state_far, state), (w_far, w_neigh), (prev_far, prev))
        )
    ]
    for move in moves:
        move.start()
    expand = atom_rows(ATOMS_DEV)
    moves[0].wait()
    count = 26 * SLOTS
    sent = jnp.broadcast_to(send[...].reshape(1, count).astype(F32), (8, count)).T
    flips = [lax.axis_index(axis) & 1 for axis in AXES]
    for bucket in range(27):
        place = 0
        for axis, digit in enumerate((bucket // 9, bucket // 3 % 3, bucket % 3)):
            place = place * 3 + digit + flips[axis] * (2 - 2 * digit)
        rows = pl.ds(pl.multiple_of(place * SLOTS, SLOTS), SLOTS)
        if bucket == 13:
            order[rows, :] = jnp.full((SLOTS, 8), -1.0, F32)
        else:
            start = (bucket - (bucket > 13)) * SLOTS
            order[rows, :] = sent[start : start + SLOTS]
    column = order[...]
    where[...] = column
    pick = one_hot_lanes(column[:, 0:1], EDGE_DEV)
    moves[1].wait()
    moves[2].wait()
    projected = dot_nn(state[...], w_neigh[...])
    hi, lo = split2(projected)
    rest = (projected - hi.astype(F32) - lo.astype(F32)).astype(BF)
    wide = dot_nn(expand, hi) + dot_nn(expand, lo) + dot_nn(expand, rest)
    moves[3].wait()
    out = (prev[...].astype(F32) + wide).astype(BF)
    message[...] = out
    payload = dot_nn(pick, out).astype(BF)
    low[...] = payload[0:SIDE]
    mid[...] = payload[SIDE : 2 * SIDE]
    high[...] = payload[2 * SIDE : 3 * SIDE]


def remote_index(slot):
    far = slot - EDGE_DEV
    bucket = far >> 4
    pair = (bucket * 11) >> 5
    first = (pair * 11) >> 5
    digits = [first, pair - 3 * first, bucket - 3 * pair]
    for i, axis in enumerate(AXES):
        flip = lax.axis_index(axis) & 1
        digits[i] = digits[i] + flip * (2 - 2 * digits[i])
    place = digits[2] * SIDE + (digits[0] * 3 + digits[1]) * SLOTS + (far & 15)
    return jnp.where(far >= 0, place, -1).astype(F32)


def lookup_kernel(slot, mask, where, far, pick, mt):
    slot_row = slot[...].reshape(1, EDGE_DEV)
    live = mask[...].reshape(1, EDGE_DEV).astype(F32)
    hot = one_hot_lanes(as_column(remote_index(slot_row)), 3 * SIDE)
    far[...] = hot
    pick[...] = one_hot_lanes(where[:, 0:1], EDGE_DEV)
    live_rows = atom_rows(ATOMS_DEV, F32) * as_column(live)
    mt[...] = dot_tn(live_rows.astype(BF), hot)


def geometry_kernel(
    disp, mask, slot, species, message, table, w_vec, w_rbf, base, kwb, feat, rows, wfeat
):
    d = disp[...]
    dist = jnp.sqrt(jnp.sum(d * d, axis=0, keepdims=True) + 0.5)
    angle = (math.pi / cutoff_radius) * dist
    cut = 0.5 * (jnp.cos(angle) + 1.0)
    live = mask[...].reshape(1, EDGE_DEV).astype(F32)
    kw = live * cut
    centres = 0.5 + 4.0 * iota((NB, 1), 0).astype(F32) / (NB - 1)
    offset = dist - centres
    radial = jnp.exp(-jnp.square(offset * (NB / 8.0)))
    feat[0:NB, :] = radial
    feat[NB:NFEAT, :] = jnp.zeros((NFEAT - NB, EDGE_DEV), F32)
    feat[NB : NB + 3, :] = d
    wfeat[0:NB, :] = w_rbf[...]
    wfeat[NB:NFEAT, :] = jnp.zeros((NFEAT - NB, D), F32)
    wfeat[NB : NB + 3, :] = w_vec[...]
    rows[0:1, :] = dist
    rows[1:2, :] = cut
    rows[2:3, :] = live
    rows[3:4, :] = kw
    rows[4:5, :] = (-0.5 * math.pi / cutoff_radius) * jnp.sin(angle)
    rows[5:8, :] = jnp.zeros((3, EDGE_DEV), F32)
    scaled = feat[...] * cut
    hi = scaled.astype(BF).astype(F32)
    left = jnp.concatenate([hi, scaled - hi, hi], axis=0).T.astype(BF)
    w = wfeat[...]
    whi = w.astype(BF).astype(F32)
    right = jnp.concatenate([whi, whi, w - whi], axis=0).astype(BF)
    kind = jnp.where(iota((NSPEC, ATOMS_DEV), 0) == species[...].reshape(1, ATOMS_DEV), 1.0, 0.0).astype(BF)
    centre = dot_tn(kind, table[...]).astype(BF)
    expand = atom_rows(ATOMS_DEV)
    slot_row = slot[...].reshape(1, EDGE_DEV)
    local = one_hot_lanes(as_column(slot_row.astype(F32)), EDGE_DEV)
    base[...] = dot_nn(left, right) + dot_nn(expand, centre) + dot_nn(local, message[...])
    kwb[...] = jnp.broadcast_to(as_column(kw), (EDGE_DEV, 128))


def sigmoid(u):
    return 0.5 * jnp.tanh(0.5 * u) + 0.5


def rms_factor(x):
    return lax.rsqrt(jnp.mean(x * x, axis=-1, keepdims=True) + norm_eps)


def rms_back(x, r, z):
    inner = jnp.mean(x * z, axis=-1, keepdims=True)
    return r * z - x * (r * r * r * inner)


LIMIT = 36 * 2**20
INNER = 4 * NBR
OUTER = EDGE_DEV - INNER


def block_list(edges, parts):
    step = edges // parts
    return [slice(i, i + step) for i in range(0, edges, step)]


def shifted(block, offset):
    return slice(block.start + offset, block.stop + offset)


def atom_spans(edges, offset=0):
    return [slice(i + offset, i + offset + NBR) for i in range(0, edges, NBR)]


def spread(x):
    tall = jnp.concatenate([x, jnp.zeros((32 - NBR, 128), F32)], axis=0).astype(BF)
    head = iota((32, 128), 1) >> 5
    return jnp.concatenate(
        [tall * jnp.where(head == h, 1.0, 0.0).astype(BF) for h in range(4)], axis=0
    )


def gather_heads(wide):
    head = iota((1, 128), 1) >> 5
    out = jnp.where(head == 0, wide[0:NBR], 0.0)
    for h in range(1, 4):
        out = jnp.where(head == h, wide[32 * h : 32 * h + NBR], out)
    return out


def forward(x, blocks, offset, kwb, gains, w_qkv, w_out, w_up, w_down, xs, qkv, ups, probs, slope, att):
    edges = blocks[-1].stop
    score_scale = 1.0 / (math.sqrt(D // HEADS) * score_cap)
    slope_scale = 1.0 / math.sqrt(D // HEADS)
    at = [(s, 128 * g) for s in atom_spans(edges) for g in range(2)]
    for layer in range(2):
        for b, v in zip(blocks, x):
            xs[2 * layer, b, :] = v
        gain = gains[2 * layer : 2 * layer + 1, :]
        normed = [(v * rms_factor(v) * gain).astype(BF) for v in x]
        for b, v in zip(blocks, normed):
            qkv[layer, b, :] = dot_nn(v, w_qkv[layer])
        q = [spread(qkv[layer, s, c : c + 128]) for s, c in at]
        k = [qkv[layer, s, D + c : D + c + 128].astype(BF) for s, c in at]
        v = [qkv[layer, s, 2 * D + c : 2 * D + c + 128].astype(BF) for s, c in at]
        t = [dot_nt(kk, qq) for kk, qq in zip(k, q)]
        t = [jnp.tanh(tt * score_scale) for tt in t]
        e = [kwb[shifted(s, offset), :] * jnp.exp(score_cap * tt) for (s, c), tt in zip(at, t)]
        p = [ee * (1.0 / jnp.sum(ee, axis=0, keepdims=True)) for ee in e]
        o = [dot_tn(pp.astype(BF), vv) for pp, vv in zip(p, v)]
        o = [gather_heads(oo) for oo in o]
        for i, (s, c) in enumerate(at):
            probs[layer, s, c : c + 128] = p[i]
            slope[layer, s, c : c + 128] = (1.0 - t[i] * t[i]) * slope_scale
            att[s, c : c + 128] = o[i]
        x = [xs[2 * layer, b, :] + dot_nn(att[b, :].astype(BF), w_out[layer]) for b in blocks]
        for b, v in zip(blocks, x):
            xs[2 * layer + 1, b, :] = v
        gain = gains[2 * layer + 1 : 2 * layer + 2, :]
        normed = [(v * rms_factor(v) * gain).astype(BF) for v in x]
        up = [dot_nn(v, w_up[layer]) for v in normed]
        for b, v in zip(blocks, up):
            ups[layer, b, :] = v
        hidden = [(u * sigmoid(u)).astype(BF) for u in up]
        x = [v + dot_nn(h, w_down[layer]) for v, h in zip(x, hidden)]
    return x


def backward(
    x, blocks, offset, kwb, gains, w_energy, w_qkv, w_out, w_up, w_down, xs, qkv, ups, probs, slope, att, dqkv, acc
):
    edges = blocks[-1].stop
    spans = atom_spans(edges)
    at = [(s, 128 * g) for s in spans for g in range(2)]
    read = gains[4:5, :] * w_energy[...]
    readout = []
    dx = []
    for b, v in zip(blocks, x):
        r = rms_factor(v)
        scaled = v * r
        terms = scaled * read
        readout.append(terms[:, 0:128] + terms[:, 128:256])
        total = jnp.sum(terms, axis=-1, keepdims=True) * (1.0 / D)
        dx.append((kwb[shifted(b, offset), 0:1] * r) * (read - scaled * total))
    for layer in (1, 0):
        dhid = [dot_nt(v.astype(BF), w_down[layer]) for v in dx]
        dup = []
        for b, dh in zip(blocks, dhid):
            u = ups[layer, b, :]
            sig = sigmoid(u)
            dup.append((dh * (sig * (1.0 + u * (1.0 - sig)))).astype(BF))
        gain = gains[2 * layer + 1 : 2 * layer + 2, :]
        dnorm = [dot_nt(v, w_up[layer]) * gain for v in dup]
        new = []
        for b, v, dn in zip(blocks, dx, dnorm):
            xv = xs[2 * layer + 1, b, :]
            new.append(v + rms_back(xv, rms_factor(xv), dn))
        dx = new
        for b, v in zip(blocks, dx):
            att[b, :] = dot_nt(v.astype(BF), w_out[layer])
        do = [spread(att[s, c : c + 128]) for s, c in at]
        v = [qkv[layer, s, 2 * D + c : 2 * D + c + 128].astype(BF) for s, c in at]
        p = [probs[layer, s, c : c + 128] for s, c in at]
        dp = [dot_nt(vv, dd) for vv, dd in zip(v, do)]
        dv = [dot_nn(pp.astype(BF), dd) for pp, dd in zip(p, do)]
        q = [spread(qkv[layer, s, c : c + 128]) for s, c in at]
        k = [qkv[layer, s, D + c : D + c + 128].astype(BF) for s, c in at]
        dl = [pp * (dd - jnp.sum(pp * dd, axis=0, keepdims=True)) for pp, dd in zip(p, dp)]
        ds = [(dd * slope[layer, s, c : c + 128]).astype(BF) for (s, c), dd in zip(at, dl)]
        dk = [dot_nn(dd, qq) for dd, qq in zip(ds, q)]
        dq = [gather_heads(dot_tn(dd, kk)) for dd, kk in zip(ds, k)]
        for i, (s, c) in enumerate(at):
            dqkv[s, c : c + 128] = dq[i]
            dqkv[s, D + c : D + c + 128] = dk[i]
            dqkv[s, 2 * D + c : 2 * D + c + 128] = dv[i]
        for u, s in enumerate(spans):
            total = dl[2 * u] + dl[2 * u + 1]
            acc[s, :] = total if layer == 1 else acc[s, :] + total
        gain = gains[2 * layer : 2 * layer + 1, :]
        dnorm = [dot_nt(dqkv[b, :].astype(BF), w_qkv[layer]) * gain for b in blocks]
        new = []
        for b, v, dn in zip(blocks, dx, dnorm):
            xv = xs[2 * layer, b, :]
            new.append(v + rms_back(xv, rms_factor(xv), dn))
        dx = new
    return readout, dx


def inner_forward_kernel(
    base, kwb, gains, w_qkv, w_out, w_up, w_down, last, xs, qkv, ups, probs, slope, att
):
    blocks = block_list(INNER, 1)
    x = forward(
        [base[0:INNER, :]], blocks, 0, kwb, gains, w_qkv, w_out, w_up, w_down, xs, qkv, ups, probs, slope, att
    )
    last[...] = x[0]


def inner_backward_kernel(
    last, xs, qkv, ups, probs, slope, kwb, gains, w_energy, w_qkv, w_out, w_up, w_down, terms, dx, acc, att, dqkv
):
    blocks = block_list(INNER, 1)
    readout, out = backward(
        [last[...]],
        blocks,
        0,
        kwb,
        gains,
        w_energy,
        w_qkv,
        w_out,
        w_up,
        w_down,
        xs,
        qkv,
        ups,
        probs,
        slope,
        att,
        dqkv,
        acc,
    )
    terms[...] = readout[0]
    dx[...] = out[0]


def layer_kernel(
    base,
    arr_r,
    arr_m,
    arr_l,
    far,
    kwb,
    feat,
    rows,
    wfeat,
    gains,
    w_qkv,
    w_out,
    w_up,
    w_down,
    w_energy,
    pick,
    inner_last,
    inner_terms,
    inner_dx,
    inner_acc,
    tokens,
    reads,
    grad,
    low,
    mid,
    high,
    xs,
    qkv,
    ups,
    probs,
    slope,
    att,
    dqkv,
    acc,
):
    blocks = block_list(OUTER, 2)
    arrived = jnp.concatenate([arr_r[...], arr_m[...], arr_l[...]], axis=0)
    x = []
    for b in blocks:
        here = shifted(b, INNER)
        x.append(base[here, :] + dot_nn(far[here, :], arrived))
    stores = (xs, qkv, ups, probs, slope, att)
    weights = (w_qkv, w_out, w_up, w_down)
    x = forward(x, blocks, INNER, kwb, gains, *weights, *stores)
    tokens[0:INNER, :] = inner_last[...].astype(BF)
    for b, v in zip(blocks, x):
        tokens[shifted(b, INNER), :] = v.astype(BF)
    terms, dx = backward(x, blocks, INNER, kwb, gains, w_energy, *weights, *stores, dqkv, acc)

    w = wfeat[...]
    whi = w.astype(BF)
    wlo = (w - whi.astype(F32)).astype(BF)
    ones8 = jnp.ones((8, 128), BF)

    def to_row(parts):
        hi, lo = split2(jnp.concatenate(parts, axis=0))
        return (dot_nt(ones8, hi) + dot_nt(ones8, lo))[0:1]

    hi, lo = split2(jnp.concatenate([inner_dx[...]] + dx, axis=0))
    back = dot_nt(whi, hi) + dot_nt(whi, lo) + dot_nt(wlo, hi)
    readout = to_row([inner_terms[...]] + terms)
    reads[...] = readout
    acc_row = to_row([inner_acc[...], acc[...]])
    live = rows[2:3, :]
    dist = rows[0:1, :]
    cut = rows[1:2, :]
    f = feat[...]
    dcut = jnp.sum(f * back, axis=0, keepdims=True) + live * (readout + acc_row / cut)
    centres = 0.5 + 4.0 * iota((NB, 1), 0).astype(F32) / (NB - 1)
    dradial = back[0:NB] * f[0:NB] * (dist - centres)
    ddist = dcut * rows[4:5, :] - (2.0 * (NB / 8.0) ** 2) * cut * jnp.sum(
        dradial, axis=0, keepdims=True
    )
    g = cut * back[NB:NFEAT] + f[NB:NFEAT] * (ddist / dist)
    grad[...] = g
    ghi = g.astype(BF).astype(F32)
    both = jnp.concatenate([ghi, g - ghi], axis=0).astype(BF)
    out = dot_nt(both, pick[...])
    out = out[0:8] + out[8:16]
    low[...] = out[:, 0:SIDE]
    mid[...] = out[:, SIDE : 2 * SIDE]
    high[...] = out[:, 2 * SIDE : 3 * SIDE]


def local_force_kernel(grad, slot, rows, reads, out, energy):
    parts = rows[3:4, :] * reads[...]
    hi = parts.astype(BF).astype(F32)
    wide = jnp.broadcast_to(hi, (8, EDGE_DEV))
    rest = jnp.broadcast_to(parts - hi, (8, EDGE_DEV))
    summed = dot_nn(jnp.concatenate([wide, rest], axis=0).astype(BF), atom_rows(ATOMS_DEV))
    energy[...] = summed[0:1] + summed[8:9]
    g = grad[...]
    ghi = g.astype(BF).astype(F32)
    both = jnp.concatenate([ghi, g - ghi], axis=0).astype(BF)
    local = one_hot_lanes(as_column(slot[...].reshape(1, EDGE_DEV).astype(F32)), EDGE_DEV)
    partner = dot_nt(both, local)
    diff = (g - partner[0:8] - partner[8:16]) * rows[2:3, :]
    hi = diff.astype(BF).astype(F32)
    both = jnp.concatenate([hi, diff - hi], axis=0).astype(BF)
    summed = dot_nn(both, atom_rows(ATOMS_DEV))
    out[...] = summed[0:8] + summed[8:16]


def force_kernel(partial, mt, r, m, l, forces):
    pieces = []
    for part in (r, m, l):
        for a in range(3):
            for b in range(3):
                pieces.append(part[b, a])
    table = jnp.concatenate(pieces, axis=1)
    hi = table.astype(BF).astype(F32)
    both = jnp.concatenate([hi, table - hi], axis=0).astype(BF)
    far = dot_nt(both, mt[...].astype(BF))
    forces[...] = (partial[...] - far[0:8] - far[8:16])[0:3]


def vmem_call(kernel, outs, *args, scratch=(), limit=12 * 2**20, place=VMEM):
    spec = pl.BlockSpec(memory_space=VMEM)
    return pl.pallas_call(
        kernel,
        out_shape=outs,
        in_specs=[pl.BlockSpec(memory_space=place)] * len(args),
        out_specs=jax.tree.map(lambda _: spec, outs),
        scratch_shapes=list(scratch),
        compiler_params=pltpu.CompilerParams(vmem_limit_bytes=limit),
    )(*args)


def shape(dims, dtype=F32):
    return jax.ShapeDtypeStruct(dims, dtype)


def messages(atom_state, w_neigh, prev_tokens, send):
    side = shape((SIDE, D), BF)
    return vmem_call(
        message_kernel,
        [shape((EDGE_DEV, D), BF), side, side, side, shape((3 * SIDE, 8))],
        atom_state,
        w_neigh,
        prev_tokens,
        send,
        scratch=[
            VMEM((3 * SIDE, 8), F32),
            VMEM((26 * SLOTS,), jnp.int32),
            VMEM((ATOMS_DEV, D), BF),
            VMEM((D, D), BF),
            VMEM((EDGE_DEV, D), BF),
            pltpu.SemaphoreType.DMA((4,)),
        ],
        place=pltpu.HBM,
        limit=62 * 2**20,
    )


def geometry(disp, mask, slot, species, message, table, w_vec, w_rbf):
    return vmem_call(
        geometry_kernel,
        [
            shape((EDGE_DEV, D)),
            shape((EDGE_DEV, 128)),
            shape((NFEAT, EDGE_DEV)),
            shape((8, EDGE_DEV)),
            shape((NFEAT, D)),
        ],
        disp,
        mask,
        slot,
        species,
        message,
        table,
        w_vec,
        w_rbf,
    )


def lookups(slot, mask, where):
    outs = [shape((EDGE_DEV, 3 * SIDE), BF), shape((3 * SIDE, EDGE_DEV), BF), shape((ATOMS_DEV, 3 * SIDE))]
    return vmem_call(lookup_kernel, outs, slot, mask, where)


def inner_stores(n):
    return [
        shape((4, n, D)),
        shape((2, n, 3 * D)),
        shape((2, n, FF)),
        shape((2, n, D)),
        shape((2, n, D)),
    ]


def inner_forward(base, kwb, gains, weights):
    n = INNER
    outs = [shape((n, D))] + inner_stores(n)
    return vmem_call(
        inner_forward_kernel, outs, base, kwb, gains, *weights, scratch=[VMEM((n, D), F32)]
    )


def inner_backward(saved, kwb, gains, w_energy, weights):
    n = INNER
    return vmem_call(
        inner_backward_kernel,
        [shape((n, 128)), shape((n, D)), shape((n, 128))],
        *saved,
        kwb,
        gains,
        w_energy,
        *weights,
        scratch=[VMEM((n, D), F32), VMEM((n, 3 * D), F32)],
    )


def layers(base, arr, far, kwb, feat, rows, wfeat, gains, weights, w_energy, pick, inner):
    side = shape((8, SIDE))
    n = EDGE_DEV
    return vmem_call(
        layer_kernel,
        [shape((n, D), BF), shape((1, n)), shape((8, n)), side, side, side],
        base,
        *arr,
        far,
        kwb,
        feat,
        rows,
        wfeat,
        gains,
        *weights,
        w_energy,
        pick,
        *inner,
        limit=LIMIT,
        scratch=[VMEM(v.shape, F32) for v in inner_stores(OUTER)]
        + [VMEM((OUTER, D), F32), VMEM((OUTER, 3 * D), F32), VMEM((OUTER, 128), F32)],
    )


def exchange(low, high, axis):
    count = lax.axis_size(axis)
    outer = [(i, (i + 1 if i % 2 else i - 1) % count) for i in range(count)]
    inner = [(i, i + 1 if i % 2 == 0 else i - 1) for i in range(count)]
    return lax.ppermute(low, axis, outer), lax.ppermute(high, axis, inner)


def on_device(
    displacement,
    neighbour_mask,
    reverse_slot,
    send_edges,
    species,
    prev_tokens,
    atom_state,
    species_table,
    w_neigh,
    w_vec,
    w_rbf,
    gains,
    w_qkv,
    w_out,
    w_up,
    w_down,
    w_energy,
):
    message, low, mid, high, where = messages(atom_state, w_neigh, prev_tokens, send_edges)
    low, high = exchange(low, high, "gx")
    far, pick, mt = lookups(reverse_slot, neighbour_mask, where)
    cells = [v.reshape(3, 3, SLOTS, D) for v in (low, mid, high)]
    low, mid, high = (jnp.stack([v[i] for v in cells]) for i in range(3))
    low, high, late = lax.optimization_barrier((low, high, displacement))
    low, high = exchange(low, high, "gy")
    base, kwb, feat, rows, wfeat = geometry(
        late, neighbour_mask, reverse_slot, species, message, species_table, w_vec, w_rbf
    )
    weights = (w_qkv, w_out, w_up, w_down)
    w_energy = w_energy.reshape(1, D)
    saved = inner_forward(base, kwb, gains, weights)
    cells = (low, mid, high)
    low, mid, high = (jnp.stack([v[:, i] for v in cells], axis=1) for i in range(3))
    low, high, *saved = lax.optimization_barrier((low, high, *saved))
    low, high = exchange(low, high, "gz")
    terms, dx, acc = inner_backward(saved, kwb, gains, w_energy, weights)
    arr = [v.reshape(SIDE, D) for v in (low, mid, high)]
    tokens, reads, grad, low, mid, high = layers(
        base,
        arr,
        far,
        kwb,
        feat,
        rows,
        wfeat,
        gains,
        weights,
        w_energy,
        pick,
        (saved[0], terms, dx, acc),
    )
    low, high = exchange(low, high, "gx")
    cells = jnp.stack([low, mid, high])
    cut = 3 * SLOTS
    low, mid, high = (cells[:, :, i * cut : (i + 1) * cut] for i in range(3))
    low, high = exchange(low, high, "gy")
    cells = jnp.stack([low, mid, high])
    cut = SLOTS
    low, mid, high = (cells[..., i * cut : (i + 1) * cut] for i in range(3))
    low, high, late = lax.optimization_barrier((low, high, grad))
    low, high = exchange(low, high, "gz")
    partial, energy = vmem_call(
        local_force_kernel,
        [shape((8, ATOMS_DEV)), shape((1, ATOMS_DEV))],
        late,
        reverse_slot,
        rows,
        reads,
    )
    forces = vmem_call(force_kernel, shape((3, ATOMS_DEV)), partial, mt, low, mid, high)
    return (tokens, energy.reshape(ATOMS_DEV), forces)


def solution(mesh):
    return jax.shard_map(
        on_device,
        mesh=mesh,
        in_specs=(
            P(None, ("gx", "gy", "gz")),
            P(("gx", "gy", "gz")),
            P(("gx", "gy", "gz")),
            P(("gx", "gy", "gz")),
            P(("gx", "gy", "gz")),
            P(("gx", "gy", "gz"), None),
            P(("gx", "gy", "gz"), None),
            P(),
            P(),
            P(),
            P(),
            P(),
            P(),
            P(),
            P(),
            P(),
            P(),
        ),
        out_specs=(P(("gx", "gy", "gz"), None), P(("gx", "gy", "gz")), P(None, ("gx", "gy", "gz"))),
        check_vma=False,
    )
```

```python
import math

import jax
import jax.numpy as jnp
from jax import lax
from jax.experimental import pallas as pl
from jax.experimental.pallas import tpu as pltpu
from jax.sharding import PartitionSpec as P

HEADS = 8
NBR = 24
ATOMS_DEV = 32
EDGE_DEV = 768
D = 256
FF = 512
NB = 64
NSPEC = 85
SLOTS = 16
SIDE = 9 * SLOTS
NFEAT = 72
score_cap = 8.0
cutoff_radius = 5.0
norm_eps = 1e-06
AXES = ("gx", "gy", "gz")

BF = jnp.bfloat16
F32 = jnp.float32
VMEM = pltpu.VMEM


def dot_nn(a, b):
    return lax.dot_general(a, b, (((1,), (0,)), ((), ())), preferred_element_type=F32)


def dot_nt(a, b):
    return lax.dot_general(a, b, (((1,), (1,)), ((), ())), preferred_element_type=F32)


def dot_tn(a, b):
    return lax.dot_general(a, b, (((0,), (0,)), ((), ())), preferred_element_type=F32)


def iota(shape, axis):
    return lax.broadcasted_iota(jnp.int32, shape, axis)


def split2(x):
    hi = x.astype(BF)
    lo = (x - hi.astype(F32)).astype(BF)
    return hi, lo


def as_column(row):
    return jnp.broadcast_to(row, (8, row.shape[1])).T[:, 0:1]


def atom_rows(count, dtype=BF):
    edge = iota((count * NBR, count), 0)
    first = iota((count * NBR, count), 1) * NBR
    return jnp.where((edge >= first) & (edge < first + NBR), 1.0, 0.0).astype(dtype)


def one_hot_lanes(column, width):
    lanes = iota((column.shape[0], width), 1).astype(F32)
    return jnp.where(lanes == column, 1.0, 0.0).astype(BF)


def message_kernel(
    state_far,
    w_far,
    prev_far,
    send_far,
    message,
    low,
    mid,
    high,
    where,
    order,
    send,
    state,
    w_neigh,
    prev,
    sems,
):
    moves = [
        pltpu.make_async_copy(src, dst, sems.at[i])
        for i, (src, dst) in enumerate(
            ((send_far, send), (state_far, state), (w_far, w_neigh), (prev_far, prev))
        )
    ]
    for move in moves:
        move.start()
    expand = atom_rows(ATOMS_DEV)
    moves[0].wait()
    count = 26 * SLOTS
    sent = jnp.broadcast_to(send[...].reshape(1, count).astype(F32), (8, count)).T
    flips = [lax.axis_index(axis) & 1 for axis in AXES]
    for bucket in range(27):
        place = 0
        for axis, digit in enumerate((bucket // 9, bucket // 3 % 3, bucket % 3)):
            place = place * 3 + digit + flips[axis] * (2 - 2 * digit)
        rows = pl.ds(pl.multiple_of(place * SLOTS, SLOTS), SLOTS)
        if bucket == 13:
            order[rows, :] = jnp.full((SLOTS, 8), -1.0, F32)
        else:
            start = (bucket - (bucket > 13)) * SLOTS
            order[rows, :] = sent[start : start + SLOTS]
    column = order[...]
    where[...] = column
    pick = one_hot_lanes(column[:, 0:1], EDGE_DEV)
    moves[1].wait()
    moves[2].wait()
    projected = dot_nn(state[...], w_neigh[...])
    hi, lo = split2(projected)
    rest = (projected - hi.astype(F32) - lo.astype(F32)).astype(BF)
    wide = dot_nn(expand, hi) + dot_nn(expand, lo) + dot_nn(expand, rest)
    moves[3].wait()
    out = (prev[...].astype(F32) + wide).astype(BF)
    message[...] = out
    payload = dot_nn(pick, out).astype(BF)
    low[...] = payload[0:SIDE]
    mid[...] = payload[SIDE : 2 * SIDE]
    high[...] = payload[2 * SIDE : 3 * SIDE]


def remote_index(slot):
    far = slot - EDGE_DEV
    bucket = far >> 4
    pair = (bucket * 11) >> 5
    first = (pair * 11) >> 5
    digits = [first, pair - 3 * first, bucket - 3 * pair]
    for i, axis in enumerate(AXES):
        flip = lax.axis_index(axis) & 1
        digits[i] = digits[i] + flip * (2 - 2 * digits[i])
    place = digits[2] * SIDE + (digits[0] * 3 + digits[1]) * SLOTS + (far & 15)
    return jnp.where(far >= 0, place, -1).astype(F32)


def lookup_kernel(slot, mask, where, far, pick, mt):
    slot_row = slot[...].reshape(1, EDGE_DEV)
    live = mask[...].reshape(1, EDGE_DEV).astype(F32)
    hot = one_hot_lanes(as_column(remote_index(slot_row)), 3 * SIDE)
    far[...] = hot
    pick[...] = one_hot_lanes(where[:, 0:1], EDGE_DEV)
    live_rows = atom_rows(ATOMS_DEV, F32) * as_column(live)
    mt[...] = dot_tn(live_rows.astype(BF), hot)


def geometry_kernel(
    disp, mask, slot, species, message, table, w_vec, w_rbf, base, kwb, feat, rows, wfeat
):
    d = disp[...]
    dist = jnp.sqrt(jnp.sum(d * d, axis=0, keepdims=True) + 0.5)
    angle = (math.pi / cutoff_radius) * dist
    cut = 0.5 * (jnp.cos(angle) + 1.0)
    live = mask[...].reshape(1, EDGE_DEV).astype(F32)
    kw = live * cut
    centres = 0.5 + 4.0 * iota((NB, 1), 0).astype(F32) / (NB - 1)
    offset = dist - centres
    radial = jnp.exp(-jnp.square(offset * (NB / 8.0)))
    feat[0:NB, :] = radial
    feat[NB:NFEAT, :] = jnp.zeros((NFEAT - NB, EDGE_DEV), F32)
    feat[NB : NB + 3, :] = d
    wfeat[0:NB, :] = w_rbf[...]
    wfeat[NB:NFEAT, :] = jnp.zeros((NFEAT - NB, D), F32)
    wfeat[NB : NB + 3, :] = w_vec[...]
    rows[0:1, :] = dist
    rows[1:2, :] = cut
    rows[2:3, :] = live
    rows[3:4, :] = kw
    rows[4:5, :] = (-0.5 * math.pi / cutoff_radius) * jnp.sin(angle)
    rows[5:8, :] = jnp.zeros((3, EDGE_DEV), F32)
    scaled = feat[...] * cut
    hi = scaled.astype(BF).astype(F32)
    left = jnp.concatenate([hi, scaled - hi, hi], axis=0).T.astype(BF)
    w = wfeat[...]
    whi = w.astype(BF).astype(F32)
    right = jnp.concatenate([whi, whi, w - whi], axis=0).astype(BF)
    kind = jnp.where(iota((NSPEC, ATOMS_DEV), 0) == species[...].reshape(1, ATOMS_DEV), 1.0, 0.0).astype(BF)
    centre = dot_tn(kind, table[...]).astype(BF)
    expand = atom_rows(ATOMS_DEV)
    slot_row = slot[...].reshape(1, EDGE_DEV)
    local = one_hot_lanes(as_column(slot_row.astype(F32)), EDGE_DEV)
    base[...] = dot_nn(left, right) + dot_nn(expand, centre) + dot_nn(local, message[...])
    kwb[...] = jnp.broadcast_to(as_column(kw), (EDGE_DEV, 128))


def sigmoid(u):
    return 0.5 * jnp.tanh(0.5 * u) + 0.5


def rms_factor(x):
    return lax.rsqrt(jnp.mean(x * x, axis=-1, keepdims=True) + norm_eps)


def rms_back(x, r, z):
    inner = jnp.mean(x * z, axis=-1, keepdims=True)
    return r * z - x * (r * r * r * inner)


LIMIT = 36 * 2**20
INNER = 4 * NBR
OUTER = EDGE_DEV - INNER


def block_list(edges, parts):
    step = edges // parts
    return [slice(i, i + step) for i in range(0, edges, step)]


def shifted(block, offset):
    return slice(block.start + offset, block.stop + offset)


def atom_spans(edges, offset=0):
    return [slice(i + offset, i + offset + NBR) for i in range(0, edges, NBR)]


def spread(x):
    tall = jnp.concatenate([x, jnp.zeros((32 - NBR, 128), F32)], axis=0).astype(BF)
    head = iota((32, 128), 1) >> 5
    return jnp.concatenate(
        [tall * jnp.where(head == h, 1.0, 0.0).astype(BF) for h in range(4)], axis=0
    )


def gather_heads(wide):
    head = iota((1, 128), 1) >> 5
    out = jnp.where(head == 0, wide[0:NBR], 0.0)
    for h in range(1, 4):
        out = jnp.where(head == h, wide[32 * h : 32 * h + NBR], out)
    return out


def forward(x, blocks, offset, kwb, gains, w_qkv, w_out, w_up, w_down, xs, qkv, ups, probs, slope, att):
    edges = blocks[-1].stop
    score_scale = 1.0 / (math.sqrt(D // HEADS) * score_cap)
    slope_scale = 1.0 / math.sqrt(D // HEADS)
    at = [(s, 128 * g) for s in atom_spans(edges) for g in range(2)]
    for layer in range(2):
        for b, v in zip(blocks, x):
            xs[2 * layer, b, :] = v
        gain = gains[2 * layer : 2 * layer + 1, :]
        normed = [(v * rms_factor(v) * gain).astype(BF) for v in x]
        for b, v in zip(blocks, normed):
            qkv[layer, b, :] = dot_nn(v, w_qkv[layer])
        q = [spread(qkv[layer, s, c : c + 128]) for s, c in at]
        k = [qkv[layer, s, D + c : D + c + 128].astype(BF) for s, c in at]
        v = [qkv[layer, s, 2 * D + c : 2 * D + c + 128].astype(BF) for s, c in at]
        t = [dot_nt(kk, qq) for kk, qq in zip(k, q)]
        t = [jnp.tanh(tt * score_scale) for tt in t]
        e = [kwb[shifted(s, offset), :] * jnp.exp(score_cap * tt) for (s, c), tt in zip(at, t)]
        p = [ee * (1.0 / jnp.sum(ee, axis=0, keepdims=True)) for ee in e]
        o = [dot_tn(pp.astype(BF), vv) for pp, vv in zip(p, v)]
        o = [gather_heads(oo) for oo in o]
        for i, (s, c) in enumerate(at):
            probs[layer, s, c : c + 128] = p[i]
            slope[layer, s, c : c + 128] = (1.0 - t[i] * t[i]) * slope_scale
            att[s, c : c + 128] = o[i]
        x = [xs[2 * layer, b, :] + dot_nn(att[b, :].astype(BF), w_out[layer]) for b in blocks]
        for b, v in zip(blocks, x):
            xs[2 * layer + 1, b, :] = v
        gain = gains[2 * layer + 1 : 2 * layer + 2, :]
        normed = [(v * rms_factor(v) * gain).astype(BF) for v in x]
        up = [dot_nn(v, w_up[layer]) for v in normed]
        for b, v in zip(blocks, up):
            ups[layer, b, :] = v
        hidden = [(u * sigmoid(u)).astype(BF) for u in up]
        x = [v + dot_nn(h, w_down[layer]) for v, h in zip(x, hidden)]
    return x


def backward(
    x, blocks, offset, kwb, gains, w_energy, w_qkv, w_out, w_up, w_down, xs, qkv, ups, probs, slope, att, dqkv, acc
):
    edges = blocks[-1].stop
    spans = atom_spans(edges)
    at = [(s, 128 * g) for s in spans for g in range(2)]
    read = gains[4:5, :] * w_energy[...]
    readout = []
    dx = []
    for b, v in zip(blocks, x):
        r = rms_factor(v)
        scaled = v * r
        terms = scaled * read
        readout.append(terms[:, 0:128] + terms[:, 128:256])
        total = jnp.sum(terms, axis=-1, keepdims=True) * (1.0 / D)
        dx.append((kwb[shifted(b, offset), 0:1] * r) * (read - scaled * total))
    for layer in (1, 0):
        dhid = [dot_nt(v.astype(BF), w_down[layer]) for v in dx]
        dup = []
        for b, dh in zip(blocks, dhid):
            u = ups[layer, b, :]
            sig = sigmoid(u)
            dup.append((dh * (sig * (1.0 + u * (1.0 - sig)))).astype(BF))
        gain = gains[2 * layer + 1 : 2 * layer + 2, :]
        dnorm = [dot_nt(v, w_up[layer]) * gain for v in dup]
        new = []
        for b, v, dn in zip(blocks, dx, dnorm):
            xv = xs[2 * layer + 1, b, :]
            new.append(v + rms_back(xv, rms_factor(xv), dn))
        dx = new
        for b, v in zip(blocks, dx):
            att[b, :] = dot_nt(v.astype(BF), w_out[layer])
        do = [spread(att[s, c : c + 128]) for s, c in at]
        v = [qkv[layer, s, 2 * D + c : 2 * D + c + 128].astype(BF) for s, c in at]
        p = [probs[layer, s, c : c + 128] for s, c in at]
        dp = [dot_nt(vv, dd) for vv, dd in zip(v, do)]
        dv = [dot_nn(pp.astype(BF), dd) for pp, dd in zip(p, do)]
        q = [spread(qkv[layer, s, c : c + 128]) for s, c in at]
        k = [qkv[layer, s, D + c : D + c + 128].astype(BF) for s, c in at]
        dl = [pp * (dd - jnp.sum(pp * dd, axis=0, keepdims=True)) for pp, dd in zip(p, dp)]
        ds = [(dd * slope[layer, s, c : c + 128]).astype(BF) for (s, c), dd in zip(at, dl)]
        dk = [dot_nn(dd, qq) for dd, qq in zip(ds, q)]
        dq = [gather_heads(dot_tn(dd, kk)) for dd, kk in zip(ds, k)]
        for i, (s, c) in enumerate(at):
            dqkv[s, c : c + 128] = dq[i]
            dqkv[s, D + c : D + c + 128] = dk[i]
            dqkv[s, 2 * D + c : 2 * D + c + 128] = dv[i]
        for u, s in enumerate(spans):
            total = dl[2 * u] + dl[2 * u + 1]
            acc[s, :] = total if layer == 1 else acc[s, :] + total
        gain = gains[2 * layer : 2 * layer + 1, :]
        dnorm = [dot_nt(dqkv[b, :].astype(BF), w_qkv[layer]) * gain for b in blocks]
        new = []
        for b, v, dn in zip(blocks, dx, dnorm):
            xv = xs[2 * layer, b, :]
            new.append(v + rms_back(xv, rms_factor(xv), dn))
        dx = new
    return readout, dx


def inner_forward_kernel(
    base, kwb, gains, w_qkv, w_out, w_up, w_down, last, xs, qkv, ups, probs, slope, att
):
    blocks = block_list(INNER, 1)
    x = forward(
        [base[0:INNER, :]], blocks, 0, kwb, gains, w_qkv, w_out, w_up, w_down, xs, qkv, ups, probs, slope, att
    )
    last[...] = x[0]


def inner_backward_kernel(
    last, xs, qkv, ups, probs, slope, kwb, gains, w_energy, w_qkv, w_out, w_up, w_down, terms, dx, acc, att, dqkv
):
    blocks = block_list(INNER, 1)
    readout, out = backward(
        [last[...]],
        blocks,
        0,
        kwb,
        gains,
        w_energy,
        w_qkv,
        w_out,
        w_up,
        w_down,
        xs,
        qkv,
        ups,
        probs,
        slope,
        att,
        dqkv,
        acc,
    )
    terms[...] = readout[0]
    dx[...] = out[0]


def layer_kernel(
    base,
    arr_r,
    arr_m,
    arr_l,
    far,
    kwb,
    feat,
    rows,
    wfeat,
    gains,
    w_qkv,
    w_out,
    w_up,
    w_down,
    w_energy,
    pick,
    inner_last,
    inner_terms,
    inner_dx,
    inner_acc,
    tokens,
    reads,
    grad,
    low,
    mid,
    high,
    xs,
    qkv,
    ups,
    probs,
    slope,
    att,
    dqkv,
    acc,
):
    blocks = block_list(OUTER, 2)
    arrived = jnp.concatenate([arr_r[...], arr_m[...], arr_l[...]], axis=0)
    x = []
    for b in blocks:
        here = shifted(b, INNER)
        x.append(base[here, :] + dot_nn(far[here, :], arrived))
    stores = (xs, qkv, ups, probs, slope, att)
    weights = (w_qkv, w_out, w_up, w_down)
    x = forward(x, blocks, INNER, kwb, gains, *weights, *stores)
    tokens[0:INNER, :] = inner_last[...].astype(BF)
    for b, v in zip(blocks, x):
        tokens[shifted(b, INNER), :] = v.astype(BF)
    terms, dx = backward(x, blocks, INNER, kwb, gains, w_energy, *weights, *stores, dqkv, acc)

    w = wfeat[...]
    whi = w.astype(BF)
    wlo = (w - whi.astype(F32)).astype(BF)
    ones8 = jnp.ones((8, 128), BF)

    def to_row(parts):
        hi, lo = split2(jnp.concatenate(parts, axis=0))
        return (dot_nt(ones8, hi) + dot_nt(ones8, lo))[0:1]

    hi, lo = split2(jnp.concatenate([inner_dx[...]] + dx, axis=0))
    back = dot_nt(whi, hi) + dot_nt(whi, lo) + dot_nt(wlo, hi)
    readout = to_row([inner_terms[...]] + terms)
    reads[...] = readout
    acc_row = to_row([inner_acc[...], acc[...]])
    live = rows[2:3, :]
    dist = rows[0:1, :]
    cut = rows[1:2, :]
    f = feat[...]
    dcut = jnp.sum(f * back, axis=0, keepdims=True) + live * (readout + acc_row / cut)
    centres = 0.5 + 4.0 * iota((NB, 1), 0).astype(F32) / (NB - 1)
    dradial = back[0:NB] * f[0:NB] * (dist - centres)
    ddist = dcut * rows[4:5, :] - (2.0 * (NB / 8.0) ** 2) * cut * jnp.sum(
        dradial, axis=0, keepdims=True
    )
    g = cut * back[NB:NFEAT] + f[NB:NFEAT] * (ddist / dist)
    grad[...] = g
    ghi = g.astype(BF).astype(F32)
    both = jnp.concatenate([ghi, g - ghi], axis=0).astype(BF)
    out = dot_nt(both, pick[...])
    out = out[0:8] + out[8:16]
    low[...] = out[:, 0:SIDE]
    mid[...] = out[:, SIDE : 2 * SIDE]
    high[...] = out[:, 2 * SIDE : 3 * SIDE]


def local_force_kernel(grad, slot, rows, reads, out, energy):
    parts = rows[3:4, :] * reads[...]
    hi = parts.astype(BF).astype(F32)
    wide = jnp.broadcast_to(hi, (8, EDGE_DEV))
    rest = jnp.broadcast_to(parts - hi, (8, EDGE_DEV))
    summed = dot_nn(jnp.concatenate([wide, rest], axis=0).astype(BF), atom_rows(ATOMS_DEV))
    energy[...] = summed[0:1] + summed[8:9]
    g = grad[...]
    ghi = g.astype(BF).astype(F32)
    both = jnp.concatenate([ghi, g - ghi], axis=0).astype(BF)
    local = one_hot_lanes(as_column(slot[...].reshape(1, EDGE_DEV).astype(F32)), EDGE_DEV)
    partner = dot_nt(both, local)
    diff = (g - partner[0:8] - partner[8:16]) * rows[2:3, :]
    hi = diff.astype(BF).astype(F32)
    both = jnp.concatenate([hi, diff - hi], axis=0).astype(BF)
    summed = dot_nn(both, atom_rows(ATOMS_DEV))
    out[...] = summed[0:8] + summed[8:16]


def force_kernel(partial, mt, r, m, l, forces):
    pieces = []
    for part in (r, m, l):
        for a in range(3):
            for b in range(3):
                pieces.append(part[b, a])
    table = jnp.concatenate(pieces, axis=1)
    hi = table.astype(BF).astype(F32)
    both = jnp.concatenate([hi, table - hi], axis=0).astype(BF)
    far = dot_nt(both, mt[...].astype(BF))
    forces[...] = (partial[...] - far[0:8] - far[8:16])[0:3]


def vmem_call(kernel, outs, *args, scratch=(), limit=12 * 2**20, place=VMEM):
    spec = pl.BlockSpec(memory_space=VMEM)
    return pl.pallas_call(
        kernel,
        out_shape=outs,
        in_specs=[pl.BlockSpec(memory_space=place)] * len(args),
        out_specs=jax.tree.map(lambda _: spec, outs),
        scratch_shapes=list(scratch),
        compiler_params=pltpu.CompilerParams(vmem_limit_bytes=limit),
    )(*args)


def shape(dims, dtype=F32):
    return jax.ShapeDtypeStruct(dims, dtype)


def messages(atom_state, w_neigh, prev_tokens, send):
    side = shape((SIDE, D), BF)
    return vmem_call(
        message_kernel,
        [shape((EDGE_DEV, D), BF), side, side, side, shape((3 * SIDE, 8))],
        *(
            pltpu.with_memory_space_constraint(v, pltpu.HBM)
            for v in (atom_state, w_neigh, prev_tokens, send)
        ),
        scratch=[
            VMEM((3 * SIDE, 8), F32),
            VMEM((26 * SLOTS,), jnp.int32),
            VMEM((ATOMS_DEV, D), BF),
            VMEM((D, D), BF),
            VMEM((EDGE_DEV, D), BF),
            pltpu.SemaphoreType.DMA((4,)),
        ],
        place=pltpu.HBM,
    )


def geometry(disp, mask, slot, species, message, table, w_vec, w_rbf):
    return vmem_call(
        geometry_kernel,
        [
            shape((EDGE_DEV, D)),
            shape((EDGE_DEV, 128)),
            shape((NFEAT, EDGE_DEV)),
            shape((8, EDGE_DEV)),
            shape((NFEAT, D)),
        ],
        disp,
        mask,
        slot,
        species,
        message,
        table,
        w_vec,
        w_rbf,
    )


def lookups(slot, mask, where):
    outs = [shape((EDGE_DEV, 3 * SIDE), BF), shape((3 * SIDE, EDGE_DEV), BF), shape((ATOMS_DEV, 3 * SIDE))]
    return vmem_call(lookup_kernel, outs, slot, mask, where)


def inner_stores(n):
    return [
        shape((4, n, D)),
        shape((2, n, 3 * D)),
        shape((2, n, FF)),
        shape((2, n, D)),
        shape((2, n, D)),
    ]


def inner_forward(base, kwb, gains, weights):
    n = INNER
    outs = [shape((n, D))] + inner_stores(n)
    return vmem_call(
        inner_forward_kernel, outs, base, kwb, gains, *weights, scratch=[VMEM((n, D), F32)]
    )


def inner_backward(saved, kwb, gains, w_energy, weights):
    n = INNER
    return vmem_call(
        inner_backward_kernel,
        [shape((n, 128)), shape((n, D)), shape((n, 128))],
        *saved,
        kwb,
        gains,
        w_energy,
        *weights,
        scratch=[VMEM((n, D), F32), VMEM((n, 3 * D), F32)],
    )


def layers(base, arr, far, kwb, feat, rows, wfeat, gains, weights, w_energy, pick, inner):
    side = shape((8, SIDE))
    n = EDGE_DEV
    return vmem_call(
        layer_kernel,
        [shape((n, D), BF), shape((1, n)), shape((8, n)), side, side, side],
        base,
        *arr,
        far,
        kwb,
        feat,
        rows,
        wfeat,
        gains,
        *weights,
        w_energy,
        pick,
        *inner,
        limit=LIMIT,
        scratch=[VMEM(v.shape, F32) for v in inner_stores(OUTER)]
        + [VMEM((OUTER, D), F32), VMEM((OUTER, 3 * D), F32), VMEM((OUTER, 128), F32)],
    )


def exchange(low, high, axis):
    count = lax.axis_size(axis)
    outer = [(i, (i + 1 if i % 2 else i - 1) % count) for i in range(count)]
    inner = [(i, i + 1 if i % 2 == 0 else i - 1) for i in range(count)]
    return lax.ppermute(low, axis, outer), lax.ppermute(high, axis, inner)


def on_device(
    displacement,
    neighbour_mask,
    reverse_slot,
    send_edges,
    species,
    prev_tokens,
    atom_state,
    species_table,
    w_neigh,
    w_vec,
    w_rbf,
    gains,
    w_qkv,
    w_out,
    w_up,
    w_down,
    w_energy,
):
    message, low, mid, high, where = messages(atom_state, w_neigh, prev_tokens, send_edges)
    low, high = exchange(low, high, "gx")
    far, pick, mt = lookups(reverse_slot, neighbour_mask, where)
    cells = [v.reshape(3, 3, SLOTS, D) for v in (low, mid, high)]
    low, mid, high = (jnp.stack([v[i] for v in cells]) for i in range(3))
    low, high, late = lax.optimization_barrier((low, high, displacement))
    low, high = exchange(low, high, "gy")
    base, kwb, feat, rows, wfeat = geometry(
        late, neighbour_mask, reverse_slot, species, message, species_table, w_vec, w_rbf
    )
    weights = (w_qkv, w_out, w_up, w_down)
    w_energy = w_energy.reshape(1, D)
    saved = inner_forward(base, kwb, gains, weights)
    cells = (low, mid, high)
    low, mid, high = (jnp.stack([v[:, i] for v in cells], axis=1) for i in range(3))
    low, high, *saved = lax.optimization_barrier((low, high, *saved))
    low, high = exchange(low, high, "gz")
    terms, dx, acc = inner_backward(saved, kwb, gains, w_energy, weights)
    arr = [v.reshape(SIDE, D) for v in (low, mid, high)]
    tokens, reads, grad, low, mid, high = layers(
        base,
        arr,
        far,
        kwb,
        feat,
        rows,
        wfeat,
        gains,
        weights,
        w_energy,
        pick,
        (saved[0], terms, dx, acc),
    )
    low, high = exchange(low, high, "gx")
    cells = jnp.stack([low, mid, high])
    cut = 3 * SLOTS
    low, mid, high = (cells[:, :, i * cut : (i + 1) * cut] for i in range(3))
    low, high = exchange(low, high, "gy")
    cells = jnp.stack([low, mid, high])
    cut = SLOTS
    low, mid, high = (cells[..., i * cut : (i + 1) * cut] for i in range(3))
    low, high, late = lax.optimization_barrier((low, high, grad))
    low, high = exchange(low, high, "gz")
    partial, energy = vmem_call(
        local_force_kernel,
        [shape((8, ATOMS_DEV)), shape((1, ATOMS_DEV))],
        late,
        reverse_slot,
        rows,
        reads,
    )
    forces = vmem_call(force_kernel, shape((3, ATOMS_DEV)), partial, mt, low, mid, high)
    return (tokens, energy.reshape(ATOMS_DEV), forces)


def solution(mesh):
    return jax.shard_map(
        on_device,
        mesh=mesh,
        in_specs=(
            P(None, ("gx", "gy", "gz")),
            P(("gx", "gy", "gz")),
            P(("gx", "gy", "gz")),
            P(("gx", "gy", "gz")),
            P(("gx", "gy", "gz")),
            P(("gx", "gy", "gz"), None),
            P(("gx", "gy", "gz"), None),
            P(),
            P(),
            P(),
            P(),
            P(),
            P(),
            P(),
            P(),
            P(),
            P(),
        ),
        out_specs=(P(("gx", "gy", "gz"), None), P(("gx", "gy", "gz")), P(None, ("gx", "gy", "gz"))),
        check_vma=False,
    )
```

```python
import math

import jax
import jax.numpy as jnp
from jax import lax
from jax.experimental import pallas as pl
from jax.experimental.pallas import tpu as pltpu
from jax.sharding import PartitionSpec as P

HEADS = 8
NBR = 24
ATOMS_DEV = 32
EDGE_DEV = 768
D = 256
FF = 512
NB = 64
NSPEC = 85
SLOTS = 16
SIDE = 9 * SLOTS
NFEAT = 72
score_cap = 8.0
cutoff_radius = 5.0
norm_eps = 1e-06
AXES = ("gx", "gy", "gz")

BF = jnp.bfloat16
F32 = jnp.float32
VMEM = pltpu.VMEM


def dot_nn(a, b):
    return lax.dot_general(a, b, (((1,), (0,)), ((), ())), preferred_element_type=F32)


def dot_nt(a, b):
    return lax.dot_general(a, b, (((1,), (1,)), ((), ())), preferred_element_type=F32)


def dot_tn(a, b):
    return lax.dot_general(a, b, (((0,), (0,)), ((), ())), preferred_element_type=F32)


def iota(shape, axis):
    return lax.broadcasted_iota(jnp.int32, shape, axis)


def split2(x):
    hi = x.astype(BF)
    lo = (x - hi.astype(F32)).astype(BF)
    return hi, lo


def as_column(row):
    return jnp.broadcast_to(row, (8, row.shape[1])).T[:, 0:1]


def atom_rows(count, dtype=BF):
    edge = iota((count * NBR, count), 0)
    first = iota((count * NBR, count), 1) * NBR
    return jnp.where((edge >= first) & (edge < first + NBR), 1.0, 0.0).astype(dtype)


def one_hot_lanes(column, width):
    lanes = iota((column.shape[0], width), 1).astype(F32)
    return jnp.where(lanes == column, 1.0, 0.0).astype(BF)


def message_kernel(
    state_far,
    w_far,
    prev_far,
    send_far,
    message,
    low,
    mid,
    high,
    where,
    order,
    send,
    state,
    w_neigh,
    prev,
    sems,
):
    moves = [
        pltpu.make_async_copy(src, dst, sems.at[i])
        for i, (src, dst) in enumerate(
            ((send_far, send), (state_far, state), (w_far, w_neigh), (prev_far, prev))
        )
    ]
    for move in moves:
        move.start()
    expand = atom_rows(ATOMS_DEV)
    moves[0].wait()
    count = 26 * SLOTS
    sent = jnp.broadcast_to(send[...].reshape(1, count).astype(F32), (8, count)).T
    flips = [lax.axis_index(axis) & 1 for axis in AXES]
    for bucket in range(27):
        place = 0
        for axis, digit in enumerate((bucket // 9, bucket // 3 % 3, bucket % 3)):
            place = place * 3 + digit + flips[axis] * (2 - 2 * digit)
        rows = pl.ds(pl.multiple_of(place * SLOTS, SLOTS), SLOTS)
        if bucket == 13:
            order[rows, :] = jnp.full((SLOTS, 8), -1.0, F32)
        else:
            start = (bucket - (bucket > 13)) * SLOTS
            order[rows, :] = sent[start : start + SLOTS]
    column = order[...]
    where[...] = column
    pick = one_hot_lanes(column[:, 0:1], EDGE_DEV)
    moves[1].wait()
    moves[2].wait()
    projected = dot_nn(state[...], w_neigh[...])
    hi, lo = split2(projected)
    rest = (projected - hi.astype(F32) - lo.astype(F32)).astype(BF)
    wide = dot_nn(expand, hi) + dot_nn(expand, lo) + dot_nn(expand, rest)
    moves[3].wait()
    out = (prev[...].astype(F32) + wide).astype(BF)
    message[...] = out
    payload = dot_nn(pick, out).astype(BF)
    low[...] = payload[0:SIDE]
    mid[...] = payload[SIDE : 2 * SIDE]
    high[...] = payload[2 * SIDE : 3 * SIDE]


def remote_index(slot):
    far = slot - EDGE_DEV
    bucket = far >> 4
    pair = (bucket * 11) >> 5
    first = (pair * 11) >> 5
    digits = [first, pair - 3 * first, bucket - 3 * pair]
    for i, axis in enumerate(AXES):
        flip = lax.axis_index(axis) & 1
        digits[i] = digits[i] + flip * (2 - 2 * digits[i])
    place = digits[2] * SIDE + (digits[0] * 3 + digits[1]) * SLOTS + (far & 15)
    return jnp.where(far >= 0, place, -1).astype(F32)


def lookup_kernel(slot, mask, where, far, pick, mt):
    slot_row = slot[...].reshape(1, EDGE_DEV)
    live = mask[...].reshape(1, EDGE_DEV).astype(F32)
    hot = one_hot_lanes(as_column(remote_index(slot_row)), 3 * SIDE)
    far[...] = hot
    pick[...] = one_hot_lanes(where[:, 0:1], EDGE_DEV)
    live_rows = atom_rows(ATOMS_DEV, F32) * as_column(live)
    mt[...] = dot_tn(live_rows.astype(BF), hot)


def geometry_kernel(
    disp, mask, slot, species, message, table, w_vec, w_rbf, base, kwb, feat, rows, wfeat
):
    d = disp[...]
    dist = jnp.sqrt(jnp.sum(d * d, axis=0, keepdims=True) + 0.5)
    angle = (math.pi / cutoff_radius) * dist
    cut = 0.5 * (jnp.cos(angle) + 1.0)
    live = mask[...].reshape(1, EDGE_DEV).astype(F32)
    kw = live * cut
    centres = 0.5 + 4.0 * iota((NB, 1), 0).astype(F32) / (NB - 1)
    offset = dist - centres
    radial = jnp.exp(-jnp.square(offset * (NB / 8.0)))
    feat[0:NB, :] = radial
    feat[NB:NFEAT, :] = jnp.zeros((NFEAT - NB, EDGE_DEV), F32)
    feat[NB : NB + 3, :] = d
    wfeat[0:NB, :] = w_rbf[...]
    wfeat[NB:NFEAT, :] = jnp.zeros((NFEAT - NB, D), F32)
    wfeat[NB : NB + 3, :] = w_vec[...]
    rows[0:1, :] = dist
    rows[1:2, :] = cut
    rows[2:3, :] = live
    rows[3:4, :] = kw
    rows[4:5, :] = (-0.5 * math.pi / cutoff_radius) * jnp.sin(angle)
    rows[5:8, :] = jnp.zeros((3, EDGE_DEV), F32)
    scaled = feat[...] * cut
    hi = scaled.astype(BF).astype(F32)
    left = jnp.concatenate([hi, scaled - hi, hi], axis=0).T.astype(BF)
    w = wfeat[...]
    whi = w.astype(BF).astype(F32)
    right = jnp.concatenate([whi, whi, w - whi], axis=0).astype(BF)
    kind = jnp.where(iota((NSPEC, ATOMS_DEV), 0) == species[...].reshape(1, ATOMS_DEV), 1.0, 0.0).astype(BF)
    centre = dot_tn(kind, table[...]).astype(BF)
    expand = atom_rows(ATOMS_DEV)
    slot_row = slot[...].reshape(1, EDGE_DEV)
    local = one_hot_lanes(as_column(slot_row.astype(F32)), EDGE_DEV)
    base[...] = dot_nn(left, right) + dot_nn(expand, centre) + dot_nn(local, message[...])
    kwb[...] = jnp.broadcast_to(as_column(kw), (EDGE_DEV, 128))


def sigmoid(u):
    return 0.5 * jnp.tanh(0.5 * u) + 0.5


def rms_factor(x):
    return lax.rsqrt(jnp.mean(x * x, axis=-1, keepdims=True) + norm_eps)


def rms_all(x, blocks, xs, rs, gains, place):
    gain = gains[place : place + 1, :]
    out = []
    for b, v in zip(blocks, x):
        r = rms_factor(v)
        scaled = v * r
        xs[place, b, :] = scaled
        rs[place, b, :] = jnp.broadcast_to(r, (v.shape[0], 128))
        out.append((scaled * gain).astype(BF))
    return out


def rms_back(scaled, r, z):
    inner = jnp.mean(scaled * z, axis=-1, keepdims=True)
    return jnp.concatenate([r, r], axis=1) * (z - scaled * inner)


LIMIT = 36 * 2**20
INNER = 4 * NBR
OUTER = EDGE_DEV - INNER


def block_list(edges, parts):
    step = edges // parts
    return [slice(i, i + step) for i in range(0, edges, step)]


def shifted(block, offset):
    return slice(block.start + offset, block.stop + offset)


def atom_spans(edges, offset=0):
    return [slice(i + offset, i + offset + NBR) for i in range(0, edges, NBR)]


def spread(x):
    tall = jnp.concatenate([x, jnp.zeros((32 - NBR, 128), F32)], axis=0).astype(BF)
    head = iota((32, 128), 1) >> 5
    return jnp.concatenate(
        [tall * jnp.where(head == h, 1.0, 0.0).astype(BF) for h in range(4)], axis=0
    )


def gather_heads(wide):
    head = iota((1, 128), 1) >> 5
    out = jnp.where(head == 0, wide[0:NBR], 0.0)
    for h in range(1, 4):
        out = jnp.where(head == h, wide[32 * h : 32 * h + NBR], out)
    return out


def forward(x, blocks, offset, kwb, gains, w_qkv, w_out, w_up, w_down, xs, rs, qkv, ups, probs, slope, att):
    edges = blocks[-1].stop
    score_scale = 1.0 / (math.sqrt(D // HEADS) * score_cap)
    slope_scale = 1.0 / math.sqrt(D // HEADS)
    at = [(s, 128 * g) for s in atom_spans(edges) for g in range(2)]
    for layer in range(2):
        normed = rms_all(x, blocks, xs, rs, gains, 2 * layer)
        for b, v in zip(blocks, normed):
            qkv[layer, b, :] = dot_nn(v, w_qkv[layer])
        q = [spread(qkv[layer, s, c : c + 128]) for s, c in at]
        k = [qkv[layer, s, D + c : D + c + 128].astype(BF) for s, c in at]
        v = [qkv[layer, s, 2 * D + c : 2 * D + c + 128].astype(BF) for s, c in at]
        t = [dot_nt(kk, qq) for kk, qq in zip(k, q)]
        t = [jnp.tanh(tt * score_scale) for tt in t]
        e = [kwb[shifted(s, offset), :] * jnp.exp(score_cap * tt) for (s, c), tt in zip(at, t)]
        p = [ee * (1.0 / jnp.sum(ee, axis=0, keepdims=True)) for ee in e]
        o = [dot_tn(pp.astype(BF), vv) for pp, vv in zip(p, v)]
        o = [gather_heads(oo) for oo in o]
        for i, (s, c) in enumerate(at):
            probs[layer, s, c : c + 128] = p[i]
            slope[layer, s, c : c + 128] = (1.0 - t[i] * t[i]) * slope_scale
            att[s, c : c + 128] = o[i]
        x = [v + dot_nn(att[b, :].astype(BF), w_out[layer]) for b, v in zip(blocks, x)]
        normed = rms_all(x, blocks, xs, rs, gains, 2 * layer + 1)
        up = [dot_nn(v, w_up[layer]) for v in normed]
        sig = [sigmoid(u) for u in up]
        hidden = [u * s for u, s in zip(up, sig)]
        for b, s, h in zip(blocks, sig, hidden):
            ups[layer, b, :] = s + h * (1.0 - s)
        x = [v + dot_nn(h.astype(BF), w_down[layer]) for v, h in zip(x, hidden)]
    return x


def backward(
    x, blocks, offset, kwb, gains, w_energy, w_qkv, w_out, w_up, w_down, xs, rs, qkv, ups, probs, slope, att, dqkv, acc
):
    edges = blocks[-1].stop
    spans = atom_spans(edges)
    at = [(s, 128 * g) for s in spans for g in range(2)]
    read = gains[4:5, :] * w_energy[...]
    readout = []
    dx = []
    for b, v in zip(blocks, x):
        r = rms_factor(v)
        scaled = v * r
        terms = scaled * read
        readout.append(terms[:, 0:128] + terms[:, 128:256])
        total = jnp.sum(terms, axis=-1, keepdims=True) * (1.0 / D)
        dx.append((kwb[shifted(b, offset), 0:1] * r) * (read - scaled * total))
    for layer in (1, 0):
        dhid = [dot_nt(v.astype(BF), w_down[layer]) for v in dx]
        dup = [(dh * ups[layer, b, :]).astype(BF) for b, dh in zip(blocks, dhid)]
        gain = gains[2 * layer + 1 : 2 * layer + 2, :]
        dnorm = [dot_nt(v, w_up[layer]) * gain for v in dup]
        new = []
        for b, v, dn in zip(blocks, dx, dnorm):
            new.append(v + rms_back(xs[2 * layer + 1, b, :], rs[2 * layer + 1, b, :], dn))
        dx = new
        for b, v in zip(blocks, dx):
            att[b, :] = dot_nt(v.astype(BF), w_out[layer])
        do = [spread(att[s, c : c + 128]) for s, c in at]
        v = [qkv[layer, s, 2 * D + c : 2 * D + c + 128].astype(BF) for s, c in at]
        p = [probs[layer, s, c : c + 128] for s, c in at]
        dp = [dot_nt(vv, dd) for vv, dd in zip(v, do)]
        dv = [dot_nn(pp.astype(BF), dd) for pp, dd in zip(p, do)]
        q = [spread(qkv[layer, s, c : c + 128]) for s, c in at]
        k = [qkv[layer, s, D + c : D + c + 128].astype(BF) for s, c in at]
        dl = [pp * (dd - jnp.sum(pp * dd, axis=0, keepdims=True)) for pp, dd in zip(p, dp)]
        ds = [(dd * slope[layer, s, c : c + 128]).astype(BF) for (s, c), dd in zip(at, dl)]
        dk = [dot_nn(dd, qq) for dd, qq in zip(ds, q)]
        dq = [gather_heads(dot_tn(dd, kk)) for dd, kk in zip(ds, k)]
        for i, (s, c) in enumerate(at):
            dqkv[s, c : c + 128] = dq[i]
            dqkv[s, D + c : D + c + 128] = dk[i]
            dqkv[s, 2 * D + c : 2 * D + c + 128] = dv[i]
        for u, s in enumerate(spans):
            total = dl[2 * u] + dl[2 * u + 1]
            acc[s, :] = total if layer == 1 else acc[s, :] + total
        gain = gains[2 * layer : 2 * layer + 1, :]
        dnorm = [dot_nt(dqkv[b, :].astype(BF), w_qkv[layer]) * gain for b in blocks]
        new = []
        for b, v, dn in zip(blocks, dx, dnorm):
            new.append(v + rms_back(xs[2 * layer, b, :], rs[2 * layer, b, :], dn))
        dx = new
    return readout, dx


def inner_forward_kernel(
    base, kwb, gains, w_qkv, w_out, w_up, w_down, last, xs, rs, qkv, ups, probs, slope, att
):
    blocks = block_list(INNER, 1)
    x = forward(
        [base[0:INNER, :]], blocks, 0, kwb, gains, w_qkv, w_out, w_up, w_down, xs, rs, qkv, ups, probs, slope, att
    )
    last[...] = x[0]


def inner_backward_kernel(
    last, xs, rs, qkv, ups, probs, slope, kwb, gains, w_energy, w_qkv, w_out, w_up, w_down, terms, dx, acc, att, dqkv
):
    blocks = block_list(INNER, 1)
    readout, out = backward(
        [last[...]],
        blocks,
        0,
        kwb,
        gains,
        w_energy,
        w_qkv,
        w_out,
        w_up,
        w_down,
        xs,
        rs,
        qkv,
        ups,
        probs,
        slope,
        att,
        dqkv,
        acc,
    )
    terms[...] = readout[0]
    dx[...] = out[0]


def layer_kernel(
    base,
    arr_r,
    arr_m,
    arr_l,
    far,
    kwb,
    feat,
    rows,
    wfeat,
    gains,
    w_qkv,
    w_out,
    w_up,
    w_down,
    w_energy,
    pick,
    inner_last,
    inner_terms,
    inner_dx,
    inner_acc,
    tokens,
    reads,
    grad,
    low,
    mid,
    high,
    xs,
    rs,
    qkv,
    ups,
    probs,
    slope,
    att,
    dqkv,
    acc,
):
    blocks = block_list(OUTER, 3)
    arrived = jnp.concatenate([arr_r[...], arr_m[...], arr_l[...]], axis=0)
    x = []
    for b in blocks:
        here = shifted(b, INNER)
        x.append(base[here, :] + dot_nn(far[here, :], arrived))
    stores = (xs, rs, qkv, ups, probs, slope, att)
    weights = (w_qkv, w_out, w_up, w_down)
    x = forward(x, blocks, INNER, kwb, gains, *weights, *stores)
    tokens[0:INNER, :] = inner_last[...].astype(BF)
    for b, v in zip(blocks, x):
        tokens[shifted(b, INNER), :] = v.astype(BF)
    terms, dx = backward(x, blocks, INNER, kwb, gains, w_energy, *weights, *stores, dqkv, acc)

    w = wfeat[...]
    whi = w.astype(BF)
    ones8 = jnp.ones((8, 128), BF)

    def to_row(parts):
        hi, lo = split2(jnp.concatenate(parts, axis=0))
        return (dot_nt(ones8, hi) + dot_nt(ones8, lo))[0:1]

    hi, lo = split2(jnp.concatenate([inner_dx[...]] + dx, axis=0))
    pair = dot_nt(jnp.concatenate([w.astype(BF).astype(F32), w - whi.astype(F32)], axis=0).astype(BF), hi)
    back = pair[0:NFEAT] + pair[NFEAT : 2 * NFEAT] + dot_nt(whi, lo)
    readout = to_row([inner_terms[...]] + terms)
    reads[...] = readout
    acc_row = to_row([inner_acc[...], acc[...]])
    live = rows[2:3, :]
    dist = rows[0:1, :]
    cut = rows[1:2, :]
    f = feat[...]
    dcut = jnp.sum(f * back, axis=0, keepdims=True) + live * (readout + acc_row / cut)
    centres = 0.5 + 4.0 * iota((NB, 1), 0).astype(F32) / (NB - 1)
    dradial = back[0:NB] * f[0:NB] * (dist - centres)
    ddist = dcut * rows[4:5, :] - (2.0 * (NB / 8.0) ** 2) * cut * jnp.sum(
        dradial, axis=0, keepdims=True
    )
    g = cut * back[NB:NFEAT] + f[NB:NFEAT] * (ddist / dist)
    grad[...] = g
    ghi = g.astype(BF).astype(F32)
    both = jnp.concatenate([ghi, g - ghi], axis=0).astype(BF)
    out = dot_nt(both, pick[...])
    out = out[0:8] + out[8:16]
    low[...] = out[:, 0:SIDE]
    mid[...] = out[:, SIDE : 2 * SIDE]
    high[...] = out[:, 2 * SIDE : 3 * SIDE]


def local_force_kernel(grad, slot, rows, reads, out, energy):
    parts = rows[3:4, :] * reads[...]
    hi = parts.astype(BF).astype(F32)
    wide = jnp.broadcast_to(hi, (8, EDGE_DEV))
    rest = jnp.broadcast_to(parts - hi, (8, EDGE_DEV))
    summed = dot_nn(jnp.concatenate([wide, rest], axis=0).astype(BF), atom_rows(ATOMS_DEV))
    energy[...] = summed[0:1] + summed[8:9]
    g = grad[...]
    ghi = g.astype(BF).astype(F32)
    both = jnp.concatenate([ghi, g - ghi], axis=0).astype(BF)
    local = one_hot_lanes(as_column(slot[...].reshape(1, EDGE_DEV).astype(F32)), EDGE_DEV)
    partner = dot_nt(both, local)
    diff = (g - partner[0:8] - partner[8:16]) * rows[2:3, :]
    hi = diff.astype(BF).astype(F32)
    both = jnp.concatenate([hi, diff - hi], axis=0).astype(BF)
    summed = dot_nn(both, atom_rows(ATOMS_DEV))
    out[...] = summed[0:8] + summed[8:16]


def force_kernel(partial, mt, r, m, l, forces):
    pieces = []
    for part in (r, m, l):
        for a in range(3):
            for b in range(3):
                pieces.append(part[b, a])
    table = jnp.concatenate(pieces, axis=1)
    hi = table.astype(BF).astype(F32)
    both = jnp.concatenate([hi, table - hi], axis=0).astype(BF)
    far = dot_nt(both, mt[...].astype(BF))
    forces[...] = (partial[...] - far[0:8] - far[8:16])[0:3]


def vmem_call(kernel, outs, *args, scratch=(), limit=12 * 2**20, place=VMEM):
    spec = pl.BlockSpec(memory_space=VMEM)
    return pl.pallas_call(
        kernel,
        out_shape=outs,
        in_specs=[pl.BlockSpec(memory_space=place)] * len(args),
        out_specs=jax.tree.map(lambda _: spec, outs),
        scratch_shapes=list(scratch),
        compiler_params=pltpu.CompilerParams(vmem_limit_bytes=limit),
    )(*args)


def shape(dims, dtype=F32):
    return jax.ShapeDtypeStruct(dims, dtype)


def messages(atom_state, w_neigh, prev_tokens, send):
    side = shape((SIDE, D), BF)
    return vmem_call(
        message_kernel,
        [shape((EDGE_DEV, D), BF), side, side, side, shape((3 * SIDE, 8))],
        *(
            pltpu.with_memory_space_constraint(v, pltpu.HBM)
            for v in (atom_state, w_neigh, prev_tokens, send)
        ),
        scratch=[
            VMEM((3 * SIDE, 8), F32),
            VMEM((26 * SLOTS,), jnp.int32),
            VMEM((ATOMS_DEV, D), BF),
            VMEM((D, D), BF),
            VMEM((EDGE_DEV, D), BF),
            pltpu.SemaphoreType.DMA((4,)),
        ],
        place=pltpu.HBM,
    )


def geometry(disp, mask, slot, species, message, table, w_vec, w_rbf):
    return vmem_call(
        geometry_kernel,
        [
            shape((EDGE_DEV, D)),
            shape((EDGE_DEV, 128)),
            shape((NFEAT, EDGE_DEV)),
            shape((8, EDGE_DEV)),
            shape((NFEAT, D)),
        ],
        disp,
        mask,
        slot,
        species,
        message,
        table,
        w_vec,
        w_rbf,
    )


def lookups(slot, mask, where):
    outs = [shape((EDGE_DEV, 3 * SIDE), BF), shape((3 * SIDE, EDGE_DEV), BF), shape((ATOMS_DEV, 3 * SIDE))]
    return vmem_call(lookup_kernel, outs, slot, mask, where)


def inner_stores(n):
    return [
        shape((4, n, D)),
        shape((4, n, 128)),
        shape((2, n, 3 * D)),
        shape((2, n, FF)),
        shape((2, n, D)),
        shape((2, n, D)),
    ]


def inner_forward(base, kwb, gains, weights):
    n = INNER
    outs = [shape((n, D))] + inner_stores(n)
    return vmem_call(
        inner_forward_kernel, outs, base, kwb, gains, *weights, scratch=[VMEM((n, D), F32)]
    )


def inner_backward(saved, kwb, gains, w_energy, weights):
    n = INNER
    return vmem_call(
        inner_backward_kernel,
        [shape((n, 128)), shape((n, D)), shape((n, 128))],
        *saved,
        kwb,
        gains,
        w_energy,
        *weights,
        scratch=[VMEM((n, D), F32), VMEM((n, 3 * D), F32)],
    )


def layers(base, arr, far, kwb, feat, rows, wfeat, gains, weights, w_energy, pick, inner):
    side = shape((8, SIDE))
    n = EDGE_DEV
    return vmem_call(
        layer_kernel,
        [shape((n, D), BF), shape((1, n)), shape((8, n)), side, side, side],
        base,
        *arr,
        far,
        kwb,
        feat,
        rows,
        wfeat,
        gains,
        *weights,
        w_energy,
        pick,
        *inner,
        limit=LIMIT,
        scratch=[VMEM(v.shape, F32) for v in inner_stores(OUTER)]
        + [VMEM((OUTER, D), F32), VMEM((OUTER, 3 * D), F32), VMEM((OUTER, 128), F32)],
    )


def exchange(low, high, axis):
    count = lax.axis_size(axis)
    outer = [(i, (i + 1 if i % 2 else i - 1) % count) for i in range(count)]
    inner = [(i, i + 1 if i % 2 == 0 else i - 1) for i in range(count)]
    return lax.ppermute(low, axis, outer), lax.ppermute(high, axis, inner)


def on_device(
    displacement,
    neighbour_mask,
    reverse_slot,
    send_edges,
    species,
    prev_tokens,
    atom_state,
    species_table,
    w_neigh,
    w_vec,
    w_rbf,
    gains,
    w_qkv,
    w_out,
    w_up,
    w_down,
    w_energy,
):
    message, low, mid, high, where = messages(atom_state, w_neigh, prev_tokens, send_edges)
    low, high = exchange(low, high, "gx")
    far, pick, mt = lookups(reverse_slot, neighbour_mask, where)
    cells = [v.reshape(3, 3, SLOTS, D) for v in (low, mid, high)]
    low, mid, high = (jnp.stack([v[i] for v in cells]) for i in range(3))
    low, high, late = lax.optimization_barrier((low, high, displacement))
    low, high = exchange(low, high, "gy")
    base, kwb, feat, rows, wfeat = geometry(
        late, neighbour_mask, reverse_slot, species, message, species_table, w_vec, w_rbf
    )
    weights = (w_qkv, w_out, w_up, w_down)
    w_energy = w_energy.reshape(1, D)
    saved = inner_forward(base, kwb, gains, weights)
    cells = (low, mid, high)
    low, mid, high = (jnp.stack([v[:, i] for v in cells], axis=1) for i in range(3))
    low, high, *saved = lax.optimization_barrier((low, high, *saved))
    low, high = exchange(low, high, "gz")
    terms, dx, acc = inner_backward(saved, kwb, gains, w_energy, weights)
    arr = [v.reshape(SIDE, D) for v in (low, mid, high)]
    tokens, reads, grad, low, mid, high = layers(
        base,
        arr,
        far,
        kwb,
        feat,
        rows,
        wfeat,
        gains,
        weights,
        w_energy,
        pick,
        (saved[0], terms, dx, acc),
    )
    low, high = exchange(low, high, "gx")
    cells = jnp.stack([low, mid, high])
    cut = 3 * SLOTS
    low, mid, high = (cells[:, :, i * cut : (i + 1) * cut] for i in range(3))
    low, high = exchange(low, high, "gy")
    cells = jnp.stack([low, mid, high])
    cut = SLOTS
    low, mid, high = (cells[..., i * cut : (i + 1) * cut] for i in range(3))
    low, high, late = lax.optimization_barrier((low, high, grad))
    low, high = exchange(low, high, "gz")
    partial, energy = vmem_call(
        local_force_kernel,
        [shape((8, ATOMS_DEV)), shape((1, ATOMS_DEV))],
        late,
        reverse_slot,
        rows,
        reads,
    )
    forces = vmem_call(force_kernel, shape((3, ATOMS_DEV)), partial, mt, low, mid, high)
    return (tokens, energy.reshape(ATOMS_DEV), forces)


def solution(mesh):
    return jax.shard_map(
        on_device,
        mesh=mesh,
        in_specs=(
            P(None, ("gx", "gy", "gz")),
            P(("gx", "gy", "gz")),
            P(("gx", "gy", "gz")),
            P(("gx", "gy", "gz")),
            P(("gx", "gy", "gz")),
            P(("gx", "gy", "gz"), None),
            P(("gx", "gy", "gz"), None),
            P(),
            P(),
            P(),
            P(),
            P(),
            P(),
            P(),
            P(),
            P(),
            P(),
        ),
        out_specs=(P(("gx", "gy", "gz"), None), P(("gx", "gy", "gz")), P(None, ("gx", "gy", "gz"))),
        check_vma=False,
    )
```

```python
import math

import jax
import jax.numpy as jnp
from jax import lax
from jax.experimental import pallas as pl
from jax.experimental.pallas import tpu as pltpu
from jax.sharding import PartitionSpec as P

HEADS = 8
NBR = 24
ATOMS_DEV = 32
EDGE_DEV = 768
D = 256
FF = 512
NB = 64
NSPEC = 85
SLOTS = 16
SIDE = 9 * SLOTS
NFEAT = 72
score_cap = 8.0
cutoff_radius = 5.0
norm_eps = 1e-06
AXES = ("gx", "gy", "gz")

BF = jnp.bfloat16
F32 = jnp.float32
VMEM = pltpu.VMEM


def dot_nn(a, b):
    return lax.dot_general(a, b, (((1,), (0,)), ((), ())), preferred_element_type=F32)


def dot_nt(a, b):
    return lax.dot_general(a, b, (((1,), (1,)), ((), ())), preferred_element_type=F32)


def dot_tn(a, b):
    return lax.dot_general(a, b, (((0,), (0,)), ((), ())), preferred_element_type=F32)


def iota(shape, axis):
    return lax.broadcasted_iota(jnp.int32, shape, axis)


def split2(x):
    hi = x.astype(BF)
    lo = (x - hi.astype(F32)).astype(BF)
    return hi, lo


def as_column(row):
    return jnp.broadcast_to(row, (8, row.shape[1])).T[:, 0:1]


def atom_rows(count, dtype=BF):
    edge = iota((count * NBR, count), 0)
    first = iota((count * NBR, count), 1) * NBR
    return jnp.where((edge >= first) & (edge < first + NBR), 1.0, 0.0).astype(dtype)


def one_hot_lanes(column, width):
    lanes = iota((column.shape[0], width), 1).astype(F32)
    return jnp.where(lanes == column, 1.0, 0.0).astype(BF)


def message_kernel(
    state_far,
    w_far,
    prev_far,
    send_far,
    message,
    low,
    mid,
    high,
    where,
    order,
    send,
    state,
    w_neigh,
    prev,
    sems,
):
    moves = [
        pltpu.make_async_copy(src, dst, sems.at[i])
        for i, (src, dst) in enumerate(
            ((send_far, send), (state_far, state), (w_far, w_neigh), (prev_far, prev))
        )
    ]
    for move in moves:
        move.start()
    expand = atom_rows(ATOMS_DEV)
    moves[0].wait()
    count = 26 * SLOTS
    sent = jnp.broadcast_to(send[...].reshape(1, count).astype(F32), (8, count)).T
    flips = [lax.axis_index(axis) & 1 for axis in AXES]
    for bucket in range(27):
        place = 0
        for axis, digit in enumerate((bucket // 9, bucket // 3 % 3, bucket % 3)):
            place = place * 3 + digit + flips[axis] * (2 - 2 * digit)
        rows = pl.ds(pl.multiple_of(place * SLOTS, SLOTS), SLOTS)
        if bucket == 13:
            order[rows, :] = jnp.full((SLOTS, 8), -1.0, F32)
        else:
            start = (bucket - (bucket > 13)) * SLOTS
            order[rows, :] = sent[start : start + SLOTS]
    column = order[...]
    where[...] = column
    pick = one_hot_lanes(column[:, 0:1], EDGE_DEV)
    moves[1].wait()
    moves[2].wait()
    projected = dot_nn(state[...], w_neigh[...])
    hi, lo = split2(projected)
    rest = (projected - hi.astype(F32) - lo.astype(F32)).astype(BF)
    wide = dot_nn(expand, hi) + dot_nn(expand, lo) + dot_nn(expand, rest)
    moves[3].wait()
    out = (prev[...].astype(F32) + wide).astype(BF)
    message[...] = out
    payload = dot_nn(pick, out).astype(BF)
    low[...] = payload[0:SIDE]
    mid[...] = payload[SIDE : 2 * SIDE]
    high[...] = payload[2 * SIDE : 3 * SIDE]


def remote_index(slot):
    far = slot - EDGE_DEV
    bucket = far >> 4
    pair = (bucket * 11) >> 5
    first = (pair * 11) >> 5
    digits = [first, pair - 3 * first, bucket - 3 * pair]
    for i, axis in enumerate(AXES):
        flip = lax.axis_index(axis) & 1
        digits[i] = digits[i] + flip * (2 - 2 * digits[i])
    place = digits[2] * SIDE + (digits[0] * 3 + digits[1]) * SLOTS + (far & 15)
    return jnp.where(far >= 0, place, -1).astype(F32)


def lookup_kernel(slot, mask, where, far, pick, mt):
    slot_row = slot[...].reshape(1, EDGE_DEV)
    live = mask[...].reshape(1, EDGE_DEV).astype(F32)
    hot = one_hot_lanes(as_column(remote_index(slot_row)), 3 * SIDE)
    far[...] = hot
    pick[...] = one_hot_lanes(where[:, 0:1], EDGE_DEV)
    live_rows = atom_rows(ATOMS_DEV, F32) * as_column(live)
    mt[...] = dot_tn(live_rows.astype(BF), hot)


def geometry_kernel(
    disp, mask, slot, species, message, table, w_vec, w_rbf, base, kwb, feat, rows, wfeat
):
    d = disp[...]
    dist = jnp.sqrt(jnp.sum(d * d, axis=0, keepdims=True) + 0.5)
    angle = (math.pi / cutoff_radius) * dist
    cut = 0.5 * (jnp.cos(angle) + 1.0)
    live = mask[...].reshape(1, EDGE_DEV).astype(F32)
    kw = live * cut
    centres = 0.5 + 4.0 * iota((NB, 1), 0).astype(F32) / (NB - 1)
    offset = dist - centres
    radial = jnp.exp(-jnp.square(offset * (NB / 8.0)))
    feat[0:NB, :] = radial
    feat[NB:NFEAT, :] = jnp.zeros((NFEAT - NB, EDGE_DEV), F32)
    feat[NB : NB + 3, :] = d
    wfeat[0:NB, :] = w_rbf[...]
    wfeat[NB:NFEAT, :] = jnp.zeros((NFEAT - NB, D), F32)
    wfeat[NB : NB + 3, :] = w_vec[...]
    rows[0:1, :] = dist
    rows[1:2, :] = cut
    rows[2:3, :] = live
    rows[3:4, :] = kw
    rows[4:5, :] = (-0.5 * math.pi / cutoff_radius) * jnp.sin(angle)
    rows[5:8, :] = jnp.zeros((3, EDGE_DEV), F32)
    scaled = feat[...] * cut
    hi = scaled.astype(BF).astype(F32)
    left = jnp.concatenate([hi, scaled - hi, hi], axis=0).T.astype(BF)
    w = wfeat[...]
    whi = w.astype(BF).astype(F32)
    right = jnp.concatenate([whi, whi, w - whi], axis=0).astype(BF)
    kind = jnp.where(iota((NSPEC, ATOMS_DEV), 0) == species[...].reshape(1, ATOMS_DEV), 1.0, 0.0).astype(BF)
    centre = dot_tn(kind, table[...]).astype(BF)
    expand = atom_rows(ATOMS_DEV)
    slot_row = slot[...].reshape(1, EDGE_DEV)
    local = one_hot_lanes(as_column(slot_row.astype(F32)), EDGE_DEV)
    base[...] = dot_nn(left, right) + dot_nn(expand, centre) + dot_nn(local, message[...])
    kwb[...] = jnp.broadcast_to(as_column(kw), (EDGE_DEV, 128))


def sigmoid(u):
    return 0.5 * jnp.tanh(0.5 * u) + 0.5


def rms_factor(x):
    return lax.rsqrt(jnp.mean(x * x, axis=-1, keepdims=True) + norm_eps)


def rms_all(x, blocks, xs, rs, gains, place):
    gain = gains[place : place + 1, :]
    out = []
    for b, v in zip(blocks, x):
        r = rms_factor(v)
        scaled = v * r
        xs[place, b, :] = scaled
        rs[place, b, :] = jnp.broadcast_to(r, (v.shape[0], 128))
        out.append((scaled * gain).astype(BF))
    return out


def rms_back(scaled, r, z):
    inner = jnp.mean(scaled * z, axis=-1, keepdims=True)
    return jnp.concatenate([r, r], axis=1) * (z - scaled * inner)


LIMIT = 36 * 2**20
INNER = 4 * NBR
OUTER = EDGE_DEV - INNER


def block_list(edges, parts):
    step = edges // parts
    return [slice(i, i + step) for i in range(0, edges, step)]


def shifted(block, offset):
    return slice(block.start + offset, block.stop + offset)


def atom_spans(edges, offset=0):
    return [slice(i + offset, i + offset + NBR) for i in range(0, edges, NBR)]


def spread(x):
    tall = jnp.concatenate([x, jnp.zeros((32 - NBR, 128), F32)], axis=0).astype(BF)
    head = iota((32, 128), 1) >> 5
    return jnp.concatenate(
        [tall * jnp.where(head == h, 1.0, 0.0).astype(BF) for h in range(4)], axis=0
    )


def gather_heads(wide):
    head = iota((1, 128), 1) >> 5
    out = jnp.where(head == 0, wide[0:NBR], 0.0)
    for h in range(1, 4):
        out = jnp.where(head == h, wide[32 * h : 32 * h + NBR], out)
    return out


def forward(x, blocks, offset, kwb, gains, w_qkv, w_out, w_up, w_down, xs, rs, qkv, ups, probs, slope, att):
    edges = blocks[-1].stop
    score_scale = 1.0 / (math.sqrt(D // HEADS) * score_cap)
    slope_scale = 1.0 / math.sqrt(D // HEADS)
    at = [(s, 128 * g) for s in atom_spans(edges) for g in range(2)]
    for layer in range(2):
        normed = rms_all(x, blocks, xs, rs, gains, 2 * layer)
        for b, v in zip(blocks, normed):
            qkv[layer, b, :] = dot_nn(v, w_qkv[layer])
        q = [spread(qkv[layer, s, c : c + 128]) for s, c in at]
        k = [qkv[layer, s, D + c : D + c + 128].astype(BF) for s, c in at]
        v = [qkv[layer, s, 2 * D + c : 2 * D + c + 128].astype(BF) for s, c in at]
        t = [dot_nt(kk, qq) for kk, qq in zip(k, q)]
        t = [jnp.tanh(tt * score_scale) for tt in t]
        e = [kwb[shifted(s, offset), :] * jnp.exp(score_cap * tt) for (s, c), tt in zip(at, t)]
        p = [ee * (1.0 / jnp.sum(ee, axis=0, keepdims=True)) for ee in e]
        o = [dot_tn(pp.astype(BF), vv) for pp, vv in zip(p, v)]
        o = [gather_heads(oo) for oo in o]
        for i, (s, c) in enumerate(at):
            probs[layer, s, c : c + 128] = p[i]
            slope[layer, s, c : c + 128] = (1.0 - t[i] * t[i]) * slope_scale
            att[s, c : c + 128] = o[i]
        x = [v + dot_nn(att[b, :].astype(BF), w_out[layer]) for b, v in zip(blocks, x)]
        normed = rms_all(x, blocks, xs, rs, gains, 2 * layer + 1)
        up = [dot_nn(v, w_up[layer]) for v in normed]
        sig = [sigmoid(u) for u in up]
        hidden = [u * s for u, s in zip(up, sig)]
        for b, s, h in zip(blocks, sig, hidden):
            ups[layer, b, :] = s + h * (1.0 - s)
        x = [v + dot_nn(h.astype(BF), w_down[layer]) for v, h in zip(x, hidden)]
    return x


def backward(
    x, blocks, offset, kwb, gains, w_energy, w_qkv, w_out, w_up, w_down, xs, rs, qkv, ups, probs, slope, att, dqkv, acc
):
    edges = blocks[-1].stop
    spans = atom_spans(edges)
    at = [(s, 128 * g) for s in spans for g in range(2)]
    read = gains[4:5, :] * w_energy[...]
    readout = []
    dx = []
    for b, v in zip(blocks, x):
        r = rms_factor(v)
        scaled = v * r
        terms = scaled * read
        readout.append(terms[:, 0:128] + terms[:, 128:256])
        total = jnp.sum(terms, axis=-1, keepdims=True) * (1.0 / D)
        dx.append((kwb[shifted(b, offset), 0:1] * r) * (read - scaled * total))
    for layer in (1, 0):
        dhid = [dot_nt(v.astype(BF), w_down[layer]) for v in dx]
        dup = [(dh * ups[layer, b, :]).astype(BF) for b, dh in zip(blocks, dhid)]
        gain = gains[2 * layer + 1 : 2 * layer + 2, :]
        dnorm = [dot_nt(v, w_up[layer]) * gain for v in dup]
        new = []
        for b, v, dn in zip(blocks, dx, dnorm):
            new.append(v + rms_back(xs[2 * layer + 1, b, :], rs[2 * layer + 1, b, :], dn))
        dx = new
        for b, v in zip(blocks, dx):
            att[b, :] = dot_nt(v.astype(BF), w_out[layer])
        do = [spread(att[s, c : c + 128]) for s, c in at]
        v = [qkv[layer, s, 2 * D + c : 2 * D + c + 128].astype(BF) for s, c in at]
        p = [probs[layer, s, c : c + 128] for s, c in at]
        dp = [dot_nt(vv, dd) for vv, dd in zip(v, do)]
        dv = [dot_nn(pp.astype(BF), dd) for pp, dd in zip(p, do)]
        q = [spread(qkv[layer, s, c : c + 128]) for s, c in at]
        k = [qkv[layer, s, D + c : D + c + 128].astype(BF) for s, c in at]
        dl = [pp * (dd - jnp.sum(pp * dd, axis=0, keepdims=True)) for pp, dd in zip(p, dp)]
        ds = [(dd * slope[layer, s, c : c + 128]).astype(BF) for (s, c), dd in zip(at, dl)]
        dk = [dot_nn(dd, qq) for dd, qq in zip(ds, q)]
        dq = [gather_heads(dot_tn(dd, kk)) for dd, kk in zip(ds, k)]
        for i, (s, c) in enumerate(at):
            dqkv[s, c : c + 128] = dq[i]
            dqkv[s, D + c : D + c + 128] = dk[i]
            dqkv[s, 2 * D + c : 2 * D + c + 128] = dv[i]
        for u, s in enumerate(spans):
            total = dl[2 * u] + dl[2 * u + 1]
            acc[s, :] = total if layer == 1 else acc[s, :] + total
        gain = gains[2 * layer : 2 * layer + 1, :]
        dnorm = [dot_nt(dqkv[b, :].astype(BF), w_qkv[layer]) * gain for b in blocks]
        new = []
        for b, v, dn in zip(blocks, dx, dnorm):
            new.append(v + rms_back(xs[2 * layer, b, :], rs[2 * layer, b, :], dn))
        dx = new
    return readout, dx


def inner_forward_kernel(
    base, kwb, gains, w_qkv, w_out, w_up, w_down, last, xs, rs, qkv, ups, probs, slope, att
):
    blocks = block_list(INNER, 1)
    x = forward(
        [base[0:INNER, :]], blocks, 0, kwb, gains, w_qkv, w_out, w_up, w_down, xs, rs, qkv, ups, probs, slope, att
    )
    last[...] = x[0]


def inner_backward_kernel(
    last, xs, rs, qkv, ups, probs, slope, kwb, gains, w_energy, w_qkv, w_out, w_up, w_down, terms, dx, acc, att, dqkv
):
    blocks = block_list(INNER, 1)
    readout, out = backward(
        [last[...]],
        blocks,
        0,
        kwb,
        gains,
        w_energy,
        w_qkv,
        w_out,
        w_up,
        w_down,
        xs,
        rs,
        qkv,
        ups,
        probs,
        slope,
        att,
        dqkv,
        acc,
    )
    terms[...] = readout[0]
    dx[...] = out[0]


def layer_kernel(
    base,
    arr_r,
    arr_m,
    arr_l,
    far,
    kwb,
    feat,
    rows,
    wfeat,
    gains,
    w_qkv,
    w_out,
    w_up,
    w_down,
    w_energy,
    pick,
    inner_last,
    inner_terms,
    inner_dx,
    inner_acc,
    tokens,
    reads,
    grad,
    low,
    mid,
    high,
    xs,
    rs,
    qkv,
    ups,
    probs,
    slope,
    att,
    dqkv,
    acc,
):
    blocks = block_list(OUTER, 3)
    arrived = jnp.concatenate([arr_l[...], arr_m[...], arr_r[...]], axis=0)
    x = []
    for b in blocks:
        here = shifted(b, INNER)
        x.append(base[here, :] + dot_nn(far[here, :], arrived))
    stores = (xs, rs, qkv, ups, probs, slope, att)
    weights = (w_qkv, w_out, w_up, w_down)
    x = forward(x, blocks, INNER, kwb, gains, *weights, *stores)
    tokens[0:INNER, :] = inner_last[...].astype(BF)
    for b, v in zip(blocks, x):
        tokens[shifted(b, INNER), :] = v.astype(BF)
    terms, dx = backward(x, blocks, INNER, kwb, gains, w_energy, *weights, *stores, dqkv, acc)

    w = wfeat[...]
    whi = w.astype(BF)
    ones8 = jnp.ones((8, 128), BF)

    def to_row(parts):
        hi, lo = split2(jnp.concatenate(parts, axis=0))
        return (dot_nt(ones8, hi) + dot_nt(ones8, lo))[0:1]

    hi, lo = split2(jnp.concatenate([inner_dx[...]] + dx, axis=0))
    pair = dot_nt(jnp.concatenate([w.astype(BF).astype(F32), w - whi.astype(F32)], axis=0).astype(BF), hi)
    back = pair[0:NFEAT] + pair[NFEAT : 2 * NFEAT] + dot_nt(whi, lo)
    readout = to_row([inner_terms[...]] + terms)
    reads[...] = readout
    acc_row = to_row([inner_acc[...], acc[...]])
    live = rows[2:3, :]
    dist = rows[0:1, :]
    cut = rows[1:2, :]
    f = feat[...]
    dcut = jnp.sum(f * back, axis=0, keepdims=True) + live * (readout + acc_row / cut)
    centres = 0.5 + 4.0 * iota((NB, 1), 0).astype(F32) / (NB - 1)
    dradial = back[0:NB] * f[0:NB] * (dist - centres)
    ddist = dcut * rows[4:5, :] - (2.0 * (NB / 8.0) ** 2) * cut * jnp.sum(
        dradial, axis=0, keepdims=True
    )
    g = cut * back[NB:NFEAT] + f[NB:NFEAT] * (ddist / dist)
    grad[...] = g
    ghi = g.astype(BF).astype(F32)
    both = jnp.concatenate([ghi, g - ghi], axis=0).astype(BF)
    out = dot_nt(both, pick[...])
    out = out[0:8] + out[8:16]
    low[...] = out[:, 0:SIDE]
    mid[...] = out[:, SIDE : 2 * SIDE]
    high[...] = out[:, 2 * SIDE : 3 * SIDE]


def local_force_kernel(grad, slot, rows, reads, out, energy):
    parts = rows[3:4, :] * reads[...]
    hi = parts.astype(BF).astype(F32)
    wide = jnp.broadcast_to(hi, (8, EDGE_DEV))
    rest = jnp.broadcast_to(parts - hi, (8, EDGE_DEV))
    summed = dot_nn(jnp.concatenate([wide, rest], axis=0).astype(BF), atom_rows(ATOMS_DEV))
    energy[...] = summed[0:1] + summed[8:9]
    g = grad[...]
    ghi = g.astype(BF).astype(F32)
    both = jnp.concatenate([ghi, g - ghi], axis=0).astype(BF)
    local = one_hot_lanes(as_column(slot[...].reshape(1, EDGE_DEV).astype(F32)), EDGE_DEV)
    partner = dot_nt(both, local)
    diff = (g - partner[0:8] - partner[8:16]) * rows[2:3, :]
    hi = diff.astype(BF).astype(F32)
    both = jnp.concatenate([hi, diff - hi], axis=0).astype(BF)
    summed = dot_nn(both, atom_rows(ATOMS_DEV))
    out[...] = summed[0:8] + summed[8:16]


def force_kernel(partial, mt, r, m, l, forces):
    pieces = []
    for part in (r, m, l):
        for a in range(3):
            for b in range(3):
                pieces.append(part[b, a])
    table = jnp.concatenate(pieces, axis=1)
    hi = table.astype(BF).astype(F32)
    both = jnp.concatenate([hi, table - hi], axis=0).astype(BF)
    far = dot_nt(both, mt[...].astype(BF))
    forces[...] = (partial[...] - far[0:8] - far[8:16])[0:3]


def vmem_call(kernel, outs, *args, scratch=(), limit=12 * 2**20, place=VMEM):
    spec = pl.BlockSpec(memory_space=VMEM)
    return pl.pallas_call(
        kernel,
        out_shape=outs,
        in_specs=[pl.BlockSpec(memory_space=place)] * len(args),
        out_specs=jax.tree.map(lambda _: spec, outs),
        scratch_shapes=list(scratch),
        compiler_params=pltpu.CompilerParams(vmem_limit_bytes=limit),
    )(*args)


def shape(dims, dtype=F32):
    return jax.ShapeDtypeStruct(dims, dtype)


def messages(atom_state, w_neigh, prev_tokens, send):
    side = shape((SIDE, D), BF)
    return vmem_call(
        message_kernel,
        [shape((EDGE_DEV, D), BF), side, side, side, shape((3 * SIDE, 8))],
        *(
            pltpu.with_memory_space_constraint(v, pltpu.HBM)
            for v in (atom_state, w_neigh, prev_tokens, send)
        ),
        scratch=[
            VMEM((3 * SIDE, 8), F32),
            VMEM((26 * SLOTS,), jnp.int32),
            VMEM((ATOMS_DEV, D), BF),
            VMEM((D, D), BF),
            VMEM((EDGE_DEV, D), BF),
            pltpu.SemaphoreType.DMA((4,)),
        ],
        place=pltpu.HBM,
    )


def geometry(disp, mask, slot, species, message, table, w_vec, w_rbf):
    return vmem_call(
        geometry_kernel,
        [
            shape((EDGE_DEV, D)),
            shape((EDGE_DEV, 128)),
            shape((NFEAT, EDGE_DEV)),
            shape((8, EDGE_DEV)),
            shape((NFEAT, D)),
        ],
        disp,
        mask,
        slot,
        species,
        message,
        table,
        w_vec,
        w_rbf,
    )


def lookups(slot, mask, where):
    outs = [shape((EDGE_DEV, 3 * SIDE), BF), shape((3 * SIDE, EDGE_DEV), BF), shape((ATOMS_DEV, 3 * SIDE))]
    return vmem_call(lookup_kernel, outs, slot, mask, where)


def inner_stores(n):
    return [
        shape((4, n, D)),
        shape((4, n, 128)),
        shape((2, n, 3 * D)),
        shape((2, n, FF)),
        shape((2, n, D)),
        shape((2, n, D)),
    ]


def inner_forward(base, kwb, gains, weights):
    n = INNER
    outs = [shape((n, D))] + inner_stores(n)
    return vmem_call(
        inner_forward_kernel, outs, base, kwb, gains, *weights, scratch=[VMEM((n, D), F32)]
    )


def inner_backward(saved, kwb, gains, w_energy, weights):
    n = INNER
    return vmem_call(
        inner_backward_kernel,
        [shape((n, 128)), shape((n, D)), shape((n, 128))],
        *saved,
        kwb,
        gains,
        w_energy,
        *weights,
        scratch=[VMEM((n, D), F32), VMEM((n, 3 * D), F32)],
    )


def layers(base, arr, far, kwb, feat, rows, wfeat, gains, weights, w_energy, pick, inner):
    side = shape((8, SIDE))
    n = EDGE_DEV
    return vmem_call(
        layer_kernel,
        [shape((n, D), BF), shape((1, n)), shape((8, n)), side, side, side],
        base,
        *arr,
        far,
        kwb,
        feat,
        rows,
        wfeat,
        gains,
        *weights,
        w_energy,
        pick,
        *inner,
        limit=LIMIT,
        scratch=[VMEM(v.shape, F32) for v in inner_stores(OUTER)]
        + [VMEM((OUTER, D), F32), VMEM((OUTER, 3 * D), F32), VMEM((OUTER, 128), F32)],
    )


def exchange(low, high, axis):
    count = lax.axis_size(axis)
    outer = [(i, (i + 1 if i % 2 else i - 1) % count) for i in range(count)]
    inner = [(i, i + 1 if i % 2 == 0 else i - 1) for i in range(count)]
    return lax.ppermute(low, axis, outer), lax.ppermute(high, axis, inner)


def on_device(
    displacement,
    neighbour_mask,
    reverse_slot,
    send_edges,
    species,
    prev_tokens,
    atom_state,
    species_table,
    w_neigh,
    w_vec,
    w_rbf,
    gains,
    w_qkv,
    w_out,
    w_up,
    w_down,
    w_energy,
):
    message, low, mid, high, where = messages(atom_state, w_neigh, prev_tokens, send_edges)
    low, high = exchange(low, high, "gx")
    far, pick, mt = lookups(reverse_slot, neighbour_mask, where)
    cells = [v.reshape(3, 3, SLOTS, D) for v in (low, mid, high)]
    low, mid, high = (jnp.stack([v[i] for v in cells]) for i in range(3))
    low, high, late = lax.optimization_barrier((low, high, displacement))
    low, high = exchange(low, high, "gy")
    base, kwb, feat, rows, wfeat = geometry(
        late, neighbour_mask, reverse_slot, species, message, species_table, w_vec, w_rbf
    )
    weights = (w_qkv, w_out, w_up, w_down)
    w_energy = w_energy.reshape(1, D)
    saved = inner_forward(base, kwb, gains, weights)
    cells = (low, mid, high)
    low, mid, high = (jnp.stack([v[:, i] for v in cells], axis=1) for i in range(3))
    low, high, *saved = lax.optimization_barrier((low, high, *saved))
    low, high = exchange(low, high, "gz")
    terms, dx, acc = inner_backward(saved, kwb, gains, w_energy, weights)
    arr = [v.reshape(SIDE, D) for v in (high, mid, low)]
    tokens, reads, grad, low, mid, high = layers(
        base,
        arr,
        far,
        kwb,
        feat,
        rows,
        wfeat,
        gains,
        weights,
        w_energy,
        pick,
        (saved[0], terms, dx, acc),
    )
    low, high = exchange(low, high, "gx")
    cells = jnp.stack([low, mid, high])
    cut = 3 * SLOTS
    low, mid, high = (cells[:, :, i * cut : (i + 1) * cut] for i in range(3))
    low, high = exchange(low, high, "gy")
    cells = jnp.stack([low, mid, high])
    cut = SLOTS
    low, mid, high = (cells[..., i * cut : (i + 1) * cut] for i in range(3))
    low, high, late = lax.optimization_barrier((low, high, grad))
    low, high = exchange(low, high, "gz")
    partial, energy = vmem_call(
        local_force_kernel,
        [shape((8, ATOMS_DEV)), shape((1, ATOMS_DEV))],
        late,
        reverse_slot,
        rows,
        reads,
    )
    forces = vmem_call(force_kernel, shape((3, ATOMS_DEV)), partial, mt, low, mid, high)
    return (tokens, energy.reshape(ATOMS_DEV), forces)


def solution(mesh):
    return jax.shard_map(
        on_device,
        mesh=mesh,
        in_specs=(
            P(None, ("gx", "gy", "gz")),
            P(("gx", "gy", "gz")),
            P(("gx", "gy", "gz")),
            P(("gx", "gy", "gz")),
            P(("gx", "gy", "gz")),
            P(("gx", "gy", "gz"), None),
            P(("gx", "gy", "gz"), None),
            P(),
            P(),
            P(),
            P(),
            P(),
            P(),
            P(),
            P(),
            P(),
            P(),
        ),
        out_specs=(P(("gx", "gy", "gz"), None), P(("gx", "gy", "gz")), P(None, ("gx", "gy", "gz"))),
        check_vma=False,
    )
```
